128 devices in a mesh: section: 2 (over core), fsdp: 64 (over x, z, y).
Axes of the slice: x: 4, y: 4, z: 4, core: 2. Of those that a mesh axis runs over, the one named last changes fastest.
Arguments:
- ends_in: float32 [2, 2, 4096, 1024], P('section', None, 'fsdp'), may hold values from -6 to 6
- routes: int32 [2, 2, 4096, 2], P('section', None, 'fsdp'), may hold values from 0 to 31, all different within a row; in each aligned block of 64 rows (0 to 63, 64 to 127, ..., all dimensions but the last counted through in order) at most 6 rows name the same one
- segments: int32 [2, 64, 64], P(None, 'fsdp'), may hold values from 0 to 3, never falling along the last dimension, each value on 1 to 32 neighbouring positions
- norm_gains: bfloat16 [2, 1024, 2], P('section', 'fsdp'), may hold values from 0.5 to 1.5
- w_qkv: bfloat16 [2, 1024, 2048], P('section', 'fsdp'), may hold values from -0.1875 to 0.1875
- w_attn_out: bfloat16 [2, 1024, 1024], P('section', 'fsdp'), may hold values from -0.5 to 0.5
- w_router: bfloat16 [2, 1024, 32], P('section', 'fsdp'), may hold values from -0.09375 to 0.09375
- w_in: bfloat16 [2, 16384, 2048], P('section', 'fsdp'), may hold values from -0.1875 to 0.1875
- w_out: bfloat16 [2, 16384, 1024], P('section', 'fsdp'), may hold values from -0.5 to 0.5
Outputs:
- ends_out: float32 [2, 2, 4096, 1024], P('section', None, 'fsdp')
- grad_gains: float32 [2, 1024, 2], P('section', 'fsdp')
- grad_qkv: float32 [2, 1024, 2048], P('section', 'fsdp')
- grad_attn_out: float32 [2, 1024, 1024], P('section', 'fsdp')
- grad_router: float32 [2, 1024, 32], P('section', 'fsdp')
- grad_in: float32 [2, 16384, 2048], P('section', 'fsdp')
- grad_out: float32 [2, 16384, 1024], P('section', 'fsdp')
The draws below stay inside these ranges and needn't reach their ends.
Inputs may be any that keep to these rules, and one draw needn't show every extreme that they name: `routes`: in each aligned block of 64 rows (one device's tokens of one micro-batch of one layer) no expert is named more than 6 times, and the 2 experts of a row differ. `segments`: each row of 64 positions is one packed sequence; numbers never fall along it and no document is longer than 32.
All inputs are finite; a program needn't handle non-finite values.
Results may differ from the reference program's by a relative error of at most 0.02.
Values may be sent and summed in bfloat16 or wider, within the bound.
No kernel may reach another device: no remote copies, remote signals or barrier semaphores. Data moves between devices by JAX's collectives and lax.ppermute only.
A program may use at most 128 MiB of HBM per device.

```python
import math
import jax
import jax.numpy as jnp
import numpy as np
from jax import lax

D = 1024
HEADS = 16
KV_HEADS = 8
HEAD = 64
E = 32
TOPK = 2
F = 512
TOK = 64
MB = 2
CAP = 6
QKVW = 2048
UNITS = 16384
N_SEQ = 64
TOKENS = 4096
N_FSDP = 64


def levels(stream_key, extent, split, smallest, high):
    def one(dim, blocks):
        draws = jax.random.uniform(jax.random.fold_in(jax.random.fold_in(stream_key, 6), dim), (blocks,), jnp.float32, smallest / len(split), high / len(split))
        return jnp.repeat(jnp.exp(draws), extent[dim] // blocks).reshape((-1,) + (1,) * (len(extent) - dim - 1))

    gain = one(*split[0])
    for cut in split[1:]:
        gain = gain * one(*cut)
    return gain


def split_up(number_of, total, reach, skew):
    portions = [(1 << 20) // math.isqrt(grade ** skew) + 1 for grade in range(2, number_of + 1)]
    surplus, given = total - reach - (number_of - 1), [1] * (number_of - 1)
    while surplus > 0:
        movable = [i for i in range(number_of - 1) if given[i] < reach]
        whole, budget = sum([portions[i] for i in movable]), surplus
        for i in movable:
            extra = min(reach - given[i], max(1, budget * portions[i] // whole), surplus)
            given[i] = given[i] + extra
            surplus = surplus - extra
    return np.array([reach] + given)


def ragged(stream_key, number_of, total, reach, slope):
    if number_of == 2:
        one = jax.random.randint(stream_key, (), max(1, total - reach), min(reach, total - 1) + 1)
        return jnp.stack([one, total - one])
    sizes = jnp.asarray(split_up(number_of, total, reach, slope), jnp.int32)
    pairs = (number_of - 1) // 2
    donor, taker = sizes[1:1 + 2 * pairs:2], sizes[2:2 + 2 * pairs:2]
    margin = jnp.minimum(donor - 1, reach - taker)
    moved = jax.random.randint(jax.random.fold_in(stream_key, 1), (pairs,), 0, 1 << 20) % (margin + 1)
    sizes = sizes.at[1:1 + 2 * pairs:2].set(donor - moved).at[2:2 + 2 * pairs:2].set(taker + moved)
    return sizes[jax.random.permutation(jax.random.fold_in(stream_key, 2), number_of)]


def shared_out(key, own, number, rows, amount, top, reach, slope):
    sequence = jax.random.permutation(key, amount)
    packed, ordinary = portions_of(amount, rows * top, reach, slope, True), portions_of(amount, rows * top, reach, slope, False)
    places = jnp.arange(amount)

    def named(lengths, turn):
        used = int((lengths > 0).sum())
        fixed = max(1, used // 4)
        moved = fixed + (places - fixed + turn * (used - fixed)) % max(1, amount - fixed)
        return jnp.zeros((amount,), jnp.int32).at[sequence[jnp.where(places < fixed, places, moved)]].set(jnp.asarray(lengths, jnp.int32))

    lengths = jnp.where(number % 4 == 0, named(packed, number // 4), named(ordinary, number - number // 4 - 1))
    mixed = jax.random.permutation(jax.random.fold_in(own, 3), amount)
    source_of, taker = mixed[0:amount // 2 * 2:2], mixed[1:amount // 2 * 2:2]
    margin = jnp.minimum(lengths[source_of] - 1, reach - lengths[taker]) // 2
    margin = jnp.where((source_of == sequence[0]) | (taker == sequence[0]) | (lengths[taker] == 0), 0, jnp.maximum(margin, 0))
    moved = jax.random.randint(jax.random.fold_in(own, 4), (amount // 2,), 0, 1 << 20) % (margin + 1)
    lengths = lengths.at[source_of].add(-moved).at[taker].add(moved)
    members = jnp.searchsorted(jnp.cumsum(lengths), jnp.arange(rows * top), side="right").astype(jnp.int32)
    grid = members.reshape(top, rows).T
    grid = grid[jax.random.permutation(jax.random.fold_in(own, 1), rows)]
    turn = jax.random.randint(jax.random.fold_in(own, 2), (rows, 1), 0, top)
    return jnp.take_along_axis(grid, (jnp.arange(top)[None, :] + turn) % top, axis=1)


def portions_of(count, total, most, lean, full):
    loads = [(1 << 20) // math.isqrt(grade ** lean) + 1 for grade in range(1, count + 1)]
    largest = most if full else min(most, max(-(-total // count), total * loads[0] // sum(loads)))
    least = 1 if total - largest >= count - 1 else 0
    holding, rest = [largest] + [least] * (count - 1), total - largest - least * (count - 1)
    while rest > 0:
        movable = [i for i in range(1, count) if holding[i] < largest] or [i for i in range(1, count) if holding[i] < most]
        whole, remaining = sum([loads[i] for i in movable]), rest
        for i in movable:
            more = min(most - holding[i], max(1, remaining * loads[i] // whole), rest)
            holding[i] = holding[i] + more
            rest = rest - more
    return np.array(holding)


def scatter_about(own_key, extent, deviation, bound, split=(), kind=jnp.bfloat16):
    entries = jax.random.normal(own_key, extent, jnp.float32) * deviation
    if len(split) > 0:
        entries = levels(own_key, extent, split, -0.22, 0.18) * entries
    return jnp.clip(entries, min=-bound, max=bound).astype(kind)


def setup_inputs(seed: int = 0) -> dict:
    arg_keys = jax.random.split(jax.random.key(seed), 10)
    ends_in = scatter_about(arg_keys[0], (2, MB, TOKENS, D), 1.0, 6.0, ((0, 2), (2, 64)), jnp.float32)
    routes_keys = jax.random.split(jax.random.fold_in(arg_keys[1], 1), 2 * MB * TOKENS // TOK)
    routes_turns = jax.random.permutation(jax.random.fold_in(arg_keys[1], 3), 2 * MB * TOKENS // TOK)
    routes = jax.vmap(lambda own, number: shared_out(jax.random.fold_in(arg_keys[1], 2), own, number, TOK, E, TOPK, CAP, 1))(routes_keys, routes_turns).reshape((2, MB, TOKENS, TOPK))
    segments = jax.vmap(lambda own: jnp.searchsorted(jnp.cumsum(ragged(own, 4, TOK, TOK // 2, 0)), jnp.arange(TOK), side="right"))(jax.random.split(arg_keys[2], MB * N_SEQ)).reshape((MB, N_SEQ, TOK)).astype(jnp.int32)
    norm_gains = jnp.clip(1.0 + 0.1 * jax.random.normal(arg_keys[3], (2, D, 2), jnp.float32), 0.5, 1.5).astype(jnp.bfloat16)
    w_qkv = scatter_about(arg_keys[4], (2, D, QKVW), D ** -0.5, 0.1875, ((0, 2), (1, 64)))
    w_attn_out = scatter_about(arg_keys[5], (2, D, HEADS * HEAD), (HEADS * HEAD // 8) ** -0.5, 0.5, ((0, 2), (1, 64)))
    w_router = scatter_about(arg_keys[6], (2, D, E), (4 * D) ** -0.5, 0.09375, ((0, 2), (1, 64)))
    w_in = scatter_about(arg_keys[7], (2, UNITS, 2 * D), D ** -0.5, 0.1875, ((0, 2), (1, 64)))
    w_out = scatter_about(arg_keys[8], (2, UNITS, D), (F // 4) ** -0.5, 0.5, ((0, 2), (1, 64)))
    return {"ends_in": ends_in, "routes": routes, "segments": segments, "norm_gains": norm_gains, "w_qkv": w_qkv, "w_attn_out": w_attn_out, "w_router": w_router, "w_in": w_in, "w_out": w_out}


EPSILON = 1e-06
ROPE_BASE = 10000.0
NEGATIVE = -1e+30
PRECISE = lax.Precision.HIGHEST

@jax.custom_vjp
def low(v):
    return lax.optimization_barrier(v.astype(jnp.bfloat16)).astype(jnp.float32)

@jax.custom_vjp
def low_back(v):
    return v

def low_keep(v):
    return (low(v), None)

def low_pass(kept, grad):
    return (grad,)

def back_keep(v):
    return (v, None)

def back_low(kept, grad):
    return (low(grad),)
low.defvjp(low_keep, low_pass)
low_back.defvjp(back_keep, back_low)

def norm_rows(matrix, weight_gain):
    return matrix * lax.rsqrt(lax.optimization_barrier(jnp.mean(matrix * matrix, -1, keepdims=True)) + EPSILON) * weight_gain

def tables(segment_row, head_size):
    length = segment_row.shape[0]
    same_doc = segment_row[:, None] == segment_row[None, :]
    row_ids = jnp.arange(length, dtype=jnp.int32)[:, None]
    col_ids = jnp.arange(length, dtype=jnp.int32)[None, :]
    allowed = same_doc & (col_ids <= row_ids)
    position = lax.optimization_barrier(jnp.sum(jnp.where(same_doc & (col_ids < row_ids), 1, 0), 1)).astype(jnp.float32)
    half_size = head_size // 2
    frequency = jnp.exp(jnp.arange(half_size, dtype=jnp.float32) * (-2.0 * math.log(ROPE_BASE) / head_size))
    angles = position[:, None] * frequency[None, :]
    cosine = jnp.concatenate([jnp.cos(angles), jnp.cos(angles)], -1)
    sine_vals = jnp.concatenate([jnp.sin(angles), jnp.sin(angles)], -1)
    return (cosine, sine_vals, allowed)

def rotate(matrix, cosine, sine_vals):
    half_size = matrix.shape[-1] // 2
    turned = jnp.concatenate([-matrix[..., half_size:], matrix[..., :half_size]], -1)
    return matrix * cosine[:, None] + turned * sine_vals[:, None]

def slot_ids(route_ids):
    flat_ids = route_ids.reshape(-1)
    one_hot = (flat_ids[:, None] == jnp.arange(E, dtype=jnp.int32)[None, :]).astype(jnp.int32)
    ranked = lax.optimization_barrier(jnp.sum(jnp.cumsum(one_hot, 0) * one_hot, 1)) - 1
    return (flat_ids * CAP + ranked).astype(jnp.int32).reshape(route_ids.shape)

def block_layer(weights, layer_in, route_ids, segment_row):
    gains, w_qkv, w_attn_out, w_router, w_in, w_out = weights
    length = layer_in.shape[0]
    group_size = HEADS // KV_HEADS
    query_width = HEADS * HEAD
    key_width = KV_HEADS * HEAD
    score_scale = 1.0 / math.sqrt(HEAD)
    cosine, sine_vals, allowed = tables(segment_row, HEAD)
    normed_in = low(norm_rows(layer_in, gains[:, 0]))
    projected = low_back(jnp.dot(normed_in, w_qkv, precision=PRECISE))
    query = low(rotate(projected[:, :query_width].reshape(length, HEADS, HEAD), cosine, sine_vals))
    query = query.reshape(length, KV_HEADS, group_size, HEAD)
    key_vecs = low(rotate(projected[:, query_width:query_width + key_width].reshape(length, KV_HEADS, HEAD), cosine, sine_vals))
    value_vecs = low(projected[:, query_width + key_width:].reshape(length, KV_HEADS, HEAD))
    scores = low_back(jnp.einsum('tkgd,skd->kgts', query, key_vecs, precision=PRECISE) * score_scale)
    scores = jnp.where(allowed, scores, NEGATIVE)
    attn_probs = jax.nn.softmax(scores, -1)
    attn_mixed = jnp.einsum('kgts,skd->tkgd', low(attn_probs), value_vecs, precision=PRECISE).reshape(length, query_width)
    attn_mixed = low_back(low(attn_mixed))
    residual_mid = layer_in + low_back(jnp.einsum('tj,dj->td', attn_mixed, w_attn_out, precision=PRECISE))
    normed_ffn = low(norm_rows(residual_mid, gains[:, 1]))
    logits = low_back(jnp.dot(normed_ffn, w_router, precision=PRECISE))
    gate_probs = jax.nn.softmax(jnp.take_along_axis(logits, route_ids, 1), -1)
    flat_ids = slot_ids(route_ids)
    slot_rows = jnp.zeros((E * CAP, D), jnp.float32).at[flat_ids.reshape(-1)].add(jnp.repeat(normed_ffn, TOPK, 0))
    slot_rows = slot_rows.reshape(E, CAP, D)
    in_weights = w_in.reshape(E, F, 2 * D)
    gate_pre = low_back(jnp.einsum('ecd,efd->ecf', slot_rows, in_weights[:, :, :D], precision=PRECISE))
    up_pre = low_back(jnp.einsum('ecd,efd->ecf', slot_rows, in_weights[:, :, D:], precision=PRECISE))
    hidden = low(jax.nn.silu(gate_pre) * up_pre)
    expert_out = low_back(jnp.einsum('ecf,efd->ecd', hidden, w_out.reshape(E, F, D), precision=PRECISE))
    expert_out = expert_out.reshape(E * CAP, D)
    mixture = lax.optimization_barrier(jnp.sum(gate_probs[:, :, None] * expert_out[flat_ids], 1))
    return residual_mid + mixture

def run_layer(weights, layer_in, route_ids, segment_ids):
    blocks = layer_in.shape[0]
    group_blocks = math.gcd(blocks, max(1, 4096 // TOK))

    def group_apply(pieces):
        return jax.vmap(block_layer, in_axes=(None, 0, 0, 0))(weights, pieces[0], pieces[1], pieces[2])
    shaped = tuple((member.reshape((blocks // group_blocks, group_blocks) + member.shape[1:]) for member in (layer_in, route_ids, segment_ids)))
    result = lax.map(jax.checkpoint(group_apply), shaped)
    return result.reshape(layer_in.shape)

def reference(ends_in, routes, segments, norm_gains, w_qkv, w_attn_out, w_router, w_in, w_out):
    blocks = MB * N_FSDP
    inputs = ends_in[0].reshape(blocks, TOK, D)
    cotangent = ends_in[1].reshape(blocks, TOK, D)
    route_ids = routes.reshape(2, blocks, TOK, TOPK)
    segment_ids = segments.reshape(blocks, TOK)
    weights = tuple((member.astype(jnp.float32) for member in (norm_gains, w_qkv, w_attn_out, w_router, w_in, w_out)))

    def forward(weights, layer_in):
        first_layer = tuple((member[0] for member in weights))
        second_layer = tuple((member[1] for member in weights))
        passed = low_back(low(run_layer(first_layer, layer_in, route_ids[0], segment_ids)))
        return run_layer(second_layer, passed, route_ids[1], segment_ids)
    result, pullback = jax.vjp(forward, weights, inputs)
    gradients, input_grad = pullback(cotangent)
    ends_out = jnp.stack([input_grad, result]).reshape(2, MB, TOKENS, D)
    return (ends_out, gradients[0], gradients[1], gradients[2], gradients[3], gradients[4], gradients[5])
```

```python
import math

import jax
import jax.numpy as jnp
from jax import lax
from jax.experimental import pallas as pl
from jax.experimental.pallas import tpu as pltpu
from jax.sharding import PartitionSpec as P

D = 1024
HEADS = 16
KV_HEADS = 8
HEAD = 64
E = 32
CAP = 6
TOK = 64
DEV = 64
SLOT = 8
ROWS = DEV * SLOT
PACK = 768
TAIL = D - PACK
WIDE = 1664
SMALL = 1536
QW = 512
KW = 256
GROUPS = 4
UNITS = 256
EPSILON = 1e-06
ROPE_BASE = 10000.0
NEGATIVE = -1e30
F32 = jnp.float32
BF16 = jnp.bfloat16


def nn(a, b):
    return lax.dot_general(a, b, (((1,), (0,)), ((), ())), preferred_element_type=F32)


def nt(a, b):
    return lax.dot_general(a, b, (((1,), (1,)), ((), ())), preferred_element_type=F32)


def tn(a, b):
    return lax.dot_general(a, b, (((0,), (0,)), ((), ())), preferred_element_type=F32)


def row_in_slot(shape):
    return lax.broadcasted_iota(jnp.int32, shape, 0) % SLOT


def tail_moves():
    row = lax.broadcasted_iota(jnp.int32, (128, 384), 0)
    col = lax.broadcasted_iota(jnp.int32, (128, 384), 1)
    piece, col = col // 128, col % 128
    slot, kept = row % SLOT, col % SLOT
    hit = ((kept == CAP) & (slot == piece)) | ((kept == CAP + 1) & (slot == piece + 3))
    return jnp.where(hit & (row // SLOT == col // SLOT), 1.0, 0.0).astype(BF16)


def unpack(packed):
    moves = tail_moves()
    main = jnp.where(row_in_slot((ROWS, PACK)) < CAP, packed.astype(F32), 0.0).astype(BF16)
    tails = []
    for block in range(0, ROWS, 128):
        part = packed[block : block + 128]
        stacked = jnp.concatenate([part[:, 256 * j : 256 * j + 256] for j in range(3)], 0)
        tails.append(nn(moves, stacked).astype(BF16))
    return jnp.concatenate([main, jnp.concatenate(tails, 0)], 1)


def pack(rows):
    moves = tail_moves()
    keep = row_in_slot((128, 256)) < CAP
    blocks = []
    for block in range(0, ROWS, 128):
        part = rows[block : block + 128]
        tail = tn(moves, part[:, PACK:])
        pieces = []
        for j in range(3):
            main = part[:, 256 * j : 256 * j + 256].astype(F32)
            pieces.append(jnp.where(keep, main, tail[128 * j : 128 * j + 128]).astype(BF16))
        blocks.append(jnp.concatenate(pieces, 1))
    return jnp.concatenate(blocks, 0)


def inverse_rms(x):
    return lax.rsqrt(jnp.mean(x * x, -1, keepdims=True) + EPSILON)


def norm_back(x, gain, grad):
    inv = inverse_rms(x)
    unit = x * inv
    scaled = grad * gain
    dx = inv * (scaled - unit * jnp.mean(scaled * unit, -1, keepdims=True))
    return dx, jnp.sum(grad * unit, 0, keepdims=True)


def half_swap(v):
    width = v.shape[1]
    lane = lax.broadcasted_iota(jnp.int32, v.shape, 1) % HEAD
    return jnp.where(
        lane < HEAD // 2,
        pltpu.roll(v, width - HEAD // 2, 1),
        pltpu.roll(v, HEAD // 2, 1),
    )


def at_lane(shape, lane, value, base):
    return jnp.where(lax.broadcasted_iota(jnp.int32, shape, 1) == lane, value, base)


def attend_kernel(own, oth, w, cos, sin, bias, normed_o, q_o, k_o, v_o, p_o, mix_o, branch_o, send_o, gain_o):
    x = jnp.concatenate([own[...].astype(F32), oth[...].astype(F32)], 0)
    small = w[:, SMALL:].astype(F32).T
    gains = small[E : E + 8]
    gain_o[...] = gains
    normed = (x * inverse_rms(x) * gains[0:1]).astype(BF16)
    normed_o[...] = normed
    proj = nn(normed, w[:, :D])
    q = proj[:, :QW]
    k = proj[:, QW : QW + KW]
    v = proj[:, QW + KW :].astype(BF16)
    q = (q * cos[...] + half_swap(q) * sin[...]).astype(BF16)
    k = (k * cos[:, :KW] + half_swap(k) * sin[:, :KW]).astype(BF16)
    q_o[...] = q
    k_o[...] = k
    v_o[...] = v
    mask = bias[...]
    mixed = []
    for h in range(2 * GROUPS):
        g = h // 2
        q_h = q[:, HEAD * h : HEAD * h + HEAD]
        k_g = k[:, HEAD * g : HEAD * g + HEAD]
        v_g = v[:, HEAD * g : HEAD * g + HEAD]
        s = nt(q_h, k_g) * (1.0 / math.sqrt(HEAD)) + mask
        top = jnp.max(s, -1, keepdims=True)
        ex = jnp.exp(s - top)
        p = ex / jnp.sum(ex, -1, keepdims=True)
        p_o[128 * h : 128 * h + 128, :] = p
        mixed.append(nn(p.astype(BF16), v_g))
    mixed = jnp.concatenate(mixed, 1).astype(BF16)
    mix_o[...] = mixed
    branch = nt(mixed, w[:, D:SMALL])
    branch_o[...] = branch[:TOK]
    send_o[...] = branch[TOK:]


def route_kernel(x, branch, recv, gains, small, routes, place, mid_o, normed_o, gate_o, out_o):
    mid = x[...].astype(F32) + branch[...] + recv[...]
    mid_o[...] = mid
    normed = (mid * inverse_rms(mid) * gains[1:2]).astype(BF16)
    normed_o[...] = normed
    logits = nn(normed, small[...])
    lane = lax.broadcasted_iota(jnp.int32, (TOK, 128), 1)
    l0 = jnp.sum(jnp.where(lane == routes[:, 0:1], logits, 0.0), -1, keepdims=True)
    l1 = jnp.sum(jnp.where(lane == routes[:, 1:2], logits, 0.0), -1, keepdims=True)
    top = jnp.maximum(l0, l1)
    e0, e1 = jnp.exp(l0 - top), jnp.exp(l1 - top)
    total = e0 + e1
    gate_o[...] = at_lane((TOK, 128), 0, e0 / total, at_lane((TOK, 128), 1, e1 / total, 0.0))
    rows = nn(place[...], jnp.concatenate([normed, normed], 0)).astype(BF16)
    out_o[...] = pack(rows)


def early_kernel(up, routes, place, out_o):
    u = up[...].astype(BF16)
    lane = lax.broadcasted_iota(jnp.int32, (TOK, 128), 1) < 128
    other0 = jnp.where(lane, routes[:, 1:2], 0).astype(F32).astype(BF16)
    other1 = jnp.where(lane, routes[:, 0:1], 0).astype(F32).astype(BF16)
    table = jnp.concatenate(
        [jnp.concatenate([u, other0], 1), jnp.concatenate([u, other1], 1)], 0
    )
    out_o[...] = nn(place[...], table).astype(BF16)


def expert_forward_kernel(arrived, w_in, w_out, rows_o, gate_o, up_o, out_o):
    rows = unpack(arrived[...])
    rows_o[...] = rows
    gate = nt(rows, w_in[:, :D])
    up = nt(rows, w_in[:, D:])
    gate_o[...] = gate
    up_o[...] = up
    hidden = (gate * (1.0 / (1.0 + jnp.exp(-gate))) * up).astype(BF16)
    out_o[...] = pack(nn(hidden, w_out[...]).astype(BF16))


def expert_grads(rows, grads, gate, up, w_in, w_out, in_o, outw_o):
    sig = 1.0 / (1.0 + jnp.exp(-gate))
    act = gate * sig
    hidden = (act * up).astype(BF16)
    grad_hidden = nt(grads, w_out[...])
    g_gate = (grad_hidden * up * sig * (1.0 + gate * (1.0 - sig))).astype(BF16)
    g_up = (grad_hidden * act).astype(BF16)
    grad_rows = nn(g_gate, w_in[:, :D]) + nn(g_up, w_in[:, D:])
    outw_o[...] = tn(hidden, grads)
    in_o[:, :D] = tn(g_gate, rows)
    in_o[:, D:] = tn(g_up, rows)
    return hidden, grad_rows


def expert_both_kernel(expert, arrived, early, small, w_in, w_out, in_o, outw_o, back_o, out_o):
    rows = unpack(arrived[...])
    u = early[:, :D].astype(F32)
    other = early[:, D:].astype(F32)[:, 0:1].astype(jnp.int32)
    logits = nn(rows, small[...])
    lane = lax.broadcasted_iota(jnp.int32, (ROWS, 128), 1)
    l0 = jnp.sum(jnp.where(lane == expert[0], logits, 0.0), -1, keepdims=True)
    l1 = jnp.sum(jnp.where(lane == other, logits, 0.0), -1, keepdims=True)
    top = jnp.maximum(l0, l1)
    e0, e1 = jnp.exp(l0 - top), jnp.exp(l1 - top)
    grads = (e0 / (e0 + e1) * u).astype(BF16)
    gate = nt(rows, w_in[:, :D])
    up = nt(rows, w_in[:, D:])
    hidden, grad_rows = expert_grads(rows, grads, gate, up, w_in, w_out, in_o, outw_o)
    out = nn(hidden, w_out[...])
    score = jnp.sum(u * out, -1, keepdims=True)
    high = score.astype(BF16).astype(F32)
    extra = at_lane((ROWS, 128), 0, high, at_lane((ROWS, 128), 1, score - high, 0.0))
    back_o[:, :PACK] = pack(grad_rows.astype(BF16))
    back_o[:, PACK:] = extra.astype(BF16)
    out_o[...] = pack(out.astype(BF16))


def expert_backward_kernel(arrived, rows, gate, up, w_in, w_out, in_o, outw_o, back_o):
    grads = unpack(arrived[...])
    _, grad_rows = expert_grads(rows[...], grads, gate[...], up[...], w_in, w_out, in_o, outw_o)
    back_o[...] = pack(grad_rows.astype(BF16))


def combine_kernel(returned, take, mid, gates, picked_o, out_o, low_o):
    picked = nn(take[...], unpack(returned[...]))
    picked_o[...] = picked
    out = mid[...] + gates[:, 0:1] * picked[:TOK] + gates[:, 1:2] * picked[TOK:]
    out_o[...] = out
    low_o[...] = out.astype(BF16)


def gate_back(s0, s1, gates, routes, small, returned, take, normed, mid, gains, up, gmid_o, branch_o, sums_o):
    g0, g1 = gates[:, 0:1], gates[:, 1:2]
    mean = g0 * s0 + g1 * s1
    lane = lax.broadcasted_iota(jnp.int32, (TOK, 128), 1)
    grad_logits = (
        jnp.where(lane == routes[:, 0:1], g0 * (s0 - mean), 0.0)
        + jnp.where(lane == routes[:, 1:2], g1 * (s1 - mean), 0.0)
    ).astype(BF16)
    both = (take[:TOK, :].astype(F32) + take[TOK:, :].astype(F32)).astype(BF16)
    grad_ffn = nt(grad_logits, small[...]) + nn(both, unpack(returned[:, :PACK]))
    dx, dgain = norm_back(mid[...], gains[1:2], grad_ffn)
    grad_mid = up[...].astype(F32) + dx
    gmid_o[...] = grad_mid
    branch_o[...] = grad_mid.astype(BF16)
    router = tn(grad_logits, normed[...])[:E]
    row = lax.broadcasted_iota(jnp.int32, (8, D), 0)
    sums_o[...] = jnp.concatenate([router, jnp.where(row == 1, dgain, 0.0)], 0)


def token_back_scored(returned, take, gates, routes, small, normed, mid, gains, up, gmid_o, branch_o, sums_o):
    scores = nn(take[...], returned[:, PACK:])
    scores = scores[:, 0:1] + scores[:, 1:2]
    gate_back(scores[:TOK], scores[TOK:], gates, routes, small, returned, take, normed, mid, gains, up, gmid_o, branch_o, sums_o)


def token_back_picked(returned, take, gates, routes, small, normed, mid, gains, up, picked, gmid_o, branch_o, sums_o):
    u = up[...].astype(F32)
    s0 = jnp.sum(u * picked[:TOK, :], -1, keepdims=True)
    s1 = jnp.sum(u * picked[TOK:, :], -1, keepdims=True)
    gate_back(s0, s1, gates, routes, small, returned, take, normed, mid, gains, up, gmid_o, branch_o, sums_o)


def attend_back_kernel(own, oth, x_own, x_oth, w, cos, sin, normed, q, k, v, p, mixed, gains, sums, grad_o, part_o, send_o):
    scale = 1.0 / math.sqrt(HEAD)
    branch = jnp.concatenate([own[...], oth[...]], 0)
    grad_mixed = nn(branch, w[:, D:SMALL]).astype(BF16)
    grad_o[:, D:SMALL] = tn(branch, mixed[...]).astype(BF16)
    d_q, d_k, d_v = [], [], []
    for g in range(GROUPS):
        k_g = k[:, HEAD * g : HEAD * g + HEAD]
        v_g = v[:, HEAD * g : HEAD * g + HEAD]
        dk = dv = 0.0
        for h in (2 * g, 2 * g + 1):
            q_h = q[:, HEAD * h : HEAD * h + HEAD]
            gm = grad_mixed[:, HEAD * h : HEAD * h + HEAD]
            ph = p[128 * h : 128 * h + 128, :]
            dp = nt(gm, v_g)
            ds = (ph * (dp - jnp.sum(ph * dp, -1, keepdims=True))).astype(BF16)
            d_q.append(nn(ds, k_g) * scale)
            dk = dk + tn(ds, q_h)
            dv = dv + tn(ph.astype(BF16), gm)
        d_k.append(dk * scale)
        d_v.append(dv)
    d_q = jnp.concatenate(d_q, 1)
    d_k = jnp.concatenate(d_k, 1)
    d_v = jnp.concatenate(d_v, 1)
    d_q = d_q * cos[...] - half_swap(d_q) * sin[...]
    d_k = d_k * cos[:, :KW] - half_swap(d_k) * sin[:, :KW]
    grad_proj = jnp.concatenate([d_q, d_k, d_v], 1).astype(BF16)
    grad_normed = nt(grad_proj, w[:, :D])
    part_o[...] = grad_normed[:TOK]
    send_o[...] = grad_normed[TOK:]
    grad_o[:, :D] = tn(normed[...], grad_proj).astype(BF16)
    x = jnp.concatenate([x_own[...].astype(F32), x_oth[...].astype(F32)], 0)
    dgain = jnp.sum(grad_normed * (x * inverse_rms(x)), 0, keepdims=True)
    row = lax.broadcasted_iota(jnp.int32, (E + 8, D), 0)
    full = jnp.where(row == E, dgain, sums[...])
    full = jnp.concatenate([full, jnp.zeros((128 - E - 8, D), F32)], 0)
    grad_o[:, SMALL:] = full.T.astype(BF16)


def input_back_kernel(part, recv, x, gains, gmid, out_o):
    dx, _ = norm_back(x[...].astype(F32), gains[0:1], part[...] + recv[...])
    out_o[...] = gmid[...] + dx


def input_back_send_kernel(part, recv, x, gains, gmid, gates, place, up_o, out_o):
    dx, _ = norm_back(x[...].astype(F32), gains[0:1], part[...] + recv[...])
    up = (gmid[...] + dx).astype(BF16)
    up_o[...] = up
    up = up.astype(F32)
    rows = jnp.concatenate([gates[:, 0:1] * up, gates[:, 1:2] * up], 0).astype(BF16)
    out_o[...] = pack(nn(place[...], rows).astype(BF16))


def whole(shape):
    return pl.BlockSpec(shape, lambda i: (0,) * len(shape))


SMALL_SPEC = pl.BlockSpec((D, 128), lambda i: (0, SMALL // 128))


def call(kernel, outs, *args, small=(), scalar=(), flops=10**9):
    in_specs = []
    for n, arg in enumerate(args):
        if n in scalar:
            in_specs.append(pl.BlockSpec(memory_space=pltpu.SMEM))
        elif n in small:
            in_specs.append(SMALL_SPEC)
        else:
            in_specs.append(whole(arg.shape))
    return pl.pallas_call(
        kernel,
        grid=(1,),
        out_shape=[jax.ShapeDtypeStruct(shape, kind) for shape, kind in outs],
        in_specs=in_specs,
        out_specs=[whole(shape) for shape, _ in outs],
        compiler_params=pltpu.CompilerParams(vmem_limit_bytes=44 * 2**20),
        cost_estimate=pl.CostEstimate(flops=flops, bytes_accessed=4 * 2**20, transcendentals=0),
    )(*args)


def exchange(rows):
    blocks = rows.reshape(DEV, rows.shape[0] // DEV, rows.shape[1])
    return lax.all_to_all(blocks, "fsdp", split_axis=0, concat_axis=0, tiled=True).reshape(rows.shape)


def twin(v):
    return lax.ppermute(v, "section", [(0, 1), (1, 0)])


def halves(qkv, out_proj, router, gains):
    pieces = []
    for c in range(2):
        pieces.append(
            jnp.concatenate(
                [
                    qkv[:, QW * c : QW * c + QW],
                    qkv[:, D + KW * c : D + KW * c + KW],
                    qkv[:, D + 2 * KW + KW * c : D + 2 * KW + KW * c + KW],
                    out_proj[:, QW * c : QW * c + QW],
                    router,
                    gains,
                    jnp.zeros((16, 128 - E - 2), BF16),
                ],
                1,
            )
        )
    return pieces


def rope_tables(segs):
    flat = segs.reshape(-1)
    tok = jnp.arange(2 * TOK, dtype=jnp.int32)
    same = (flat[:, None] == flat[None, :]) & (tok[:, None] // TOK == tok[None, :] // TOK)
    bias = jnp.where(same & (tok[None, :] <= tok[:, None]), 0.0, NEGATIVE).astype(F32)
    position = jnp.sum(jnp.where(same & (tok[None, :] < tok[:, None]), 1, 0), 1).astype(F32)
    frequency = jnp.exp(jnp.arange(HEAD // 2, dtype=F32) * (-2.0 * math.log(ROPE_BASE) / HEAD))
    angles = position[:, None] * frequency[None, :]
    cos, sin = jnp.cos(angles), jnp.sin(angles)
    cos = jnp.tile(jnp.concatenate([cos, cos], 1), (1, 8))
    sin = jnp.tile(jnp.concatenate([-sin, sin], 1), (1, 8))
    return cos, sin, bias


def placements(routes):
    flat = routes.T.reshape(-1)
    order = jnp.arange(2 * TOK, dtype=jnp.int32)
    earlier = (flat[:, None] == flat[None, :]) & (order[None, :] < order[:, None])
    rank = jnp.sum(jnp.where(earlier, 1, 0), 1)
    first = flat * (2 * SLOT) + rank
    row = jnp.arange(ROWS, dtype=jnp.int32)
    take = (row[None, :] == first[:, None]) | (row[None, :] == first[:, None] + SLOT)
    place = (row[:, None] == first[None, :]) | (row[:, None] == first[None, :] + SLOT)
    return take.astype(BF16), place.astype(BF16)


def shards(ends_in, routes, segments, norm_gains, w_qkv, w_attn_out, w_router, w_in, w_out):
    core = lax.axis_index("section")
    is_first = core == 0
    expert = (lax.axis_index("fsdp") // 2).astype(jnp.int32).reshape(1)

    def layers(mine, theirs):
        return jnp.where(is_first, mine, theirs), jnp.where(is_first, theirs, mine)

    def own_oth(pair):
        return jnp.where(is_first, pair[0], pair[1]), jnp.where(is_first, pair[1], pair[0])

    half0, half1 = halves(w_qkv[0], w_attn_out[0], w_router[0], norm_gains[0])
    kept, sent = own_oth((half0, half1))
    shard0, shard1 = layers(kept, twin(sent))
    w0 = exchange(jnp.tile(shard0, (DEV, 1)))
    w1 = lax.all_gather(shard1, "fsdp", axis=0, tiled=True)

    inputs, cotangent = layers(ends_in[0], twin(ends_in[0]))
    x0_own, x0_oth = own_oth(inputs)
    up1, _ = own_oth(cotangent)
    routes0, routes1 = layers(routes[0], twin(routes[0]))
    routes0, _ = own_oth(routes0)
    routes1, _ = own_oth(routes1)
    segs = jnp.stack(own_oth(segments[:, 0]))
    cos, sin, bias = rope_tables(segs)
    take0, place0 = placements(routes0)
    take1, place1 = placements(routes1)
    win0, win1 = layers(w_in[0], twin(w_in[0]))
    wout0, wout1 = layers(w_out[0], twin(w_out[0]))

    (early,) = call(early_kernel, [((ROWS, D + 128), BF16)], up1, routes1, place1)
    early = exchange(early)

    def attend(own, oth, w):
        return call(
            attend_kernel,
            [
                ((128, D), BF16),
                ((128, QW), BF16),
                ((128, KW), BF16),
                ((128, KW), BF16),
                ((1024, 128), F32),
                ((128, QW), BF16),
                ((TOK, D), F32),
                ((TOK, D), F32),
                ((8, D), F32),
            ],
            own, oth, w, cos, sin, bias,
        )

    def route(x, branch, recv, gains, w, route_ids, place):
        return call(
            route_kernel,
            [((TOK, D), F32), ((TOK, D), BF16), ((TOK, 128), F32), ((ROWS, PACK), BF16)],
            x, branch, recv, gains, w, route_ids, place,
            small=(4,),
        )

    def combine(returned, take, mid, gates):
        return call(
            combine_kernel,
            [((128, D), F32), ((TOK, D), F32), ((TOK, D), BF16)],
            returned, take, mid, gates,
        )

    weight_grads = [((UNITS, 2 * D), F32), ((UNITS, D), F32)]

    normed0, q0, k0, v0, p0, mix0, branch0, send0, gain0 = attend(x0_own, x0_oth, w0)
    mid0, ffn0, gate0, out0 = route(x0_own, branch0, twin(send0), gain0, w0, routes0, place0)
    rows0, pre0, upp0, back0 = call(
        expert_forward_kernel,
        [((ROWS, D), BF16), ((ROWS, UNITS), F32), ((ROWS, UNITS), F32), ((ROWS, PACK), BF16)],
        exchange(out0), win0, wout0,
    )
    picked0, _, x1_own = combine(exchange(back0), take0, mid0, gate0)
    x1_oth = twin(x1_own)

    normed1, q1, k1, v1, p1, mix1, branch1, send1, gain1 = attend(x1_own, x1_oth, w1)
    mid1, ffn1, gate1, out1 = route(x1_own, branch1, twin(send1), gain1, w1, routes1, place1)
    gin1, gout1, back1, exp1 = call(
        expert_both_kernel,
        weight_grads + [((ROWS, PACK + 128), BF16), ((ROWS, PACK), BF16)],
        expert, exchange(out1), early, w1, win1, wout1,
        small=(3,), scalar=(0,),
    )
    back1 = exchange(back1)
    _, result1, _ = combine(exchange(exp1), take1, mid1, gate1)

    def attend_back(gb, w, x_own, x_oth, saved, gains, sums):
        normed, q, k, v, p, mix = saved
        return call(
            attend_back_kernel,
            [((D, WIDE), BF16), ((TOK, D), F32), ((TOK, D), F32)],
            gb, twin(gb), x_own, x_oth, w, cos, sin, normed, q, k, v, p, mix, gains, sums,
        )

    token_outs = [((TOK, D), F32), ((TOK, D), BF16), ((E + 8, D), F32)]

    gmid1, gb1, sums1 = call(
        token_back_scored, token_outs,
        back1, take1, gate1, routes1, w1, ffn1, mid1, gain1, up1,
        small=(4,),
    )
    grad1, part1, psend1 = attend_back(
        gb1, w1, x1_own, x1_oth, (normed1, q1, k1, v1, p1, mix1), gain1, sums1
    )
    up0, gout_rows0 = call(
        input_back_send_kernel,
        [((TOK, D), BF16), ((ROWS, PACK), BF16)],
        part1, twin(psend1), x1_own, gain1, gmid1, gate0, place0,
    )

    gin0, gout0, gback0 = call(
        expert_backward_kernel,
        weight_grads + [((ROWS, PACK), BF16)],
        exchange(gout_rows0), rows0, pre0, upp0, win0, wout0,
    )
    gmid0, gb0, sums0 = call(
        token_back_picked, token_outs,
        exchange(gback0), take0, gate0, routes0, w0, ffn0, mid0, gain0, up0, picked0,
        small=(4,),
    )
    grad0, part0, psend0 = attend_back(
        gb0, w0, x0_own, x0_oth, (normed0, q0, k0, v0, p0, mix0), gain0, sums0
    )
    (grad_in0,) = call(
        input_back_kernel, [((TOK, D), F32)], part0, twin(psend0), x0_own, gain0, gmid0
    )

    def summed(grad):
        blocks = exchange(grad).reshape(DEV, 16, WIDE)
        return jnp.sum(blocks.astype(F32), 0)

    total0, total1 = summed(grad0), summed(grad1)
    keep, send = layers(total0, total1)
    got = twin(send)
    lower, upper = layers(keep, got)
    grad_qkv = jnp.concatenate(
        [lower[:, :QW], upper[:, :QW], lower[:, QW : QW + KW], upper[:, QW : QW + KW],
         lower[:, QW + KW : D], upper[:, QW + KW : D]], 1,
    )
    grad_attn_out = jnp.concatenate([lower[:, D:SMALL], upper[:, D:SMALL]], 1)
    rest = lower[:, SMALL:] + upper[:, SMALL:]

    def one_way(first, second):
        to_second = lax.ppermute(second, "section", [(0, 1)])
        to_first = lax.ppermute(first, "section", [(1, 0)])
        return jnp.where(is_first, first + to_first, second + to_second)

    grad_in = one_way(gin0, gin1)
    grad_out = one_way(gout0, gout1)

    keep, send = layers(grad_in0, result1)
    got = twin(send)
    ends_out = jnp.stack(layers(keep, got))
    return (
        ends_out[None],
        rest[None, :, E : E + 2],
        grad_qkv[None],
        grad_attn_out[None],
        rest[None, :, :E],
        grad_in[None],
        grad_out[None],
    )


def solution(mesh):
    tokens = P("section", None, "fsdp", None)
    weights = P("section", "fsdp", None)
    return jax.shard_map(
        shards,
        mesh=mesh,
        in_specs=(tokens, tokens, P(None, "fsdp", None)) + (weights,) * 6,
        out_specs=(tokens,) + (weights,) * 6,
        check_vma=False,
    )
```

```python
import math

import jax
import jax.numpy as jnp
from jax import lax
from jax.experimental import pallas as pl
from jax.experimental.pallas import tpu as pltpu
from jax.sharding import PartitionSpec as P

D = 1024
HEADS = 16
KV_HEADS = 8
HEAD = 64
E = 32
CAP = 6
TOK = 64
DEV = 64
SLOT = 8
ROWS = DEV * SLOT
PACK = 768
TAIL = D - PACK
WIDE = 1664
SMALL = 1536
QW = 512
KW = 256
GROUPS = 4
UNITS = 256
EPSILON = 1e-06
ROPE_BASE = 10000.0
NEGATIVE = -1e30
F32 = jnp.float32
BF16 = jnp.bfloat16
GRANT = 60


def nn(a, b):
    return lax.dot_general(a, b, (((1,), (0,)), ((), ())), preferred_element_type=F32)


def nt(a, b):
    return lax.dot_general(a, b, (((1,), (1,)), ((), ())), preferred_element_type=F32)


def tn(a, b):
    return lax.dot_general(a, b, (((0,), (0,)), ((), ())), preferred_element_type=F32)


def row_in_slot(shape):
    return lax.broadcasted_iota(jnp.int32, shape, 0) % SLOT


def tail_moves():
    row = lax.broadcasted_iota(jnp.int32, (128, 384), 0)
    col = lax.broadcasted_iota(jnp.int32, (128, 384), 1)
    piece, col = col // 128, col % 128
    slot, kept = row % SLOT, col % SLOT
    hit = ((kept == CAP) & (slot == piece)) | ((kept == CAP + 1) & (slot == piece + 3))
    return jnp.where(hit & (row // SLOT == col // SLOT), 1.0, 0.0).astype(BF16)


def unpack(packed):
    moves = tail_moves()
    main = jnp.where(row_in_slot((ROWS, PACK)) < CAP, packed.astype(F32), 0.0).astype(BF16)
    tails = []
    for block in range(0, ROWS, 128):
        part = packed[block : block + 128]
        stacked = jnp.concatenate([part[:, 256 * j : 256 * j + 256] for j in range(3)], 0)
        tails.append(nn(moves, stacked).astype(BF16))
    return jnp.concatenate([main, jnp.concatenate(tails, 0)], 1)


def pack(rows):
    moves = tail_moves()
    keep = row_in_slot((128, 256)) < CAP
    blocks = []
    for block in range(0, ROWS, 128):
        part = rows[block : block + 128]
        tail = tn(moves, part[:, PACK:])
        pieces = []
        for j in range(3):
            main = part[:, 256 * j : 256 * j + 256].astype(F32)
            pieces.append(jnp.where(keep, main, tail[128 * j : 128 * j + 128]).astype(BF16))
        blocks.append(jnp.concatenate(pieces, 1))
    return jnp.concatenate(blocks, 0)


def inverse_rms(x):
    return lax.rsqrt(jnp.mean(x * x, -1, keepdims=True) + EPSILON)


def norm_back(x, gain, grad):
    inv = inverse_rms(x)
    unit = x * inv
    scaled = grad * gain
    dx = inv * (scaled - unit * jnp.mean(scaled * unit, -1, keepdims=True))
    return dx, jnp.sum(grad * unit, 0, keepdims=True)


def half_swap(v):
    width = v.shape[1]
    lane = lax.broadcasted_iota(jnp.int32, v.shape, 1) % HEAD
    return jnp.where(
        lane < HEAD // 2,
        pltpu.roll(v, width - HEAD // 2, 1),
        pltpu.roll(v, HEAD // 2, 1),
    )


def at_lane(shape, lane, value, base):
    return jnp.where(lax.broadcasted_iota(jnp.int32, shape, 1) == lane, value, base)


def attend_kernel(own, oth, w, cos, sin, bias, normed_o, q_o, k_o, v_o, p_o, mix_o, branch_o, send_o, gain_o):
    x = jnp.concatenate([own[...].astype(F32), oth[...].astype(F32)], 0)
    small = w[:, SMALL:].astype(F32).T
    gains = small[E : E + 8]
    gain_o[...] = gains
    normed = (x * inverse_rms(x) * gains[0:1]).astype(BF16)
    normed_o[...] = normed
    proj = nn(normed, w[:, :D])
    q = proj[:, :QW]
    k = proj[:, QW : QW + KW]
    v = proj[:, QW + KW :].astype(BF16)
    q = (q * cos[...] + half_swap(q) * sin[...]).astype(BF16)
    k = (k * cos[:, :KW] + half_swap(k) * sin[:, :KW]).astype(BF16)
    q_o[...] = q
    k_o[...] = k
    v_o[...] = v
    mask = bias[...]
    mixed = []
    for h in range(2 * GROUPS):
        g = h // 2
        q_h = q[:, HEAD * h : HEAD * h + HEAD]
        k_g = k[:, HEAD * g : HEAD * g + HEAD]
        v_g = v[:, HEAD * g : HEAD * g + HEAD]
        s = nt(q_h, k_g) * (1.0 / math.sqrt(HEAD)) + mask
        top = jnp.max(s, -1, keepdims=True)
        ex = jnp.exp(s - top)
        p = ex / jnp.sum(ex, -1, keepdims=True)
        p_o[128 * h : 128 * h + 128, :] = p
        mixed.append(nn(p.astype(BF16), v_g))
    mixed = jnp.concatenate(mixed, 1).astype(BF16)
    mix_o[...] = mixed
    branch = nt(mixed, w[:, D:SMALL])
    branch_o[...] = branch[:TOK]
    send_o[...] = branch[TOK:]


def route_rows(x, branch, recv, gains, small, routes, place, mid_o, normed_o, gate_o, out_o):
    mid = x[...].astype(F32) + branch[...] + recv[...]
    mid_o[...] = mid
    normed = (mid * inverse_rms(mid) * gains[1:2]).astype(BF16)
    normed_o[...] = normed
    logits = nn(normed, small[...])
    lane = lax.broadcasted_iota(jnp.int32, (TOK, 128), 1)
    l0 = jnp.sum(jnp.where(lane == routes[:, 0:1], logits, 0.0), -1, keepdims=True)
    l1 = jnp.sum(jnp.where(lane == routes[:, 1:2], logits, 0.0), -1, keepdims=True)
    top = jnp.maximum(l0, l1)
    e0, e1 = jnp.exp(l0 - top), jnp.exp(l1 - top)
    total = e0 + e1
    gate_o[...] = at_lane((TOK, 128), 0, e0 / total, at_lane((TOK, 128), 1, e1 / total, 0.0))
    rows = nn(place[...], jnp.concatenate([normed, normed], 0)).astype(BF16)
    out_o[:, :PACK] = pack(rows)
    return e0 / total, e1 / total


def route_kernel(*refs):
    route_rows(*refs)


def route_both_kernel(x, branch, recv, gains, small, routes, place, up, mid_o, normed_o, gate_o, out_o):
    g0, g1 = route_rows(x, branch, recv, gains, small, routes, place, mid_o, normed_o, gate_o, out_o)
    u = up[...]
    rows = jnp.concatenate([g0 * u, g1 * u], 0).astype(BF16)
    out_o[:, PACK:] = pack(nn(place[...], rows).astype(BF16))


def expert_forward_kernel(arrived, w_in, w_out, rows_o, gate_o, up_o, out_o):
    rows = unpack(arrived[...])
    rows_o[...] = rows
    gate = nt(rows, w_in[:, :D])
    up = nt(rows, w_in[:, D:])
    gate_o[...] = gate
    up_o[...] = up
    hidden = (gate * (1.0 / (1.0 + jnp.exp(-gate))) * up).astype(BF16)
    out_o[...] = pack(nn(hidden, w_out[...]).astype(BF16))


def expert_grads(rows, grads, gate, up, w_in, w_out, in_o, outw_o):
    sig = 1.0 / (1.0 + jnp.exp(-gate))
    act = gate * sig
    hidden = (act * up).astype(BF16)
    grad_hidden = nt(grads, w_out[...])
    g_gate = (grad_hidden * up * sig * (1.0 + gate * (1.0 - sig))).astype(BF16)
    g_up = (grad_hidden * act).astype(BF16)
    grad_rows = nn(g_gate, w_in[:, :D]) + nn(g_up, w_in[:, D:])
    outw_o[...] = tn(hidden, grads)
    in_o[:, :D] = tn(g_gate, rows)
    in_o[:, D:] = tn(g_up, rows)
    return hidden, grad_rows


def expert_both_kernel(arrived, w_in, w_out, in_o, outw_o, back_o):
    rows = unpack(arrived[:, :PACK])
    grads = unpack(arrived[:, PACK:])
    gate = nt(rows, w_in[:, :D])
    up = nt(rows, w_in[:, D:])
    hidden, grad_rows = expert_grads(rows, grads, gate, up, w_in, w_out, in_o, outw_o)
    back_o[:, :PACK] = pack(grad_rows.astype(BF16))
    back_o[:, PACK:] = pack(nn(hidden, w_out[...]).astype(BF16))


def expert_backward_kernel(arrived, rows, gate, up, w_in, w_out, in_o, outw_o, back_o):
    grads = unpack(arrived[...])
    _, grad_rows = expert_grads(rows[...], grads, gate[...], up[...], w_in, w_out, in_o, outw_o)
    back_o[...] = pack(grad_rows.astype(BF16))


def combine_kernel(returned, take, mid, gates, picked_o, low_o):
    picked = nn(take[...], unpack(returned[...]))
    picked_o[...] = picked
    out = mid[...] + gates[:, 0:1] * picked[:TOK] + gates[:, 1:2] * picked[TOK:]
    low_o[...] = out.astype(BF16)


def gate_back(s0, s1, gates, routes, small, returned, take, normed, mid, gains, up, gmid_o, branch_o, sums_o):
    g0, g1 = gates[:, 0:1], gates[:, 1:2]
    mean = g0 * s0 + g1 * s1
    lane = lax.broadcasted_iota(jnp.int32, (TOK, 128), 1)
    grad_logits = (
        jnp.where(lane == routes[:, 0:1], g0 * (s0 - mean), 0.0)
        + jnp.where(lane == routes[:, 1:2], g1 * (s1 - mean), 0.0)
    ).astype(BF16)
    both = (take[:TOK, :].astype(F32) + take[TOK:, :].astype(F32)).astype(BF16)
    grad_ffn = nt(grad_logits, small[...]) + nn(both, unpack(returned[:, :PACK]))
    dx, dgain = norm_back(mid[...], gains[1:2], grad_ffn)
    grad_mid = up[...].astype(F32) + dx
    gmid_o[...] = grad_mid
    branch_o[...] = grad_mid.astype(BF16)
    router = tn(grad_logits, normed[...])[:E]
    row = lax.broadcasted_iota(jnp.int32, (8, D), 0)
    sums_o[...] = jnp.concatenate([router, jnp.where(row == 1, dgain, 0.0)], 0)


def token_back_kernel(returned, take, gates, routes, small, normed, mid, gains, up, picked, gmid_o, branch_o, sums_o):
    u = up[...].astype(F32)
    s0 = jnp.sum(u * picked[:TOK, :], -1, keepdims=True)
    s1 = jnp.sum(u * picked[TOK:, :], -1, keepdims=True)
    gate_back(s0, s1, gates, routes, small, returned, take, normed, mid, gains, up, gmid_o, branch_o, sums_o)


def token_both_kernel(returned, take, gates, routes, small, normed, mid, gains, up, gmid_o, branch_o, sums_o, out_o):
    picked = nn(take[...], unpack(returned[:, PACK:]))
    out_o[...] = mid[...] + gates[:, 0:1] * picked[:TOK] + gates[:, 1:2] * picked[TOK:]
    token_back_kernel(returned, take, gates, routes, small, normed, mid, gains, up, picked, gmid_o, branch_o, sums_o)


def attend_back(own, oth, x_own, x_oth, w, cos, sin, q, k, v, p, gains, sums, part_o, send_o):
    scale = 1.0 / math.sqrt(HEAD)
    branch = jnp.concatenate([own[...], oth[...]], 0)
    grad_mixed = nn(branch, w[:, D:SMALL]).astype(BF16)
    d_q, d_k, d_v = [], [], []
    for g in range(GROUPS):
        k_g = k[:, HEAD * g : HEAD * g + HEAD]
        v_g = v[:, HEAD * g : HEAD * g + HEAD]
        dk = dv = 0.0
        for h in (2 * g, 2 * g + 1):
            q_h = q[:, HEAD * h : HEAD * h + HEAD]
            gm = grad_mixed[:, HEAD * h : HEAD * h + HEAD]
            ph = p[128 * h : 128 * h + 128, :]
            dp = nt(gm, v_g)
            ds = (ph * (dp - jnp.sum(ph * dp, -1, keepdims=True))).astype(BF16)
            d_q.append(nn(ds, k_g) * scale)
            dk = dk + tn(ds, q_h)
            dv = dv + tn(ph.astype(BF16), gm)
        d_k.append(dk * scale)
        d_v.append(dv)
    d_q = jnp.concatenate(d_q, 1)
    d_k = jnp.concatenate(d_k, 1)
    d_v = jnp.concatenate(d_v, 1)
    d_q = d_q * cos[...] - half_swap(d_q) * sin[...]
    d_k = d_k * cos[:, :KW] - half_swap(d_k) * sin[:, :KW]
    grad_proj = jnp.concatenate([d_q, d_k, d_v], 1).astype(BF16)
    grad_normed = nt(grad_proj, w[:, :D])
    part_o[...] = grad_normed[:TOK]
    send_o[...] = grad_normed[TOK:]
    x = jnp.concatenate([x_own[...].astype(F32), x_oth[...].astype(F32)], 0)
    dgain = jnp.sum(grad_normed * (x * inverse_rms(x)), 0, keepdims=True)
    row = lax.broadcasted_iota(jnp.int32, (E + 8, D), 0)
    return branch, grad_proj, jnp.where(row == E, dgain, sums[...])


def attend_back_share_kernel(own, oth, x_own, x_oth, w, cos, sin, q, k, v, p, gains, sums, normed, mixed, acts_o, part_o, send_o, sums_o):
    branch, grad_proj, sums_o[...] = attend_back(
        own, oth, x_own, x_oth, w, cos, sin, q, k, v, p, gains, sums, part_o, send_o
    )
    acts_o[:, :D] = normed[...]
    acts_o[:, D : 2 * D] = branch
    acts_o[:, 2 * D : 3 * D] = grad_proj
    acts_o[:, 3 * D :] = mixed[...]


def attend_back_sum_kernel(own, oth, x_own, x_oth, w, cos, sin, q, k, v, p, gains, sums, normed, mixed, other, grad_o, part_o, send_o):
    branch, grad_proj, full = attend_back(
        own, oth, x_own, x_oth, w, cos, sin, q, k, v, p, gains, sums, part_o, send_o
    )
    grad_o[:, :D] = tn(normed[...], grad_proj).astype(BF16)
    grad_o[:, D:SMALL] = tn(branch, mixed[...]).astype(BF16)
    pad = jnp.zeros((64 - E - 8, D), F32)
    grad_o[:, SMALL:] = jnp.concatenate([full, pad, other[...], pad], 0).T.astype(BF16)


def share_grad_kernel(y, acts, grad_o):
    row = lax.broadcasted_iota(jnp.int32, (D, D // 4), 0)
    col = lax.broadcasted_iota(jnp.int32, (D, D // 4), 1)
    mine = jnp.where(row == col // 16 * 64 + y[0] * 16 + col % 16, 1.0, 0.0).astype(BF16)
    normed = nn(acts[:, :D], mine).astype(BF16)
    branch = nn(acts[:, D : 2 * D], mine).astype(BF16)
    grad_o[:, :D] = tn(normed, acts[:, 2 * D : 3 * D]).astype(BF16)
    grad_o[:, D:] = tn(branch, acts[:, 3 * D :]).astype(BF16)


def input_back_kernel(part, recv, x, gains, gmid, out_o):
    dx, _ = norm_back(x[...].astype(F32), gains[0:1], part[...] + recv[...])
    out_o[...] = gmid[...] + dx


def input_back_send_kernel(part, recv, x, gains, gmid, gates, place, up_o, out_o):
    dx, _ = norm_back(x[...].astype(F32), gains[0:1], part[...] + recv[...])
    up = (gmid[...] + dx).astype(BF16)
    up_o[...] = up
    up = up.astype(F32)
    rows = jnp.concatenate([gates[:, 0:1] * up, gates[:, 1:2] * up], 0).astype(BF16)
    out_o[...] = pack(nn(place[...], rows).astype(BF16))


def whole(shape):
    return pl.BlockSpec(shape, lambda i: (0,) * len(shape))


SMALL_SPEC = pl.BlockSpec((D, 128), lambda i: (0, SMALL // 128))


def call(kernel, outs, *args, small=(), scalar=(), flops=10**9):
    in_specs = []
    for n, arg in enumerate(args):
        if n in scalar:
            in_specs.append(pl.BlockSpec(memory_space=pltpu.SMEM))
        else:
            in_specs.append(SMALL_SPEC if n in small else whole(arg.shape))
    return pl.pallas_call(
        kernel,
        grid=(1,),
        out_shape=[jax.ShapeDtypeStruct(shape, kind) for shape, kind in outs],
        in_specs=in_specs,
        out_specs=[whole(shape) for shape, _ in outs],
        compiler_params=pltpu.CompilerParams(vmem_limit_bytes=GRANT * 2**20),
        cost_estimate=pl.CostEstimate(flops=flops, bytes_accessed=4 * 2**20, transcendentals=0),
    )(*args)


def exchange(rows):
    blocks = rows.reshape(DEV, rows.shape[0] // DEV, rows.shape[1])
    return lax.all_to_all(blocks, "fsdp", split_axis=0, concat_axis=0, tiled=True).reshape(rows.shape)


def along(span):
    first = [i for i in range(DEV) if i // span % 4 == 0]
    return [[i + span * k for k in range(4)] for i in first]


def staged(rows, place):
    for span in (16, 4):
        blocks = rows.reshape(4, rows.shape[0] // 4, rows.shape[1])
        here = place // span % 4
        total = lax.dynamic_index_in_dim(blocks, here, 0, keepdims=False).astype(F32)
        for by in (1, 2, 3):
            pairs = [(g[k], g[(k + by) % 4]) for g in along(span) for k in range(4)]
            block = lax.dynamic_index_in_dim(blocks, (here + by) % 4, 0, keepdims=False)
            total = total + lax.ppermute(block, "fsdp", pairs).astype(F32)
        rows = total if span == 4 else total.astype(BF16)
    return rows


def twin(v):
    return lax.ppermute(v, "section", [(0, 1), (1, 0)])


def halves(qkv, out_proj, router, gains):
    pieces = []
    for c in range(2):
        pieces.append(
            jnp.concatenate(
                [
                    qkv[:, QW * c : QW * c + QW],
                    qkv[:, D + KW * c : D + KW * c + KW],
                    qkv[:, D + 2 * KW + KW * c : D + 2 * KW + KW * c + KW],
                    out_proj[:, QW * c : QW * c + QW],
                    router,
                    gains,
                    jnp.zeros((16, 128 - E - 2), BF16),
                ],
                1,
            )
        )
    return pieces


def rope_tables(segs):
    flat = segs.reshape(-1)
    tok = jnp.arange(2 * TOK, dtype=jnp.int32)
    same = (flat[:, None] == flat[None, :]) & (tok[:, None] // TOK == tok[None, :] // TOK)
    bias = jnp.where(same & (tok[None, :] <= tok[:, None]), 0.0, NEGATIVE).astype(F32)
    position = jnp.sum(jnp.where(same & (tok[None, :] < tok[:, None]), 1, 0), 1).astype(F32)
    frequency = jnp.exp(jnp.arange(HEAD // 2, dtype=F32) * (-2.0 * math.log(ROPE_BASE) / HEAD))
    angles = position[:, None] * frequency[None, :]
    cos, sin = jnp.cos(angles), jnp.sin(angles)
    cos = jnp.tile(jnp.concatenate([cos, cos], 1), (1, 8))
    sin = jnp.tile(jnp.concatenate([-sin, sin], 1), (1, 8))
    return cos, sin, bias


def placements(routes):
    flat = routes.T.reshape(-1)
    order = jnp.arange(2 * TOK, dtype=jnp.int32)
    earlier = (flat[:, None] == flat[None, :]) & (order[None, :] < order[:, None])
    rank = jnp.sum(jnp.where(earlier, 1, 0), 1)
    first = flat * (2 * SLOT) + rank
    row = jnp.arange(ROWS, dtype=jnp.int32)
    take = (row[None, :] == first[:, None]) | (row[None, :] == first[:, None] + SLOT)
    place = (row[:, None] == first[None, :]) | (row[:, None] == first[None, :] + SLOT)
    return take.astype(BF16), place.astype(BF16)


def shards(ends_in, routes, segments, norm_gains, w_qkv, w_attn_out, w_router, w_in, w_out):
    core = lax.axis_index("section")
    is_first = core == 0

    def layers(mine, theirs):
        return jnp.where(is_first, mine, theirs), jnp.where(is_first, theirs, mine)

    def own_oth(pair):
        return jnp.where(is_first, pair[0], pair[1]), jnp.where(is_first, pair[1], pair[0])

    half0, half1 = halves(w_qkv[0], w_attn_out[0], w_router[0], norm_gains[0])
    kept, sent = own_oth((half0, half1))
    shard0, shard1 = layers(kept, twin(sent))
    w0 = exchange(jnp.tile(shard0, (DEV, 1)))
    w0, shard1 = lax.optimization_barrier((w0, shard1))
    w1 = lax.all_gather(shard1, "fsdp", axis=0, tiled=True)

    inputs, cotangent = layers(ends_in[0], twin(ends_in[0]))
    x0_own, x0_oth = own_oth(inputs)
    up1, _ = own_oth(cotangent)
    routes0, routes1 = layers(routes[0], twin(routes[0]))
    routes0, _ = own_oth(routes0)
    routes1, _ = own_oth(routes1)
    segs = jnp.stack(own_oth(segments[:, 0]))
    cos, sin, bias = rope_tables(segs)
    take0, place0 = placements(routes0)
    take1, place1 = placements(routes1)
    win0, win1 = layers(w_in[0], twin(w_in[0]))
    wout0, wout1 = layers(w_out[0], twin(w_out[0]))

    def attend(own, oth, w):
        return call(
            attend_kernel,
            [
                ((128, D), BF16),
                ((128, QW), BF16),
                ((128, KW), BF16),
                ((128, KW), BF16),
                ((1024, 128), F32),
                ((128, QW), BF16),
                ((TOK, D), F32),
                ((TOK, D), F32),
                ((8, D), F32),
            ],
            own, oth, w, cos, sin, bias,
        )

    def route(kernel, width, *args):
        return call(
            kernel,
            [((TOK, D), F32), ((TOK, D), BF16), ((TOK, 128), F32), ((ROWS, width), BF16)],
            *args,
            small=(4,),
        )

    weight_grads = [((UNITS, 2 * D), F32), ((UNITS, D), F32)]

    normed0, q0, k0, v0, p0, mix0, branch0, send0, gain0 = attend(x0_own, x0_oth, w0)
    mid0, ffn0, gate0, out0 = route(
        route_kernel, PACK, x0_own, branch0, twin(send0), gain0, w0, routes0, place0
    )
    rows0, pre0, upp0, back0 = call(
        expert_forward_kernel,
        [((ROWS, D), BF16), ((ROWS, UNITS), F32), ((ROWS, UNITS), F32), ((ROWS, PACK), BF16)],
        exchange(out0), win0, wout0,
    )
    picked0, x1_own = call(
        combine_kernel,
        [((128, D), F32), ((TOK, D), BF16)],
        exchange(back0), take0, mid0, gate0,
    )
    x1_oth = twin(x1_own)

    normed1, q1, k1, v1, p1, mix1, branch1, send1, gain1 = attend(x1_own, x1_oth, w1)
    mid1, ffn1, gate1, out1 = route(
        route_both_kernel, 2 * PACK, x1_own, branch1, twin(send1), gain1, w1, routes1, place1, up1
    )
    gin1, gout1, back1 = call(
        expert_both_kernel,
        weight_grads + [((ROWS, 2 * PACK), BF16)],
        exchange(out1), win1, wout1,
    )
    back1 = exchange(back1)
    gin1_got = lax.ppermute(gin1, "section", [(0, 1)])
    gout1_got = lax.ppermute(gout1, "section", [(0, 1)])
    back1, gin1_got, gout1_got = lax.optimization_barrier((back1, gin1_got, gout1_got))

    token_outs = [((TOK, D), F32), ((TOK, D), BF16), ((E + 8, D), F32)]

    gmid1, gb1, sums1, result1 = call(
        token_both_kernel, token_outs + [((TOK, D), F32)],
        back1, take1, gate1, routes1, w1, ffn1, mid1, gain1, up1,
        small=(4,),
    )
    acts1, part1, psend1, sums1 = call(
        attend_back_share_kernel,
        [((128, 7 * D // 2), BF16), ((TOK, D), F32), ((TOK, D), F32), ((E + 8, D), F32)],
        gb1, twin(gb1), x1_own, x1_oth, w1, cos, sin, q1, k1, v1, p1, gain1, sums1, normed1, mix1,
    )
    acts1 = lax.all_gather(acts1, "fsdp", axis=0, tiled=True, axis_index_groups=along(1))
    up0, gout_rows0 = call(
        input_back_send_kernel,
        [((TOK, D), BF16), ((ROWS, PACK), BF16)],
        part1, twin(psend1), x1_own, gain1, gmid1, gate0, place0,
    )

    gin0, gout0, gback0 = call(
        expert_backward_kernel,
        weight_grads + [((ROWS, PACK), BF16)],
        exchange(gout_rows0), rows0, pre0, upp0, win0, wout0,
    )
    gback0 = exchange(gback0)
    gin0_got = lax.ppermute(gin0, "section", [(1, 0)])
    gout0_got = lax.ppermute(gout0, "section", [(1, 0)])
    grad_in = jnp.where(is_first, gin0 + gin0_got, gin1 + gin1_got)
    grad_out = jnp.where(is_first, gout0 + gout0_got, gout1 + gout1_got)
    gback0, grad_in, grad_out = lax.optimization_barrier((gback0, grad_in, grad_out))
    gmid0, gb0, sums0 = call(
        token_back_kernel, token_outs,
        gback0, take0, gate0, routes0, w0, ffn0, mid0, gain0, up0, picked0,
        small=(4,),
    )
    grads, part0, psend0 = call(
        attend_back_sum_kernel,
        [((D, WIDE), BF16), ((TOK, D), F32), ((TOK, D), F32)],
        gb0, twin(gb0), x0_own, x0_oth, w0, cos, sin, q0, k0, v0, p0, gain0, sums0, normed0, mix0, sums1,
    )
    place = lax.axis_index("fsdp")
    (share1,) = call(
        share_grad_kernel, [((D // 4, SMALL), BF16)],
        (place % 4).astype(jnp.int32).reshape(1), acts1, scalar=(0,),
    )
    total1 = staged(share1, place)
    (grad_in0,) = call(
        input_back_kernel, [((TOK, D), F32)], part0, twin(psend0), x0_own, gain0, gmid0
    )

    total0 = jnp.sum(exchange(grads).reshape(DEV, 16, WIDE).astype(F32), 0)
    rest0, rest1 = total0[:, SMALL : SMALL + 64], total0[:, SMALL + 64 :]
    keep, send = layers(
        jnp.concatenate([total0[:, :SMALL], rest0], 1), jnp.concatenate([total1, rest1], 1)
    )
    got = twin(send)
    lower, upper = layers(keep, got)
    grad_qkv = jnp.concatenate(
        [lower[:, :QW], upper[:, :QW], lower[:, QW : QW + KW], upper[:, QW : QW + KW],
         lower[:, QW + KW : D], upper[:, QW + KW : D]], 1,
    )
    grad_attn_out = jnp.concatenate([lower[:, D:SMALL], upper[:, D:SMALL]], 1)
    rest = lower[:, SMALL:] + upper[:, SMALL:]

    keep, send = layers(grad_in0, result1)
    got = twin(send)
    ends_out = jnp.stack(layers(keep, got))
    return (
        ends_out[None],
        rest[None, :, E : E + 2],
        grad_qkv[None],
        grad_attn_out[None],
        rest[None, :, :E],
        grad_in[None],
        grad_out[None],
    )


def solution(mesh):
    tokens = P("section", None, "fsdp", None)
    weights = P("section", "fsdp", None)
    return jax.shard_map(
        shards,
        mesh=mesh,
        in_specs=(tokens, tokens, P(None, "fsdp", None)) + (weights,) * 6,
        out_specs=(tokens,) + (weights,) * 6,
        check_vma=False,
    )
```

```python
import math

import jax
import jax.numpy as jnp
from jax import lax
from jax.experimental import pallas as pl
from jax.experimental.pallas import tpu as pltpu
from jax.sharding import PartitionSpec as P

D = 1024
HEADS = 16
KV_HEADS = 8
HEAD = 64
E = 32
CAP = 6
TOK = 64
DEV = 64
SLOT = 8
ROWS = DEV * SLOT
PACK = 768
TAIL = D - PACK
WIDE = 1664
SMALL = 1536
SHARE = 384
QW = 512
KW = 256
GROUPS = 4
UNITS = 256
EPSILON = 1e-06
ROPE_BASE = 10000.0
NEGATIVE = -1e30
F32 = jnp.float32
BF16 = jnp.bfloat16


def nn(a, b):
    return lax.dot_general(a, b, (((1,), (0,)), ((), ())), preferred_element_type=F32)


def nt(a, b):
    return lax.dot_general(a, b, (((1,), (1,)), ((), ())), preferred_element_type=F32)


def tn(a, b):
    return lax.dot_general(a, b, (((0,), (0,)), ((), ())), preferred_element_type=F32)


def row_in_slot(shape):
    return lax.broadcasted_iota(jnp.int32, shape, 0) % SLOT


def tail_moves():
    row = lax.broadcasted_iota(jnp.int32, (128, 384), 0)
    col = lax.broadcasted_iota(jnp.int32, (128, 384), 1)
    piece, col = col // 128, col % 128
    slot, kept = row % SLOT, col % SLOT
    hit = ((kept == CAP) & (slot == piece)) | ((kept == CAP + 1) & (slot == piece + 3))
    return jnp.where(hit & (row // SLOT == col // SLOT), 1.0, 0.0).astype(BF16)


def unpack(packed):
    moves = tail_moves()
    main = jnp.where(row_in_slot((ROWS, PACK)) < CAP, packed.astype(F32), 0.0).astype(BF16)
    tails = []
    for block in range(0, ROWS, 128):
        part = packed[block : block + 128]
        stacked = jnp.concatenate([part[:, 256 * j : 256 * j + 256] for j in range(3)], 0)
        tails.append(nn(moves, stacked).astype(BF16))
    return jnp.concatenate([main, jnp.concatenate(tails, 0)], 1)


def pack(rows):
    moves = tail_moves()
    keep = row_in_slot((128, 256)) < CAP
    blocks = []
    for block in range(0, ROWS, 128):
        part = rows[block : block + 128]
        tail = tn(moves, part[:, PACK:])
        pieces = []
        for j in range(3):
            main = part[:, 256 * j : 256 * j + 256].astype(F32)
            pieces.append(jnp.where(keep, main, tail[128 * j : 128 * j + 128]).astype(BF16))
        blocks.append(jnp.concatenate(pieces, 1))
    return jnp.concatenate(blocks, 0)


def inverse_rms(x):
    return lax.rsqrt(jnp.mean(x * x, -1, keepdims=True) + EPSILON)


def norm_back(x, gain, grad):
    inv = inverse_rms(x)
    unit = x * inv
    scaled = grad * gain
    dx = inv * (scaled - unit * jnp.mean(scaled * unit, -1, keepdims=True))
    return dx, jnp.sum(grad * unit, 0, keepdims=True)


def half_swap(v):
    width = v.shape[1]
    lane = lax.broadcasted_iota(jnp.int32, v.shape, 1) % HEAD
    return jnp.where(
        lane < HEAD // 2,
        pltpu.roll(v, width - HEAD // 2, 1),
        pltpu.roll(v, HEAD // 2, 1),
    )


def at_lane(shape, lane, value, base):
    return jnp.where(lax.broadcasted_iota(jnp.int32, shape, 1) == lane, value, base)


def attend_kernel(own, oth, w, cos, sin, bias, normed_o, q_o, k_o, v_o, p_o, mix_o, branch_o, send_o, gain_o):
    x = jnp.concatenate([own[...].astype(F32), oth[...].astype(F32)], 0)
    small = w[:, SMALL:].astype(F32).T
    gains = small[E : E + 8]
    gain_o[...] = gains
    normed = (x * inverse_rms(x) * gains[0:1]).astype(BF16)
    normed_o[...] = normed
    proj = nn(normed, w[:, :D])
    q = proj[:, :QW]
    k = proj[:, QW : QW + KW]
    v = proj[:, QW + KW :].astype(BF16)
    cos = jnp.concatenate([cos[...]] * GROUPS, 1)
    sin = jnp.concatenate([sin[...]] * GROUPS, 1)
    q = (q * cos + half_swap(q) * sin).astype(BF16)
    k = (k * cos[:, :KW] + half_swap(k) * sin[:, :KW]).astype(BF16)
    q_o[...] = q
    k_o[...] = k
    v_o[...] = v
    mask = bias[...]
    mixed = []
    for h in range(2 * GROUPS):
        g = h // 2
        q_h = q[:, HEAD * h : HEAD * h + HEAD]
        k_g = k[:, HEAD * g : HEAD * g + HEAD]
        v_g = v[:, HEAD * g : HEAD * g + HEAD]
        s = nt(q_h, k_g) * (1.0 / math.sqrt(HEAD)) + mask
        top = jnp.max(s, -1, keepdims=True)
        ex = jnp.exp(s - top)
        p = ex / jnp.sum(ex, -1, keepdims=True)
        p_o[128 * h : 128 * h + 128, :] = p
        mixed.append(nn(p.astype(BF16), v_g))
    mixed = jnp.concatenate(mixed, 1).astype(BF16)
    mix_o[...] = mixed
    branch = nt(mixed, w[:, D:SMALL])
    branch_o[...] = branch[:TOK]
    send_o[...] = branch[TOK:]


def route_rows(x, branch, recv, gains, small, routes, place, mid_o, normed_o, gate_o, out_o):
    mid = x[...].astype(F32) + branch[...] + recv[...]
    mid_o[...] = mid
    normed = (mid * inverse_rms(mid) * gains[1:2]).astype(BF16)
    normed_o[...] = normed
    logits = nn(normed, small[...])
    lane = lax.broadcasted_iota(jnp.int32, (TOK, 128), 1)
    l0 = jnp.sum(jnp.where(lane == routes[:, 0:1], logits, 0.0), -1, keepdims=True)
    l1 = jnp.sum(jnp.where(lane == routes[:, 1:2], logits, 0.0), -1, keepdims=True)
    top = jnp.maximum(l0, l1)
    e0, e1 = jnp.exp(l0 - top), jnp.exp(l1 - top)
    total = e0 + e1
    gate_o[...] = at_lane((TOK, 128), 0, e0 / total, at_lane((TOK, 128), 1, e1 / total, 0.0))
    rows = nn(place[...], jnp.concatenate([normed, normed], 0)).astype(BF16)
    out_o[:, :PACK] = pack(rows)
    return e0 / total, e1 / total


def route_kernel(*refs):
    route_rows(*refs)


def route_both_kernel(x, branch, recv, gains, small, routes, place, up, mid_o, normed_o, gate_o, out_o):
    g0, g1 = route_rows(x, branch, recv, gains, small, routes, place, mid_o, normed_o, gate_o, out_o)
    u = up[...]
    rows = jnp.concatenate([g0 * u, g1 * u], 0).astype(BF16)
    out_o[:, PACK:] = pack(nn(place[...], rows).astype(BF16))


def expert_forward_kernel(arrived, w_in, w_out, rows_o, gate_o, up_o, out_o):
    rows = unpack(arrived[...])
    rows_o[...] = rows
    gate = nt(rows, w_in[:, :D])
    up = nt(rows, w_in[:, D:])
    gate_o[...] = gate
    up_o[...] = up
    hidden = (gate * (1.0 / (1.0 + jnp.exp(-gate))) * up).astype(BF16)
    out_o[...] = pack(nn(hidden, w_out[...]).astype(BF16))


def expert_grads(rows, grads, gate, up, w_in, w_out, in_o, outw_o):
    sig = 1.0 / (1.0 + jnp.exp(-gate))
    act = gate * sig
    hidden = (act * up).astype(BF16)
    grad_hidden = nt(grads, w_out[...])
    g_gate = (grad_hidden * up * sig * (1.0 + gate * (1.0 - sig))).astype(BF16)
    g_up = (grad_hidden * act).astype(BF16)
    grad_rows = nn(g_gate, w_in[:, :D]) + nn(g_up, w_in[:, D:])
    outw_o[...] = tn(hidden, grads)
    in_o[:, :D] = tn(g_gate, rows)
    in_o[:, D:] = tn(g_up, rows)
    return hidden, grad_rows


def expert_both_kernel(arrived, w_in, w_out, in_o, outw_o, back_o):
    rows = unpack(arrived[:, :PACK])
    grads = unpack(arrived[:, PACK:])
    gate = nt(rows, w_in[:, :D])
    up = nt(rows, w_in[:, D:])
    hidden, grad_rows = expert_grads(rows, grads, gate, up, w_in, w_out, in_o, outw_o)
    back_o[:, :PACK] = pack(grad_rows.astype(BF16))
    back_o[:, PACK:] = pack(nn(hidden, w_out[...]).astype(BF16))


def expert_backward_kernel(arrived, rows, gate, up, w_in, w_out, in_o, outw_o, back_o):
    grads = unpack(arrived[...])
    _, grad_rows = expert_grads(rows[...], grads, gate[...], up[...], w_in, w_out, in_o, outw_o)
    back_o[...] = pack(grad_rows.astype(BF16))


def combine_kernel(returned, take, mid, gates, picked_o, low_o):
    picked = nn(take[...], unpack(returned[...]))
    picked_o[...] = picked
    out = mid[...] + gates[:, 0:1] * picked[:TOK] + gates[:, 1:2] * picked[TOK:]
    low_o[...] = out.astype(BF16)


def gate_back(s0, s1, gates, routes, small, returned, take, normed, mid, gains, up, gmid_o, branch_o, sums_o):
    g0, g1 = gates[:, 0:1], gates[:, 1:2]
    mean = g0 * s0 + g1 * s1
    lane = lax.broadcasted_iota(jnp.int32, (TOK, 128), 1)
    grad_logits = (
        jnp.where(lane == routes[:, 0:1], g0 * (s0 - mean), 0.0)
        + jnp.where(lane == routes[:, 1:2], g1 * (s1 - mean), 0.0)
    ).astype(BF16)
    both = (take[:TOK, :].astype(F32) + take[TOK:, :].astype(F32)).astype(BF16)
    grad_ffn = nt(grad_logits, small[...]) + nn(both, unpack(returned[:, :PACK]))
    dx, dgain = norm_back(mid[...], gains[1:2], grad_ffn)
    grad_mid = up[...].astype(F32) + dx
    gmid_o[...] = grad_mid
    branch_o[...] = grad_mid.astype(BF16)
    router = tn(grad_logits, normed[...])[:E]
    row = lax.broadcasted_iota(jnp.int32, (8, D), 0)
    sums_o[...] = jnp.concatenate([router, jnp.where(row == 1, dgain, 0.0)], 0)


def token_back_kernel(returned, take, gates, routes, small, normed, mid, gains, up, picked, gmid_o, branch_o, sums_o):
    u = up[...].astype(F32)
    s0 = jnp.sum(u * picked[:TOK, :], -1, keepdims=True)
    s1 = jnp.sum(u * picked[TOK:, :], -1, keepdims=True)
    gate_back(s0, s1, gates, routes, small, returned, take, normed, mid, gains, up, gmid_o, branch_o, sums_o)


def token_both_kernel(returned, take, gates, routes, small, normed, mid, gains, up, gmid_o, branch_o, sums_o, out_o):
    picked = nn(take[...], unpack(returned[:, PACK:]))
    out_o[...] = mid[...] + gates[:, 0:1] * picked[:TOK] + gates[:, 1:2] * picked[TOK:]
    token_back_kernel(returned, take, gates, routes, small, normed, mid, gains, up, picked, gmid_o, branch_o, sums_o)


def attend_back(own, oth, x_own, x_oth, w, cos, sin, q, k, v, p, gains, sums, part_o, send_o):
    scale = 1.0 / math.sqrt(HEAD)
    branch = jnp.concatenate([own[...], oth[...]], 0)
    grad_mixed = nn(branch, w[:, D:SMALL]).astype(BF16)
    d_q, d_k, d_v = [], [], []
    for g in range(GROUPS):
        k_g = k[:, HEAD * g : HEAD * g + HEAD]
        v_g = v[:, HEAD * g : HEAD * g + HEAD]
        dk = dv = 0.0
        for h in (2 * g, 2 * g + 1):
            q_h = q[:, HEAD * h : HEAD * h + HEAD]
            gm = grad_mixed[:, HEAD * h : HEAD * h + HEAD]
            ph = p[128 * h : 128 * h + 128, :]
            dp = nt(gm, v_g)
            ds = (ph * (dp - jnp.sum(ph * dp, -1, keepdims=True))).astype(BF16)
            d_q.append(nn(ds, k_g) * scale)
            dk = dk + tn(ds, q_h)
            dv = dv + tn(ph.astype(BF16), gm)
        d_k.append(dk * scale)
        d_v.append(dv)
    d_q = jnp.concatenate(d_q, 1)
    d_k = jnp.concatenate(d_k, 1)
    d_v = jnp.concatenate(d_v, 1)
    cos = jnp.concatenate([cos[...]] * GROUPS, 1)
    sin = jnp.concatenate([sin[...]] * GROUPS, 1)
    d_q = d_q * cos - half_swap(d_q) * sin
    d_k = d_k * cos[:, :KW] - half_swap(d_k) * sin[:, :KW]
    grad_proj = jnp.concatenate([d_q, d_k, d_v], 1).astype(BF16)
    grad_normed = nt(grad_proj, w[:, :D])
    part_o[...] = grad_normed[:TOK]
    send_o[...] = grad_normed[TOK:]
    x = jnp.concatenate([x_own[...].astype(F32), x_oth[...].astype(F32)], 0)
    dgain = jnp.sum(grad_normed * (x * inverse_rms(x)), 0, keepdims=True)
    row = lax.broadcasted_iota(jnp.int32, (E + 8, D), 0)
    return branch, grad_proj, jnp.where(row == E, dgain, sums[...])


def attend_back_share_kernel(own, oth, x_own, x_oth, w, cos, sin, q, k, v, p, gains, sums, normed, mixed, acts_o, part_o, send_o, sums_o):
    branch, grad_proj, sums_o[...] = attend_back(
        own, oth, x_own, x_oth, w, cos, sin, q, k, v, p, gains, sums, part_o, send_o
    )
    acts_o[:, :D] = normed[...]
    acts_o[:, D : 2 * D] = branch
    acts_o[:, 2 * D : 3 * D] = grad_proj
    acts_o[:, 3 * D :] = mixed[...]


def attend_back_sum_kernel(own, oth, x_own, x_oth, w, cos, sin, q, k, v, p, gains, sums, normed, mixed, other, y, acts, grad_o, part_o, send_o):
    for n in range(3):
        chunk = 3 * y[0] + n
        rows = acts[:, pl.ds(pl.multiple_of(jnp.where(chunk < 8, 0, D), D), D)]
        cols = acts[:, pl.ds(pl.multiple_of(2 * D + 128 * chunk, 128), 128)]
        grad_o[:, WIDE + 128 * n : WIDE + 128 * n + 128] = tn(rows, cols).astype(BF16)
    branch, grad_proj, full = attend_back(
        own, oth, x_own, x_oth, w, cos, sin, q, k, v, p, gains, sums, part_o, send_o
    )
    grad_o[:, :D] = tn(normed[...], grad_proj).astype(BF16)
    grad_o[:, D:SMALL] = tn(branch, mixed[...]).astype(BF16)
    pad = jnp.zeros((64 - E - 8, D), F32)
    grad_o[:, SMALL:WIDE] = jnp.concatenate([full, pad, other[...], pad], 0).T.astype(BF16)


def input_back_kernel(part, recv, x, gains, gmid, out_o):
    dx, _ = norm_back(x[...].astype(F32), gains[0:1], part[...] + recv[...])
    out_o[...] = gmid[...] + dx


def input_back_send_kernel(part, recv, x, gains, gmid, gates, place, up_o, out_o):
    dx, _ = norm_back(x[...].astype(F32), gains[0:1], part[...] + recv[...])
    up = (gmid[...] + dx).astype(BF16)
    up_o[...] = up
    up = up.astype(F32)
    rows = jnp.concatenate([gates[:, 0:1] * up, gates[:, 1:2] * up], 0).astype(BF16)
    out_o[...] = pack(nn(place[...], rows).astype(BF16))


def halves_kernel(core, qkv, out_proj, router, gains, keep_o, send_o):
    rest = jnp.concatenate(
        [router[...], gains[...], jnp.zeros((16, 128 - E - 2), BF16)], 1
    ).astype(F32)
    for c in range(2):
        left = jnp.concatenate(
            [
                qkv[:, QW * c : QW * c + QW],
                qkv[:, D + KW * c : D + KW * c + KW],
                qkv[:, D + 2 * KW + KW * c : D + 2 * KW + KW * c + KW],
                out_proj[:, QW * c : QW * c + QW],
            ],
            1,
        )

        def fill(ref):
            ref[:, :SMALL] = left
            ref[:, SMALL:] = rest.astype(BF16)

        pl.when(core[0] == c)(lambda: fill(keep_o))
        pl.when(core[0] != c)(lambda: fill(send_o))


def copies_kernel(core, keep, got, all_o, own_o):
    def fill(first, second):
        own_o[...] = second[...]
        block = first[...]
        for i in range(DEV):
            all_o[16 * i : 16 * i + 16, :] = block

    pl.when(core[0] == 0)(lambda: fill(keep, got))
    pl.when(core[0] != 0)(lambda: fill(got, keep))


def total_kernel(core, blocks, keep_o, send_o):
    total = jnp.zeros((16, WIDE), F32)
    parts = [jnp.zeros((16, SHARE), F32) for _ in range(4)]
    for i in range(DEV):
        block = blocks[16 * i : 16 * i + 16, :].astype(F32)
        total = total + block[:, :WIDE]
        parts[i % 4] = parts[i % 4] + block[:, WIDE:]
    total1 = jnp.concatenate(parts, 1)

    def fill(first, second):
        first[...] = total
        second[:, :SMALL] = total1
        second[:, SMALL:] = pltpu.roll(total[:, SMALL:], 64, 1)

    pl.when(core[0] == 0)(lambda: fill(keep_o, send_o))
    pl.when(core[0] != 0)(lambda: fill(send_o, keep_o))


def ends_kernel(core, grad, result, got, out_o):
    def fill(c, mine):
        out_o[c] = mine[...]
        out_o[1 - c] = got[...]

    pl.when(core[0] == 0)(lambda: fill(0, grad))
    pl.when(core[0] != 0)(lambda: fill(1, result))


def owners_kernel(core, keep, got, qkv_o, out_o, router_o, gains_o):
    rest = keep[:, SMALL:] + got[:, SMALL:]
    router_o[...] = rest[:, :E]
    gains_o[...] = rest[:, E : E + 2]

    def fill(c, part):
        qkv_o[:, QW * c : QW * c + QW] = part[:, :QW]
        qkv_o[:, D + KW * c : D + KW * c + KW] = part[:, QW : QW + KW]
        qkv_o[:, D + 2 * KW + KW * c : D + 2 * KW + KW * c + KW] = part[:, QW + KW : D]
        out_o[:, QW * c : QW * c + QW] = part[:, D:SMALL]

    def both(lower, upper):
        fill(0, lower)
        fill(1, upper)

    pl.when(core[0] == 0)(lambda: both(keep, got))
    pl.when(core[0] != 0)(lambda: both(got, keep))


def whole(shape):
    return pl.BlockSpec(shape, lambda i: (0,) * len(shape))


SMALL_SPEC = pl.BlockSpec((D, 128), lambda i: (0, SMALL // 128))


def call(kernel, outs, *args, small=(), scalar=(), near=(), near_out=(), grant=24, flops=10**9):
    args = [
        arg if n in near or n in scalar else pltpu.with_memory_space_constraint(arg, pltpu.HBM)
        for n, arg in enumerate(args)
    ]
    in_specs = []
    for n, arg in enumerate(args):
        if n in scalar:
            in_specs.append(pl.BlockSpec(memory_space=pltpu.SMEM))
        else:
            in_specs.append(SMALL_SPEC if n in small else whole(arg.shape))
    return pl.pallas_call(
        kernel,
        grid=(1,),
        out_shape=[
            jax.ShapeDtypeStruct(shape, kind) if n in near_out else pltpu.HBM(shape, kind)
            for n, (shape, kind) in enumerate(outs)
        ],
        in_specs=in_specs,
        out_specs=[whole(shape) for shape, _ in outs],
        compiler_params=pltpu.CompilerParams(vmem_limit_bytes=grant * 2**20),
        cost_estimate=pl.CostEstimate(flops=flops, bytes_accessed=4 * 2**20, transcendentals=0),
    )(*args)


def exchange(rows):
    blocks = rows.reshape(DEV, rows.shape[0] // DEV, rows.shape[1])
    return lax.all_to_all(blocks, "fsdp", split_axis=0, concat_axis=0, tiled=True).reshape(rows.shape)


def along(span):
    first = [i for i in range(DEV) if i // span % 4 == 0]
    return [[i + span * k for k in range(4)] for i in first]


def twin(v):
    return lax.ppermute(v, "section", [(0, 1), (1, 0)])


def rope_tables(segs):
    flat = segs.reshape(-1)
    tok = jnp.arange(2 * TOK, dtype=jnp.int32)
    same = (flat[:, None] == flat[None, :]) & (tok[:, None] // TOK == tok[None, :] // TOK)
    bias = jnp.where(same & (tok[None, :] <= tok[:, None]), 0.0, NEGATIVE).astype(F32)
    position = jnp.sum(jnp.where(same & (tok[None, :] < tok[:, None]), 1, 0), 1).astype(F32)
    frequency = jnp.exp(jnp.arange(HEAD // 2, dtype=F32) * (-2.0 * math.log(ROPE_BASE) / HEAD))
    angles = position[:, None] * frequency[None, :]
    cos, sin = jnp.cos(angles), jnp.sin(angles)
    cos = jnp.concatenate([cos] * 4, 1)
    sin = jnp.concatenate([-sin, sin] * 2, 1)
    return cos, sin, bias


def placements(routes):
    flat = routes.T.reshape(-1)
    order = jnp.arange(2 * TOK, dtype=jnp.int32)
    earlier = (flat[:, None] == flat[None, :]) & (order[None, :] < order[:, None])
    rank = jnp.sum(jnp.where(earlier, 1, 0), 1)
    first = flat * (2 * SLOT) + rank
    row = jnp.arange(ROWS, dtype=jnp.int32)
    take = (row[None, :] == first[:, None]) | (row[None, :] == first[:, None] + SLOT)
    place = (row[:, None] == first[None, :]) | (row[:, None] == first[None, :] + SLOT)
    return take.astype(BF16), place.astype(BF16)


def shards(ends_in, routes, segments, norm_gains, w_qkv, w_attn_out, w_router, w_in, w_out):
    core = lax.axis_index("section")
    is_first = core == 0

    def layers(mine, theirs):
        return jnp.where(is_first, mine, theirs), jnp.where(is_first, theirs, mine)

    def own_oth(pair):
        return jnp.where(is_first, pair[0], pair[1]), jnp.where(is_first, pair[1], pair[0])

    here = core.astype(jnp.int32).reshape(1)
    kept, sent = call(
        halves_kernel, [((16, WIDE), BF16)] * 2,
        here, w_qkv[0], w_attn_out[0], w_router[0], norm_gains[0], scalar=(0,), near=(1, 2, 3, 4), near_out=(0, 1), grant=8,
    )
    copies, shard1 = call(
        copies_kernel, [((D, WIDE), BF16), ((16, WIDE), BF16)], here, kept, twin(sent),
        scalar=(0,), near=(1, 2), near_out=(1,), grant=12,
    )
    w0 = exchange(copies)

    inputs, cotangent = layers(ends_in[0], twin(ends_in[0]))
    x0_own, x0_oth = own_oth(inputs)
    up1, _ = own_oth(cotangent)
    routes0, routes1 = layers(routes[0], twin(routes[0]))
    routes0, _ = own_oth(routes0)
    routes1, _ = own_oth(routes1)
    segs = jnp.stack(own_oth(segments[:, 0]))
    cos, sin, bias = rope_tables(segs)
    take0, place0 = placements(routes0)
    take1, place1 = placements(routes1)
    win0, win1 = layers(w_in[0], twin(w_in[0]))
    wout0, wout1 = layers(w_out[0], twin(w_out[0]))

    ones = place0[:1, :1] + take0[:1, :1] + place1[:1, :1] + take1[:1, :1]
    shard1 = jnp.where(cos[:1, :1] + sin[:1, :1] + ones > 9.0, jnp.zeros_like(shard1), shard1)
    w1 = lax.all_gather(shard1, "fsdp", axis=0, tiled=True)

    def attend(own, oth, w, near=()):
        return call(
            attend_kernel,
            [
                ((128, D), BF16),
                ((128, QW), BF16),
                ((128, KW), BF16),
                ((128, KW), BF16),
                ((1024, 128), F32),
                ((128, QW), BF16),
                ((TOK, D), F32),
                ((TOK, D), F32),
                ((8, D), F32),
            ],
            own, oth, w, cos, sin, bias,
            near=near, near_out=(6, 7), grant=24,
        )

    def route(kernel, width, *args):
        return call(
            kernel,
            [((TOK, D), F32), ((TOK, D), BF16), ((TOK, 128), F32), ((ROWS, width), BF16)],
            *args,
            small=(4,), near=(1, 2), near_out=(3,), grant=16,
        )

    weight_grads = [((UNITS, 2 * D), F32), ((UNITS, D), F32)]

    normed0, q0, k0, v0, p0, mix0, branch0, send0, gain0 = attend(x0_own, x0_oth, w0, near=(2,))
    mid0, ffn0, gate0, out0 = route(
        route_kernel, PACK, x0_own, branch0, twin(send0), gain0, w0, routes0, place0
    )
    rows0, pre0, upp0, back0 = call(
        expert_forward_kernel,
        [((ROWS, D), BF16), ((ROWS, UNITS), F32), ((ROWS, UNITS), F32), ((ROWS, PACK), BF16)],
        exchange(out0), win0, wout0,
        near=(0,), near_out=(3,),
    )
    picked0, x1_own = call(
        combine_kernel,
        [((128, D), F32), ((TOK, D), BF16)],
        exchange(back0), take0, mid0, gate0,
        near=(0,), grant=16,
    )
    x1_oth = twin(x1_own)

    normed1, q1, k1, v1, p1, mix1, branch1, send1, gain1 = attend(x1_own, x1_oth, w1)
    mid1, ffn1, gate1, out1 = route(
        route_both_kernel, 2 * PACK, x1_own, branch1, twin(send1), gain1, w1, routes1, place1, up1
    )
    gin1, gout1, back1 = call(
        expert_both_kernel,
        weight_grads + [((ROWS, 2 * PACK), BF16)],
        exchange(out1), win1, wout1,
        near=(0,), near_out=(2,),
    )
    back1 = exchange(back1)
    gin1_got, gout1_got = twin(gin1), twin(gout1)
    back1, gin1_got, gout1_got = lax.optimization_barrier((back1, gin1_got, gout1_got))

    token_outs = [((TOK, D), F32), ((TOK, D), BF16), ((E + 8, D), F32)]

    gmid1, gb1, sums1, result1 = call(
        token_both_kernel, token_outs + [((TOK, D), F32)],
        back1, take1, gate1, routes1, w1, ffn1, mid1, gain1, up1,
        small=(4,), near=(0,), near_out=(1,),
    )
    acts1, part1, psend1, sums1 = call(
        attend_back_share_kernel,
        [((128, 7 * D // 2), BF16), ((TOK, D), F32), ((TOK, D), F32), ((E + 8, D), F32)],
        gb1, twin(gb1), x1_own, x1_oth, w1, cos, sin, q1, k1, v1, p1, gain1, sums1, normed1, mix1,
        near=(0, 1), near_out=(1, 2), grant=28,
    )
    acts1 = lax.all_gather(acts1, "fsdp", axis=0, tiled=True, axis_index_groups=along(1))
    up0, gout_rows0 = call(
        input_back_send_kernel,
        [((TOK, D), BF16), ((ROWS, PACK), BF16)],
        part1, twin(psend1), x1_own, gain1, gmid1, gate0, place0,
        near=(0, 1), near_out=(1,), grant=16,
    )

    gin0, gout0, gback0 = call(
        expert_backward_kernel,
        weight_grads + [((ROWS, PACK), BF16)],
        exchange(gout_rows0), rows0, pre0, upp0, win0, wout0,
        near=(0,), near_out=(2,),
    )
    gback0 = exchange(gback0)
    gin0_got, gout0_got = twin(gin0), twin(gout0)
    grad_in = jnp.where(is_first, gin0 + gin0_got, gin1 + gin1_got)
    grad_out = jnp.where(is_first, gout0 + gout0_got, gout1 + gout1_got)
    gback0, grad_in, grad_out = lax.optimization_barrier((gback0, grad_in, grad_out))
    gmid0, gb0, sums0 = call(
        token_back_kernel, token_outs,
        gback0, take0, gate0, routes0, w0, ffn0, mid0, gain0, up0, picked0,
        small=(4,), near=(0,), near_out=(1,),
    )
    grads, part0, psend0 = call(
        attend_back_sum_kernel,
        [((D, WIDE + SHARE), BF16), ((TOK, D), F32), ((TOK, D), F32)],
        gb0, twin(gb0), x0_own, x0_oth, w0, cos, sin, q0, k0, v0, p0, gain0, sums0, normed0, mix0, sums1,
        (lax.axis_index("fsdp") % 4).astype(jnp.int32).reshape(1), acts1,
        scalar=(16,), near=(0, 1), near_out=(1, 2), grant=36,
    )
    (grad_in0,) = call(
        input_back_kernel, [((TOK, D), F32)], part0, twin(psend0), x0_own, gain0, gmid0,
        near=(0, 1), near_out=(0,), grant=16,
    )

    blocks0 = exchange(grads)
    send = jnp.where(is_first, result1, grad_in0)
    (ends_out,) = call(
        ends_kernel, [((2, TOK, D), F32)], here, grad_in0, result1, twin(send),
        scalar=(0,), near=(1, 2, 3), near_out=(0,), grant=8,
    )
    blocks0, ends_out = lax.optimization_barrier((blocks0, ends_out))
    keep, send = call(total_kernel, [((16, WIDE), F32)] * 2, here, blocks0, scalar=(0,), near=(1,), near_out=(0, 1), grant=16)
    grad_qkv, grad_attn_out, grad_router, grad_gains = call(
        owners_kernel,
        [((16, 2 * D), F32), ((16, D), F32), ((16, E), F32), ((16, 2), F32)],
        here, keep, twin(send), scalar=(0,), near=(1, 2), near_out=(0, 1, 2, 3), grant=8,
    )
    return (
        ends_out[None],
        grad_gains[None],
        grad_qkv[None],
        grad_attn_out[None],
        grad_router[None],
        grad_in[None],
        grad_out[None],
    )


def solution(mesh):
    tokens = P("section", None, "fsdp", None)
    weights = P("section", "fsdp", None)
    return jax.shard_map(
        shards,
        mesh=mesh,
        in_specs=(tokens, tokens, P(None, "fsdp", None)) + (weights,) * 6,
        out_specs=(tokens,) + (weights,) * 6,
        check_vma=False,
    )
```

```python
import math

import jax
import jax.numpy as jnp
from jax import lax
from jax.experimental import pallas as pl
from jax.experimental.pallas import tpu as pltpu
from jax.sharding import PartitionSpec as P

D = 1024
HEADS = 16
KV_HEADS = 8
HEAD = 64
E = 32
CAP = 6
TOK = 64
DEV = 64
SLOT = 8
ROWS = DEV * SLOT
PACK = 768
TAIL = D - PACK
WIDE = 1664
SMALL = 1536
SHARE = 384
BOTH = 3584
QW = 512
KW = 256
GROUPS = 4
UNITS = 256
EPSILON = 1e-06
ROPE_BASE = 10000.0
NEGATIVE = -1e30
F32 = jnp.float32
BF16 = jnp.bfloat16


def nn(a, b):
    return lax.dot_general(a, b, (((1,), (0,)), ((), ())), preferred_element_type=F32)


def nt(a, b):
    return lax.dot_general(a, b, (((1,), (1,)), ((), ())), preferred_element_type=F32)


def tn(a, b):
    return lax.dot_general(a, b, (((0,), (0,)), ((), ())), preferred_element_type=F32)


def row_in_slot(shape):
    return lax.broadcasted_iota(jnp.int32, shape, 0) % SLOT


def tail_moves():
    row = lax.broadcasted_iota(jnp.int32, (128, 384), 0)
    col = lax.broadcasted_iota(jnp.int32, (128, 384), 1)
    piece, col = col // 128, col % 128
    slot, kept = row % SLOT, col % SLOT
    hit = ((kept == CAP) & (slot == piece)) | ((kept == CAP + 1) & (slot == piece + 3))
    return jnp.where(hit & (row // SLOT == col // SLOT), 1.0, 0.0).astype(BF16)


def unpack(packed):
    moves = tail_moves()
    main = jnp.where(row_in_slot((ROWS, PACK)) < CAP, packed.astype(F32), 0.0).astype(BF16)
    tails = []
    for block in range(0, ROWS, 128):
        part = packed[block : block + 128]
        stacked = jnp.concatenate([part[:, 256 * j : 256 * j + 256] for j in range(3)], 0)
        tails.append(nn(moves, stacked).astype(BF16))
    return jnp.concatenate([main, jnp.concatenate(tails, 0)], 1)


def pack(rows):
    moves = tail_moves()
    keep = row_in_slot((128, 256)) < CAP
    blocks = []
    for block in range(0, ROWS, 128):
        part = rows[block : block + 128]
        tail = tn(moves, part[:, PACK:])
        pieces = []
        for j in range(3):
            main = part[:, 256 * j : 256 * j + 256].astype(F32)
            pieces.append(jnp.where(keep, main, tail[128 * j : 128 * j + 128]).astype(BF16))
        blocks.append(jnp.concatenate(pieces, 1))
    return jnp.concatenate(blocks, 0)


def inverse_rms(x):
    return lax.rsqrt(jnp.mean(x * x, -1, keepdims=True) + EPSILON)


def norm_back(x, gain, grad):
    inv = inverse_rms(x)
    unit = x * inv
    scaled = grad * gain
    dx = inv * (scaled - unit * jnp.mean(scaled * unit, -1, keepdims=True))
    return dx, jnp.sum(grad * unit, 0, keepdims=True)


def half_swap(v):
    width = v.shape[1]
    lane = lax.broadcasted_iota(jnp.int32, v.shape, 1) % HEAD
    return jnp.where(
        lane < HEAD // 2,
        pltpu.roll(v, width - HEAD // 2, 1),
        pltpu.roll(v, HEAD // 2, 1),
    )


def at_lane(shape, lane, value, base):
    return jnp.where(lax.broadcasted_iota(jnp.int32, shape, 1) == lane, value, base)


def attend_kernel(own, oth, w, cos, sin, bias, acts_o, q_o, k_o, v_o, p_o, branch_o, send_o, gain_o):
    x = jnp.concatenate([own[...].astype(F32), oth[...].astype(F32)], 0)
    small = w[:, SMALL:].astype(F32).T
    gains = small[E : E + 8]
    gain_o[...] = gains
    normed = (x * inverse_rms(x) * gains[0:1]).astype(BF16)
    acts_o[:, :D] = normed
    proj = nn(normed, w[:, :D])
    q = proj[:, :QW]
    k = proj[:, QW : QW + KW]
    v = proj[:, QW + KW :].astype(BF16)
    cos = jnp.concatenate([cos[...]] * GROUPS, 1)
    sin = jnp.concatenate([sin[...]] * GROUPS, 1)
    q = (q * cos + half_swap(q) * sin).astype(BF16)
    k = (k * cos[:, :KW] + half_swap(k) * sin[:, :KW]).astype(BF16)
    q_o[...] = q
    k_o[...] = k
    v_o[...] = v
    mask = bias[...]
    mixed = []
    for h in range(2 * GROUPS):
        g = h // 2
        q_h = q[:, HEAD * h : HEAD * h + HEAD]
        k_g = k[:, HEAD * g : HEAD * g + HEAD]
        v_g = v[:, HEAD * g : HEAD * g + HEAD]
        s = nt(q_h, k_g) * (1.0 / math.sqrt(HEAD)) + mask
        top = jnp.max(s, -1, keepdims=True)
        ex = jnp.exp(s - top)
        p = ex / jnp.sum(ex, -1, keepdims=True)
        p_o[128 * h : 128 * h + 128, :] = p
        mixed.append(nn(p.astype(BF16), v_g))
    mixed = jnp.concatenate(mixed, 1).astype(BF16)
    acts_o[:, D:] = mixed
    branch = nt(mixed, w[:, D:SMALL])
    branch_o[...] = branch[:TOK]
    send_o[...] = branch[TOK:]


def route_rows(x, branch, recv, gains, small, routes, place, mid_o, normed_o, gate_o, out_o):
    mid = x[...].astype(F32) + branch[...] + recv[...]
    mid_o[...] = mid
    normed = (mid * inverse_rms(mid) * gains[1:2]).astype(BF16)
    normed_o[...] = normed
    logits = nn(normed, small[...])
    lane = lax.broadcasted_iota(jnp.int32, (TOK, 128), 1)
    l0 = jnp.sum(jnp.where(lane == routes[:, 0:1], logits, 0.0), -1, keepdims=True)
    l1 = jnp.sum(jnp.where(lane == routes[:, 1:2], logits, 0.0), -1, keepdims=True)
    top = jnp.maximum(l0, l1)
    e0, e1 = jnp.exp(l0 - top), jnp.exp(l1 - top)
    total = e0 + e1
    gate_o[...] = at_lane((TOK, 128), 0, e0 / total, at_lane((TOK, 128), 1, e1 / total, 0.0))
    rows = nn(place[...], jnp.concatenate([normed, normed], 0)).astype(BF16)
    out_o[:, :PACK] = pack(rows)
    return e0 / total, e1 / total


def route_kernel(*refs):
    route_rows(*refs)


def route_both_kernel(x, branch, recv, gains, small, routes, place, up, mid_o, normed_o, gate_o, out_o):
    g0, g1 = route_rows(x, branch, recv, gains, small, routes, place, mid_o, normed_o, gate_o, out_o)
    u = up[...]
    rows = jnp.concatenate([g0 * u, g1 * u], 0).astype(BF16)
    out_o[:, PACK:] = pack(nn(place[...], rows).astype(BF16))


def expert_forward_kernel(arrived, w_in, w_out, rows_o, gate_o, up_o, out_o):
    rows = unpack(arrived[...])
    rows_o[...] = rows
    gate = nt(rows, w_in[:, :D])
    up = nt(rows, w_in[:, D:])
    gate_o[...] = gate
    up_o[...] = up
    hidden = (gate * (1.0 / (1.0 + jnp.exp(-gate))) * up).astype(BF16)
    out_o[...] = pack(nn(hidden, w_out[...]).astype(BF16))


def expert_grads(rows, grads, gate, up, w_in, w_out, in_o, outw_o):
    sig = 1.0 / (1.0 + jnp.exp(-gate))
    act = gate * sig
    hidden = (act * up).astype(BF16)
    grad_hidden = nt(grads, w_out[...])
    g_gate = (grad_hidden * up * sig * (1.0 + gate * (1.0 - sig))).astype(BF16)
    g_up = (grad_hidden * act).astype(BF16)
    grad_rows = nn(g_gate, w_in[:, :D]) + nn(g_up, w_in[:, D:])
    outw_o[...] = tn(hidden, grads)
    in_o[:, :D] = tn(g_gate, rows)
    in_o[:, D:] = tn(g_up, rows)
    return hidden, grad_rows


def expert_both_kernel(arrived, w_in, w_out, in_o, outw_o, back_o):
    rows = unpack(arrived[:, :PACK])
    grads = unpack(arrived[:, PACK:])
    gate = nt(rows, w_in[:, :D])
    up = nt(rows, w_in[:, D:])
    hidden, grad_rows = expert_grads(rows, grads, gate, up, w_in, w_out, in_o, outw_o)
    back_o[:, :PACK] = pack(grad_rows.astype(BF16))
    back_o[:, PACK:] = pack(nn(hidden, w_out[...]).astype(BF16))


def expert_backward_kernel(arrived, rows, gate, up, w_in, w_out, in_o, outw_o, back_o):
    grads = unpack(arrived[...])
    _, grad_rows = expert_grads(rows[...], grads, gate[...], up[...], w_in, w_out, in_o, outw_o)
    back_o[...] = pack(grad_rows.astype(BF16))


def combine_kernel(returned, take, mid, gates, picked_o, low_o):
    picked = nn(take[...], unpack(returned[...]))
    picked_o[...] = picked
    out = mid[...] + gates[:, 0:1] * picked[:TOK] + gates[:, 1:2] * picked[TOK:]
    low_o[...] = out.astype(BF16)


def gate_back(s0, s1, gates, routes, small, returned, take, normed, mid, gains, up, gmid_o, branch_o, sums_o):
    g0, g1 = gates[:, 0:1], gates[:, 1:2]
    mean = g0 * s0 + g1 * s1
    lane = lax.broadcasted_iota(jnp.int32, (TOK, 128), 1)
    grad_logits = (
        jnp.where(lane == routes[:, 0:1], g0 * (s0 - mean), 0.0)
        + jnp.where(lane == routes[:, 1:2], g1 * (s1 - mean), 0.0)
    ).astype(BF16)
    both = (take[:TOK, :].astype(F32) + take[TOK:, :].astype(F32)).astype(BF16)
    grad_ffn = nt(grad_logits, small[...]) + nn(both, unpack(returned[:, :PACK]))
    dx, dgain = norm_back(mid[...], gains[1:2], grad_ffn)
    grad_mid = up[...].astype(F32) + dx
    gmid_o[...] = grad_mid
    branch_o[...] = grad_mid.astype(BF16)
    router = tn(grad_logits, normed[...])[:E]
    row = lax.broadcasted_iota(jnp.int32, (8, D), 0)
    sums_o[...] = jnp.concatenate([router, jnp.where(row == 1, dgain, 0.0)], 0)


def token_back_kernel(returned, take, gates, routes, small, normed, mid, gains, up, picked, gmid_o, branch_o, sums_o):
    u = up[...].astype(F32)
    s0 = jnp.sum(u * picked[:TOK, :], -1, keepdims=True)
    s1 = jnp.sum(u * picked[TOK:, :], -1, keepdims=True)
    gate_back(s0, s1, gates, routes, small, returned, take, normed, mid, gains, up, gmid_o, branch_o, sums_o)


def token_both_kernel(returned, take, gates, routes, small, normed, mid, gains, up, gmid_o, branch_o, sums_o, out_o):
    picked = nn(take[...], unpack(returned[:, PACK:]))
    out_o[...] = mid[...] + gates[:, 0:1] * picked[:TOK] + gates[:, 1:2] * picked[TOK:]
    token_back_kernel(returned, take, gates, routes, small, normed, mid, gains, up, picked, gmid_o, branch_o, sums_o)


def attend_back(own, oth, x_own, x_oth, w, cos, sin, q, k, v, p, gains, sums, part_o, send_o):
    scale = 1.0 / math.sqrt(HEAD)
    branch = jnp.concatenate([own[...], oth[...]], 0)
    grad_mixed = nn(branch, w[:, D:SMALL]).astype(BF16)
    d_q, d_k, d_v = [], [], []
    for g in range(GROUPS):
        k_g = k[:, HEAD * g : HEAD * g + HEAD]
        v_g = v[:, HEAD * g : HEAD * g + HEAD]
        dk = dv = 0.0
        for h in (2 * g, 2 * g + 1):
            q_h = q[:, HEAD * h : HEAD * h + HEAD]
            gm = grad_mixed[:, HEAD * h : HEAD * h + HEAD]
            ph = p[128 * h : 128 * h + 128, :]
            dp = nt(gm, v_g)
            ds = (ph * (dp - jnp.sum(ph * dp, -1, keepdims=True))).astype(BF16)
            d_q.append(nn(ds, k_g) * scale)
            dk = dk + tn(ds, q_h)
            dv = dv + tn(ph.astype(BF16), gm)
        d_k.append(dk * scale)
        d_v.append(dv)
    d_q = jnp.concatenate(d_q, 1)
    d_k = jnp.concatenate(d_k, 1)
    d_v = jnp.concatenate(d_v, 1)
    cos = jnp.concatenate([cos[...]] * GROUPS, 1)
    sin = jnp.concatenate([sin[...]] * GROUPS, 1)
    d_q = d_q * cos - half_swap(d_q) * sin
    d_k = d_k * cos[:, :KW] - half_swap(d_k) * sin[:, :KW]
    grad_proj = jnp.concatenate([d_q, d_k, d_v], 1).astype(BF16)
    grad_normed = nt(grad_proj, w[:, :D])
    part_o[...] = grad_normed[:TOK]
    send_o[...] = grad_normed[TOK:]
    x = jnp.concatenate([x_own[...].astype(F32), x_oth[...].astype(F32)], 0)
    dgain = jnp.sum(grad_normed * (x * inverse_rms(x)), 0, keepdims=True)
    row = lax.broadcasted_iota(jnp.int32, (E + 8, D), 0)
    return branch, grad_proj, jnp.where(row == E, dgain, sums[...])


def attend_back_share_kernel(own, oth, x_own, x_oth, w, cos, sin, q, k, v, p, gains, sums, acts, first, acts_o, part_o, send_o, sums_o):
    branch, grad_proj, sums_o[...] = attend_back(
        own, oth, x_own, x_oth, w, cos, sin, q, k, v, p, gains, sums, part_o, send_o
    )
    acts_o[:, :D] = acts[:, :D]
    acts_o[:, D : 2 * D] = branch
    acts_o[:, 2 * D : 3 * D] = grad_proj
    acts_o[:, 3 * D : BOTH] = acts[:, D:]
    acts_o[:, BOTH:] = first[...]


def attend_back_send_kernel(own, oth, x_own, x_oth, w, cos, sin, q, k, v, p, gains, sums, moves, out_o, part_o, send_o, sums_o):
    branch, grad_proj, sums_o[...] = attend_back(
        own, oth, x_own, x_oth, w, cos, sin, q, k, v, p, gains, sums, part_o, send_o
    )
    branch = nn(branch, moves[...]).astype(BF16)
    for y in range(4):
        out_o[128 * y : 128 * y + 128, :256] = grad_proj[:, 256 * y : 256 * y + 256]
        out_o[128 * y : 128 * y + 128, 256:] = branch[:, 256 * y : 256 * y + 256]


def share_after_kernel(y, acts, sums0, sums1, grad_o):
    for n in range(3):
        chunk = 3 * y[0] + n
        rows = acts[:, pl.ds(pl.multiple_of(jnp.where(chunk < 8, 0, D), D), D)]
        cols = acts[:, pl.ds(pl.multiple_of(2 * D + 128 * chunk, 128), 128)]
        grad_o[:, 128 * n : 128 * n + 128] = tn(rows, cols).astype(BF16)
    pad = jnp.zeros((64 - E - 8, D), F32)
    grad_o[:, SHARE:] = jnp.concatenate([sums0[...], pad, sums1[...], pad], 0).T.astype(BF16)


def share_first_kernel(got, acts, moves, after, grad_o):
    grad_o[:, :KW] = tn(acts[:, BOTH : BOTH + D], got[:, :256]).astype(BF16)
    out = tn(got[:, 256:], acts[:, BOTH + D :]).astype(BF16)
    stacked = jnp.concatenate([out[:, 128 * c : 128 * c + 128] for c in range(4)], 0)
    grad_o[:, KW:SHARE] = nn(moves[...], stacked).astype(BF16)
    grad_o[:, SHARE:] = after[...]


def input_back_kernel(part, recv, x, gains, gmid, out_o):
    dx, _ = norm_back(x[...].astype(F32), gains[0:1], part[...] + recv[...])
    out_o[...] = gmid[...] + dx


def input_back_send_kernel(part, recv, x, gains, gmid, gates, place, up_o, out_o):
    dx, _ = norm_back(x[...].astype(F32), gains[0:1], part[...] + recv[...])
    up = (gmid[...] + dx).astype(BF16)
    up_o[...] = up
    up = up.astype(F32)
    rows = jnp.concatenate([gates[:, 0:1] * up, gates[:, 1:2] * up], 0).astype(BF16)
    out_o[...] = pack(nn(place[...], rows).astype(BF16))


def halves_kernel(core, qkv, out_proj, router, gains, keep_o, send_o):
    rest = jnp.concatenate(
        [router[...], gains[...], jnp.zeros((16, 128 - E - 2), BF16)], 1
    ).astype(F32)
    for c in range(2):
        left = jnp.concatenate(
            [
                qkv[:, QW * c : QW * c + QW],
                qkv[:, D + KW * c : D + KW * c + KW],
                qkv[:, D + 2 * KW + KW * c : D + 2 * KW + KW * c + KW],
                out_proj[:, QW * c : QW * c + QW],
            ],
            1,
        )

        def fill(ref):
            ref[:, :SMALL] = left
            ref[:, SMALL:] = rest.astype(BF16)

        pl.when(core[0] == c)(lambda: fill(keep_o))
        pl.when(core[0] != c)(lambda: fill(send_o))


def copies_kernel(core, keep, got, all_o, own_o):
    def fill(first, second):
        own_o[...] = second[...]
        block = first[...]
        for i in range(DEV):
            all_o[16 * i : 16 * i + 16, :] = block

    pl.when(core[0] == 0)(lambda: fill(keep, got))
    pl.when(core[0] != 0)(lambda: fill(got, keep))


def total_kernel(core, blocks, keep_o, send_o):
    parts = [jnp.zeros((16, 2 * SHARE), F32) for _ in range(4)]
    rest = jnp.zeros((16, 128), F32)
    for i in range(DEV):
        block = blocks[16 * i : 16 * i + 16, :].astype(F32)
        parts[i % 4] = parts[i % 4] + block[:, : 2 * SHARE]
        rest = rest + block[:, 2 * SHARE :]

    def fill(first, second):
        for y in range(4):
            first[:, KW * y : KW * y + KW] = parts[y][:, :KW]
            for c in range(4):
                first[4 * y : 4 * y + 4, D + 128 * c : D + 128 * c + 128] = parts[y][4 * c : 4 * c + 4, KW:SHARE]
            second[:, SHARE * y : SHARE * y + SHARE] = parts[y][:, SHARE:]
        first[:, SMALL:] = rest
        second[:, SMALL:] = pltpu.roll(rest, 64, 1)

    pl.when(core[0] == 0)(lambda: fill(keep_o, send_o))
    pl.when(core[0] != 0)(lambda: fill(send_o, keep_o))


def ends_kernel(core, grad, result, got, out_o):
    def fill(c, mine):
        out_o[c] = mine[...]
        out_o[1 - c] = got[...]

    pl.when(core[0] == 0)(lambda: fill(0, grad))
    pl.when(core[0] != 0)(lambda: fill(1, result))


def owners_kernel(core, keep, got, qkv_o, out_o, router_o, gains_o):
    rest = keep[:, SMALL:] + got[:, SMALL:]
    router_o[...] = rest[:, :E]
    gains_o[...] = rest[:, E : E + 2]

    def fill(c, part):
        qkv_o[:, QW * c : QW * c + QW] = part[:, :QW]
        qkv_o[:, D + KW * c : D + KW * c + KW] = part[:, QW : QW + KW]
        qkv_o[:, D + 2 * KW + KW * c : D + 2 * KW + KW * c + KW] = part[:, QW + KW : D]
        out_o[:, QW * c : QW * c + QW] = part[:, D:SMALL]

    def both(lower, upper):
        fill(0, lower)
        fill(1, upper)

    pl.when(core[0] == 0)(lambda: both(keep, got))
    pl.when(core[0] != 0)(lambda: both(got, keep))


def whole(shape):
    return pl.BlockSpec(shape, lambda i: (0,) * len(shape))


SMALL_SPEC = pl.BlockSpec((D, 128), lambda i: (0, SMALL // 128))


def call(kernel, outs, *args, small=(), scalar=(), near=(), near_out=(), grant=24, flops=10**9):
    args = [
        arg if n in near or n in scalar else pltpu.with_memory_space_constraint(arg, pltpu.HBM)
        for n, arg in enumerate(args)
    ]
    in_specs = []
    for n, arg in enumerate(args):
        if n in scalar:
            in_specs.append(pl.BlockSpec(memory_space=pltpu.SMEM))
        else:
            in_specs.append(SMALL_SPEC if n in small else whole(arg.shape))
    return pl.pallas_call(
        kernel,
        grid=(1,),
        out_shape=[
            jax.ShapeDtypeStruct(shape, kind) if n in near_out else pltpu.HBM(shape, kind)
            for n, (shape, kind) in enumerate(outs)
        ],
        in_specs=in_specs,
        out_specs=[whole(shape) for shape, _ in outs],
        compiler_params=pltpu.CompilerParams(vmem_limit_bytes=grant * 2**20),
        cost_estimate=pl.CostEstimate(flops=flops, bytes_accessed=4 * 2**20, transcendentals=0),
    )(*args)


def exchange(rows):
    blocks = rows.reshape(DEV, rows.shape[0] // DEV, rows.shape[1])
    return lax.all_to_all(blocks, "fsdp", split_axis=0, concat_axis=0, tiled=True).reshape(rows.shape)


def along(span):
    first = [i for i in range(DEV) if i // span % 4 == 0]
    return [[i + span * k for k in range(4)] for i in first]


def twin(v):
    return lax.ppermute(v, "section", [(0, 1), (1, 0)])


def rope_tables(segs):
    flat = segs.reshape(-1)
    tok = jnp.arange(2 * TOK, dtype=jnp.int32)
    same = (flat[:, None] == flat[None, :]) & (tok[:, None] // TOK == tok[None, :] // TOK)
    bias = jnp.where(same & (tok[None, :] <= tok[:, None]), 0.0, NEGATIVE).astype(F32)
    position = jnp.sum(jnp.where(same & (tok[None, :] < tok[:, None]), 1, 0), 1).astype(F32)
    frequency = jnp.exp(jnp.arange(HEAD // 2, dtype=F32) * (-2.0 * math.log(ROPE_BASE) / HEAD))
    angles = position[:, None] * frequency[None, :]
    cos, sin = jnp.cos(angles), jnp.sin(angles)
    cos = jnp.concatenate([cos] * 4, 1)
    sin = jnp.concatenate([-sin, sin] * 2, 1)
    return cos, sin, bias


def placements(routes):
    flat = routes.T.reshape(-1)
    order = jnp.arange(2 * TOK, dtype=jnp.int32)
    earlier = (flat[:, None] == flat[None, :]) & (order[None, :] < order[:, None])
    rank = jnp.sum(jnp.where(earlier, 1, 0), 1)
    first = flat * (2 * SLOT) + rank
    row = jnp.arange(ROWS, dtype=jnp.int32)
    take = (row[None, :] == first[:, None]) | (row[None, :] == first[:, None] + SLOT)
    place = (row[:, None] == first[None, :]) | (row[:, None] == first[None, :] + SLOT)
    return take.astype(BF16), place.astype(BF16)


def shards(ends_in, routes, segments, norm_gains, w_qkv, w_attn_out, w_router, w_in, w_out):
    core = lax.axis_index("section")
    is_first = core == 0

    def layers(mine, theirs):
        return jnp.where(is_first, mine, theirs), jnp.where(is_first, theirs, mine)

    def own_oth(pair):
        return jnp.where(is_first, pair[0], pair[1]), jnp.where(is_first, pair[1], pair[0])

    here = core.astype(jnp.int32).reshape(1)
    kept, sent = call(
        halves_kernel, [((16, WIDE), BF16)] * 2,
        here, w_qkv[0], w_attn_out[0], w_router[0], norm_gains[0], scalar=(0,), near_out=(0, 1), grant=8,
    )
    copies, shard1 = call(
        copies_kernel, [((D, WIDE), BF16), ((16, WIDE), BF16)], here, kept, twin(sent),
        scalar=(0,), near=(1, 2), near_out=(1,), grant=12,
    )
    w0 = exchange(copies)

    inputs, cotangent = layers(ends_in[0], twin(ends_in[0]))
    x0_own, x0_oth = own_oth(inputs)
    up1, _ = own_oth(cotangent)
    routes0, routes1 = layers(routes[0], twin(routes[0]))
    routes0, _ = own_oth(routes0)
    routes1, _ = own_oth(routes1)
    segs = jnp.stack(own_oth(segments[:, 0]))
    cos, sin, bias = rope_tables(segs)
    take0, place0 = placements(routes0)
    take1, place1 = placements(routes1)
    win0, win1 = layers(w_in[0], twin(w_in[0]))
    wout0, wout1 = layers(w_out[0], twin(w_out[0]))

    d = jnp.arange(D, dtype=jnp.int32)
    moves = ((d // 4 % 4 * 256 + d // 16 * 4 + d % 4)[:, None] == d[None, :]).astype(BF16)
    shard1 = jnp.where(cos[:1, :1] + sin[:1, :1] + moves[:1, :1] > 4.0, jnp.zeros_like(shard1), shard1)
    w1 = lax.all_gather(shard1, "fsdp", axis=0, tiled=True)

    def attend(own, oth, w, near=(), near_out=(6,)):
        return call(
            attend_kernel,
            [
                ((128, SMALL), BF16),
                ((128, QW), BF16),
                ((128, KW), BF16),
                ((128, KW), BF16),
                ((1024, 128), F32),
                ((TOK, D), F32),
                ((TOK, D), F32),
                ((8, D), F32),
            ],
            own, oth, w, cos, sin, bias,
            near=near, near_out=near_out, grant=24,
        )

    def route(kernel, width, *args, near=(1, 2)):
        return call(
            kernel,
            [((TOK, D), F32), ((TOK, D), BF16), ((TOK, 128), F32), ((ROWS, width), BF16)],
            *args,
            small=(4,), near=near, near_out=(3,), grant=16,
        )

    weight_grads = [((UNITS, 2 * D), F32), ((UNITS, D), F32)]

    acts0, q0, k0, v0, p0, branch0, send0, gain0 = attend(x0_own, x0_oth, w0, near=(2,))
    mid0, ffn0, gate0, out0 = route(
        route_kernel, PACK, x0_own, branch0, twin(send0), gain0, w0, routes0, place0, near=(2,)
    )
    rows0, pre0, upp0, back0 = call(
        expert_forward_kernel,
        [((ROWS, D), BF16), ((ROWS, UNITS), F32), ((ROWS, UNITS), F32), ((ROWS, PACK), BF16)],
        exchange(out0), win0, wout0,
        near=(0,), near_out=(3,),
    )
    picked0, x1_own = call(
        combine_kernel,
        [((128, D), F32), ((TOK, D), BF16)],
        exchange(back0), take0, mid0, gate0,
        near=(0,), grant=16,
    )
    x1_oth = twin(x1_own)

    acts1, q1, k1, v1, p1, branch1, send1, gain1 = attend(x1_own, x1_oth, w1, near_out=(5, 6))
    mid1, ffn1, gate1, out1 = route(
        route_both_kernel, 2 * PACK, x1_own, branch1, twin(send1), gain1, w1, routes1, place1, up1
    )
    gin1, gout1, back1 = call(
        expert_both_kernel,
        weight_grads + [((ROWS, 2 * PACK), BF16)],
        exchange(out1), win1, wout1,
        near=(0,), near_out=(2,),
    )
    back1 = exchange(back1)
    gin1_got, gout1_got = twin(gin1), twin(gout1)
    back1, gin1_got, gout1_got = lax.optimization_barrier((back1, gin1_got, gout1_got))

    token_outs = [((TOK, D), F32), ((TOK, D), BF16), ((E + 8, D), F32)]

    gmid1, gb1, sums1, result1 = call(
        token_both_kernel, token_outs + [((TOK, D), F32)],
        back1, take1, gate1, routes1, w1, ffn1, mid1, gain1, up1,
        small=(4,), near=(0,), near_out=(1,),
    )
    acts1, part1, psend1, sums1 = call(
        attend_back_share_kernel,
        [((128, BOTH + SMALL), BF16), ((TOK, D), F32), ((TOK, D), F32), ((E + 8, D), F32)],
        gb1, twin(gb1), x1_own, x1_oth, w1, cos, sin, q1, k1, v1, p1, gain1, sums1, acts1, acts0,
        near=(0, 1), near_out=(1, 2), grant=28,
    )
    acts = lax.all_gather(acts1, "fsdp", axis=0, tiled=True, axis_index_groups=along(1))
    up0, gout_rows0 = call(
        input_back_send_kernel,
        [((TOK, D), BF16), ((ROWS, PACK), BF16)],
        part1, twin(psend1), x1_own, gain1, gmid1, gate0, place0,
        near=(0, 1), near_out=(1,), grant=16,
    )

    gin0, gout0, gback0 = call(
        expert_backward_kernel,
        weight_grads + [((ROWS, PACK), BF16)],
        exchange(gout_rows0), rows0, pre0, upp0, win0, wout0,
        near=(0,), near_out=(2,),
    )
    gback0 = exchange(gback0)
    gin0_got, gout0_got = twin(gin0), twin(gout0)
    grad_in = jnp.where(is_first, gin0 + gin0_got, gin1 + gin1_got)
    grad_out = jnp.where(is_first, gout0 + gout0_got, gout1 + gout1_got)
    gback0, grad_in, grad_out = lax.optimization_barrier((gback0, grad_in, grad_out))
    gmid0, gb0, sums0 = call(
        token_back_kernel, token_outs,
        gback0, take0, gate0, routes0, w0, ffn0, mid0, gain0, up0, picked0,
        small=(4,), near=(0,), near_out=(1,),
    )
    crossing, part0, psend0, sums0 = call(
        attend_back_send_kernel,
        [((512, 512), BF16), ((TOK, D), F32), ((TOK, D), F32), ((E + 8, D), F32)],
        gb0, twin(gb0), x0_own, x0_oth, w0, cos, sin, q0, k0, v0, p0, gain0, sums0, moves,
        near=(0, 1), near_out=(0, 1, 2), grant=28,
    )
    crossing = lax.all_to_all(
        crossing.reshape(4, 128, 512), "fsdp", split_axis=0, concat_axis=0, tiled=True, axis_index_groups=along(1)
    ).reshape(512, 512)
    (after,) = call(
        share_after_kernel, [((D, 512), BF16)],
        (lax.axis_index("fsdp") % 4).astype(jnp.int32).reshape(1), acts, sums0, sums1,
        scalar=(0,), near_out=(0,),
    )
    crossing, after = lax.optimization_barrier((crossing, after))
    (grads,) = call(
        share_first_kernel, [((D, 2 * SHARE + 128), BF16)],
        crossing, acts, moves, after,
        near=(0, 3),
    )
    (grad_in0,) = call(
        input_back_kernel, [((TOK, D), F32)], part0, twin(psend0), x0_own, gain0, gmid0,
        near=(0, 1), near_out=(0,), grant=16,
    )

    blocks0 = exchange(grads)
    send = jnp.where(is_first, result1, grad_in0)
    (ends_out,) = call(
        ends_kernel, [((2, TOK, D), F32)], here, grad_in0, result1, twin(send),
        scalar=(0,), near=(1, 2, 3), near_out=(0,), grant=8,
    )
    blocks0, ends_out = lax.optimization_barrier((blocks0, ends_out))
    keep, send = call(total_kernel, [((16, WIDE), F32)] * 2, here, blocks0, scalar=(0,), near=(1,), near_out=(0, 1), grant=16)
    grad_qkv, grad_attn_out, grad_router, grad_gains = call(
        owners_kernel,
        [((16, 2 * D), F32), ((16, D), F32), ((16, E), F32), ((16, 2), F32)],
        here, keep, twin(send), scalar=(0,), near=(1, 2), near_out=(0, 1, 2, 3), grant=8,
    )
    return (
        ends_out[None],
        grad_gains[None],
        grad_qkv[None],
        grad_attn_out[None],
        grad_router[None],
        grad_in[None],
        grad_out[None],
    )


def solution(mesh):
    tokens = P("section", None, "fsdp", None)
    weights = P("section", "fsdp", None)
    return jax.shard_map(
        shards,
        mesh=mesh,
        in_specs=(tokens, tokens, P(None, "fsdp", None)) + (weights,) * 6,
        out_specs=(tokens,) + (weights,) * 6,
        check_vma=False,
    )
```

```python
import math

import jax
import jax.numpy as jnp
from jax import lax
from jax.experimental import pallas as pl
from jax.experimental.pallas import tpu as pltpu
from jax.sharding import PartitionSpec as P

D = 1024
HEADS = 16
KV_HEADS = 8
HEAD = 64
E = 32
CAP = 6
TOK = 64
DEV = 64
SLOT = 8
ROWS = DEV * SLOT
PACK = 768
TAIL = D - PACK
WIDE = 1664
SMALL = 1536
SHARE = 384
BOTH = 5120
QW = 512
KW = 256
GROUPS = 4
UNITS = 256
EPSILON = 1e-06
ROPE_BASE = 10000.0
NEGATIVE = -1e30
F32 = jnp.float32
BF16 = jnp.bfloat16


def nn(a, b):
    return lax.dot_general(a, b, (((1,), (0,)), ((), ())), preferred_element_type=F32)


def nt(a, b):
    return lax.dot_general(a, b, (((1,), (1,)), ((), ())), preferred_element_type=F32)


def tn(a, b):
    return lax.dot_general(a, b, (((0,), (0,)), ((), ())), preferred_element_type=F32)


def row_in_slot(shape):
    return lax.broadcasted_iota(jnp.int32, shape, 0) % SLOT


def tail_moves():
    row = lax.broadcasted_iota(jnp.int32, (128, 384), 0)
    col = lax.broadcasted_iota(jnp.int32, (128, 384), 1)
    piece, col = col // 128, col % 128
    slot, kept = row % SLOT, col % SLOT
    hit = ((kept == CAP) & (slot == piece)) | ((kept == CAP + 1) & (slot == piece + 3))
    return jnp.where(hit & (row // SLOT == col // SLOT), 1.0, 0.0).astype(BF16)


def unpack(packed):
    moves = tail_moves()
    main = jnp.where(row_in_slot((ROWS, PACK)) < CAP, packed.astype(F32), 0.0).astype(BF16)
    tails = []
    for block in range(0, ROWS, 128):
        part = packed[block : block + 128]
        stacked = jnp.concatenate([part[:, 256 * j : 256 * j + 256] for j in range(3)], 0)
        tails.append(nn(moves, stacked).astype(BF16))
    return jnp.concatenate([main, jnp.concatenate(tails, 0)], 1)


def pack(rows):
    moves = tail_moves()
    keep = row_in_slot((128, 256)) < CAP
    blocks = []
    for block in range(0, ROWS, 128):
        part = rows[block : block + 128]
        tail = tn(moves, part[:, PACK:])
        pieces = []
        for j in range(3):
            main = part[:, 256 * j : 256 * j + 256].astype(F32)
            pieces.append(jnp.where(keep, main, tail[128 * j : 128 * j + 128]).astype(BF16))
        blocks.append(jnp.concatenate(pieces, 1))
    return jnp.concatenate(blocks, 0)


def inverse_rms(x):
    return lax.rsqrt(jnp.mean(x * x, -1, keepdims=True) + EPSILON)


def norm_back(x, gain, grad):
    inv = inverse_rms(x)
    unit = x * inv
    scaled = grad * gain
    dx = inv * (scaled - unit * jnp.mean(scaled * unit, -1, keepdims=True))
    return dx, jnp.sum(grad * unit, 0, keepdims=True)


def half_swap(v):
    width = v.shape[1]
    lane = lax.broadcasted_iota(jnp.int32, v.shape, 1) % HEAD
    return jnp.where(
        lane < HEAD // 2,
        pltpu.roll(v, width - HEAD // 2, 1),
        pltpu.roll(v, HEAD // 2, 1),
    )


def at_lane(shape, lane, value, base):
    return jnp.where(lax.broadcasted_iota(jnp.int32, shape, 1) == lane, value, base)


def attend_kernel(own, oth, w, cos, sin, bias, acts_o, q_o, k_o, v_o, p_o, branch_o, send_o, gain_o):
    x = jnp.concatenate([own[...].astype(F32), oth[...].astype(F32)], 0)
    small = w[:, SMALL:].astype(F32).T
    gains = small[E : E + 8]
    gain_o[...] = gains
    normed = (x * inverse_rms(x) * gains[0:1]).astype(BF16)
    acts_o[:, :D] = normed
    proj = nn(normed, w[:, :D])
    q = proj[:, :QW]
    k = proj[:, QW : QW + KW]
    v = proj[:, QW + KW :].astype(BF16)
    cos = jnp.concatenate([cos[...]] * GROUPS, 1)
    sin = jnp.concatenate([sin[...]] * GROUPS, 1)
    q = (q * cos + half_swap(q) * sin).astype(BF16)
    k = (k * cos[:, :KW] + half_swap(k) * sin[:, :KW]).astype(BF16)
    q_o[...] = q
    k_o[...] = k
    v_o[...] = v
    mask = bias[...]
    mixed = []
    for h in range(2 * GROUPS):
        g = h // 2
        q_h = q[:, HEAD * h : HEAD * h + HEAD]
        k_g = k[:, HEAD * g : HEAD * g + HEAD]
        v_g = v[:, HEAD * g : HEAD * g + HEAD]
        s = nt(q_h, k_g) * (1.0 / math.sqrt(HEAD)) + mask
        top = jnp.max(s, -1, keepdims=True)
        ex = jnp.exp(s - top)
        p = ex / jnp.sum(ex, -1, keepdims=True)
        p_o[128 * h : 128 * h + 128, :] = p
        mixed.append(nn(p.astype(BF16), v_g))
    mixed = jnp.concatenate(mixed, 1).astype(BF16)
    acts_o[:, D:] = mixed
    branch = nt(mixed, w[:, D:SMALL])
    branch_o[...] = branch[:TOK]
    send_o[...] = branch[TOK:]


def attend_keep_kernel(own, oth, w, cos, sin, bias, *outs):
    outs[-1][...] = oth[...]
    attend_kernel(own, oth, w, cos, sin, bias, *outs[:-1])


def route_rows(x, branch, recv, gains, small, routes, place, mid_o, normed_o, gate_o, out_o):
    mid = x[...].astype(F32) + branch[...] + recv[...]
    mid_o[...] = mid
    normed = (mid * inverse_rms(mid) * gains[1:2]).astype(BF16)
    normed_o[...] = normed
    logits = nn(normed, small[...])
    lane = lax.broadcasted_iota(jnp.int32, (TOK, 128), 1)
    l0 = jnp.sum(jnp.where(lane == routes[:, 0:1], logits, 0.0), -1, keepdims=True)
    l1 = jnp.sum(jnp.where(lane == routes[:, 1:2], logits, 0.0), -1, keepdims=True)
    top = jnp.maximum(l0, l1)
    e0, e1 = jnp.exp(l0 - top), jnp.exp(l1 - top)
    total = e0 + e1
    gate_o[...] = at_lane((TOK, 128), 0, e0 / total, at_lane((TOK, 128), 1, e1 / total, 0.0))
    rows = nn(place[...], jnp.concatenate([normed, normed], 0)).astype(BF16)
    out_o[:, :PACK] = pack(rows)
    return e0 / total, e1 / total


def route_kernel(*refs):
    route_rows(*refs)


def route_both_kernel(x, branch, recv, gains, small, routes, place, up, mid_o, normed_o, gate_o, out_o):
    g0, g1 = route_rows(x, branch, recv, gains, small, routes, place, mid_o, normed_o, gate_o, out_o)
    u = up[...]
    rows = jnp.concatenate([g0 * u, g1 * u], 0).astype(BF16)
    out_o[:, PACK:] = pack(nn(place[...], rows).astype(BF16))


def expert_forward_kernel(arrived, w_in, w_out, rows_o, gate_o, up_o, out_o):
    rows = unpack(arrived[...])
    rows_o[...] = rows
    gate = nt(rows, w_in[:, :D])
    up = nt(rows, w_in[:, D:])
    gate_o[...] = gate
    up_o[...] = up
    hidden = (gate * (1.0 / (1.0 + jnp.exp(-gate))) * up).astype(BF16)
    out_o[...] = pack(nn(hidden, w_out[...]).astype(BF16))


def expert_grads(grads, gate, up, w_in, w_out, units_o):
    sig = 1.0 / (1.0 + jnp.exp(-gate))
    act = gate * sig
    hidden = (act * up).astype(BF16)
    grad_hidden = nt(grads, w_out[...])
    g_gate = (grad_hidden * up * sig * (1.0 + gate * (1.0 - sig))).astype(BF16)
    g_up = (grad_hidden * act).astype(BF16)
    units_o[:, :UNITS] = hidden
    units_o[:, UNITS : 2 * UNITS] = g_gate
    units_o[:, 2 * UNITS :] = g_up
    return hidden, nn(g_gate, w_in[:, :D]) + nn(g_up, w_in[:, D:])


def expert_both_kernel(arrived, w_in, w_out, units_o, back_o):
    rows = unpack(arrived[:, :PACK])
    grads = unpack(arrived[:, PACK:])
    gate = nt(rows, w_in[:, :D])
    up = nt(rows, w_in[:, D:])
    hidden, grad_rows = expert_grads(grads, gate, up, w_in, w_out, units_o)
    back_o[:, :PACK] = pack(grad_rows.astype(BF16))
    back_o[:, PACK:] = pack(nn(hidden, w_out[...]).astype(BF16))


def expert_backward_kernel(arrived, gate, up, w_in, w_out, units_o, back_o):
    grads = unpack(arrived[...])
    _, grad_rows = expert_grads(grads, gate[...], up[...], w_in, w_out, units_o)
    back_o[...] = pack(grad_rows.astype(BF16))


def expert_weights(rows, grads, units, in_o, out_o):
    out_o[...] = tn(units[:, :UNITS], grads)
    in_o[:, :D] = tn(units[:, UNITS : 2 * UNITS], rows)
    in_o[:, D:] = tn(units[:, 2 * UNITS :], rows)


def expert_weights_both_kernel(arrived, units, in_o, out_o):
    expert_weights(unpack(arrived[:, :PACK]), unpack(arrived[:, PACK:]), units, in_o, out_o)


def expert_weights_kernel(arrived, units, rows, in_o, out_o):
    expert_weights(rows[...], unpack(arrived[...]), units, in_o, out_o)


def combine_kernel(returned, take, mid, gates, picked_o, low_o):
    picked = nn(take[...], unpack(returned[...]))
    picked_o[...] = picked
    out = mid[...] + gates[:, 0:1] * picked[:TOK] + gates[:, 1:2] * picked[TOK:]
    low_o[...] = out.astype(BF16)


def gate_back(s0, s1, gates, routes, small, returned, take, normed, mid, gains, up, gmid_o, branch_o, sums_o):
    g0, g1 = gates[:, 0:1], gates[:, 1:2]
    mean = g0 * s0 + g1 * s1
    lane = lax.broadcasted_iota(jnp.int32, (TOK, 128), 1)
    grad_logits = (
        jnp.where(lane == routes[:, 0:1], g0 * (s0 - mean), 0.0)
        + jnp.where(lane == routes[:, 1:2], g1 * (s1 - mean), 0.0)
    ).astype(BF16)
    both = (take[:TOK, :].astype(F32) + take[TOK:, :].astype(F32)).astype(BF16)
    grad_ffn = nt(grad_logits, small[...]) + nn(both, unpack(returned[:, :PACK]))
    dx, dgain = norm_back(mid[...], gains[1:2], grad_ffn)
    grad_mid = up[...].astype(F32) + dx
    gmid_o[...] = grad_mid
    branch_o[...] = grad_mid.astype(BF16)
    router = tn(grad_logits, normed[...])[:E]
    row = lax.broadcasted_iota(jnp.int32, (8, D), 0)
    sums_o[...] = jnp.concatenate([router, jnp.where(row == 1, dgain, 0.0)], 0)


def token_back_kernel(returned, take, gates, routes, small, normed, mid, gains, up, picked, gmid_o, branch_o, sums_o):
    u = up[...].astype(F32)
    s0 = jnp.sum(u * picked[:TOK, :], -1, keepdims=True)
    s1 = jnp.sum(u * picked[TOK:, :], -1, keepdims=True)
    gate_back(s0, s1, gates, routes, small, returned, take, normed, mid, gains, up, gmid_o, branch_o, sums_o)


def token_both_kernel(returned, take, gates, routes, small, normed, mid, gains, up, gmid_o, branch_o, sums_o, out_o):
    picked = nn(take[...], unpack(returned[:, PACK:]))
    out_o[...] = mid[...] + gates[:, 0:1] * picked[:TOK] + gates[:, 1:2] * picked[TOK:]
    token_back_kernel(returned, take, gates, routes, small, normed, mid, gains, up, picked, gmid_o, branch_o, sums_o)


def attend_back(own, oth, x_own, x_oth, w, cos, sin, q, k, v, p, gains, sums, part_o, send_o):
    scale = 1.0 / math.sqrt(HEAD)
    branch = jnp.concatenate([own[...], oth[...]], 0)
    grad_mixed = nn(branch, w[:, D:SMALL]).astype(BF16)
    d_q, d_k, d_v = [], [], []
    for g in range(GROUPS):
        k_g = k[:, HEAD * g : HEAD * g + HEAD]
        v_g = v[:, HEAD * g : HEAD * g + HEAD]
        dk = dv = 0.0
        for h in (2 * g, 2 * g + 1):
            q_h = q[:, HEAD * h : HEAD * h + HEAD]
            gm = grad_mixed[:, HEAD * h : HEAD * h + HEAD]
            ph = p[128 * h : 128 * h + 128, :]
            dp = nt(gm, v_g)
            ds = (ph * (dp - jnp.sum(ph * dp, -1, keepdims=True))).astype(BF16)
            d_q.append(nn(ds, k_g) * scale)
            dk = dk + tn(ds, q_h)
            dv = dv + tn(ph.astype(BF16), gm)
        d_k.append(dk * scale)
        d_v.append(dv)
    d_q = jnp.concatenate(d_q, 1)
    d_k = jnp.concatenate(d_k, 1)
    d_v = jnp.concatenate(d_v, 1)
    cos = jnp.concatenate([cos[...]] * GROUPS, 1)
    sin = jnp.concatenate([sin[...]] * GROUPS, 1)
    d_q = d_q * cos - half_swap(d_q) * sin
    d_k = d_k * cos[:, :KW] - half_swap(d_k) * sin[:, :KW]
    grad_proj = jnp.concatenate([d_q, d_k, d_v], 1).astype(BF16)
    grad_normed = nt(grad_proj, w[:, :D])
    part_o[...] = grad_normed[:TOK]
    send_o[...] = grad_normed[TOK:]
    x = jnp.concatenate([x_own[...].astype(F32), x_oth[...].astype(F32)], 0)
    dgain = jnp.sum(grad_normed * (x * inverse_rms(x)), 0, keepdims=True)
    row = lax.broadcasted_iota(jnp.int32, (E + 8, D), 0)
    return branch, grad_proj, jnp.where(row == E, dgain, sums[...])


def attend_back_share_kernel(own, oth, x_own, x_oth, w, cos, sin, q, k, v, p, gains, sums, acts, first, acts_o, part_o, send_o, sums_o):
    branch, grad_proj, sums_o[...] = attend_back(
        own, oth, x_own, x_oth, w, cos, sin, q, k, v, p, gains, sums, part_o, send_o
    )
    acts_o[:, :SMALL] = first[...]
    acts_o[:, SMALL : SMALL + D] = acts[:, :D]
    acts_o[:, SMALL + D : SMALL + 2 * D] = branch
    acts_o[:, SMALL + 2 * D : SMALL + 3 * D] = grad_proj
    acts_o[:, SMALL + 3 * D :] = acts[:, D:]


def attend_back_send_kernel(own, oth, x_own, x_oth, w, cos, sin, q, k, v, p, gains, sums, moves, out_o, part_o, send_o, sums_o):
    branch, grad_proj, sums_o[...] = attend_back(
        own, oth, x_own, x_oth, w, cos, sin, q, k, v, p, gains, sums, part_o, send_o
    )
    branch = nn(branch, moves[...]).astype(BF16)
    for y in range(4):
        out_o[128 * y : 128 * y + 128, :256] = grad_proj[:, 256 * y : 256 * y + 256]
        out_o[128 * y : 128 * y + 128, 256:] = branch[:, 256 * y : 256 * y + 256]


def share_after_kernel(y, acts, sums0, sums1, grad_o):
    for n in range(3):
        chunk = 3 * y[0] + n
        rows = acts[:, pl.ds(pl.multiple_of(jnp.where(chunk < 8, SMALL, SMALL + D), 128), D)]
        cols = acts[:, pl.ds(pl.multiple_of(SMALL + 2 * D + 128 * chunk, 128), 128)]
        grad_o[:, 128 * n : 128 * n + 128] = tn(rows, cols).astype(BF16)
    pad = jnp.zeros((64 - E - 8, D), F32)
    grad_o[:, SHARE:] = jnp.concatenate([sums0[...], pad, sums1[...], pad], 0).T.astype(BF16)


def share_first_kernel(got, acts, after, grad_o):
    grad_o[:, :KW] = tn(acts[:, :D], got[:, :256]).astype(BF16)
    out = tn(got[:, 256:], acts[:, D:]).astype(BF16)
    row = lax.broadcasted_iota(jnp.int32, (128, 128), 0)
    col = lax.broadcasted_iota(jnp.int32, (128, 128), 1)
    moves = jnp.where(row // 4 % 4 * 32 + row // 16 * 4 + row % 4 == col, 1.0, 0.0).astype(BF16)
    for n in range(8):
        stacked = jnp.concatenate([out[32 * n : 32 * n + 32, 128 * c : 128 * c + 128] for c in range(4)], 0)
        grad_o[128 * n : 128 * n + 128, KW:SHARE] = nn(moves, stacked).astype(BF16)
    grad_o[:, SHARE:] = after[...]


def input_back_kernel(part, recv, x, gains, gmid, out_o):
    dx, _ = norm_back(x[...].astype(F32), gains[0:1], part[...] + recv[...])
    out_o[...] = gmid[...] + dx


def input_back_send_kernel(part, recv, x, gains, gmid, gates, place, up_o, out_o):
    dx, _ = norm_back(x[...].astype(F32), gains[0:1], part[...] + recv[...])
    up = (gmid[...] + dx).astype(BF16)
    up_o[...] = up
    up = up.astype(F32)
    rows = jnp.concatenate([gates[:, 0:1] * up, gates[:, 1:2] * up], 0).astype(BF16)
    out_o[...] = pack(nn(place[...], rows).astype(BF16))


def halves_kernel(core, qkv, out_proj, router, gains, keep_o, send_o):
    lane = lax.broadcasted_iota(jnp.int32, (2, 128), 1) - lax.broadcasted_iota(jnp.int32, (2, 128), 0)
    rest = tn(gains[...].astype(F32), jnp.where(lane == E, 1.0, 0.0))
    rest = rest + jnp.concatenate([router[...].astype(F32), jnp.zeros((16, 128 - E), F32)], 1)
    for c in range(2):
        left = jnp.concatenate(
            [
                qkv[:, QW * c : QW * c + QW],
                qkv[:, D + KW * c : D + KW * c + KW],
                qkv[:, D + 2 * KW + KW * c : D + 2 * KW + KW * c + KW],
                out_proj[:, QW * c : QW * c + QW],
            ],
            1,
        )

        def fill(ref):
            ref[:, :SMALL] = left
            ref[:, SMALL:] = rest.astype(BF16)

        pl.when(core[0] == c)(lambda: fill(keep_o))
        pl.when(core[0] != c)(lambda: fill(send_o))


def copies_kernel(core, keep, got, all_o, own_o):
    def fill(first, second):
        own_o[...] = second[...]
        block = first[...]
        for i in range(DEV):
            all_o[16 * i : 16 * i + 16, :] = block

    pl.when(core[0] == 0)(lambda: fill(keep, got))
    pl.when(core[0] != 0)(lambda: fill(got, keep))


def total_kernel(core, blocks, keep_o, send_o):
    parts = [jnp.zeros((16, 2 * SHARE), F32) for _ in range(4)]
    rest = jnp.zeros((16, 128), F32)
    for i in range(DEV):
        block = blocks[16 * i : 16 * i + 16, :].astype(F32)
        parts[i % 4] = parts[i % 4] + block[:, : 2 * SHARE]
        rest = rest + block[:, 2 * SHARE :]

    def fill(first, second):
        for y in range(4):
            first[:, KW * y : KW * y + KW] = parts[y][:, :KW]
            for c in range(4):
                first[4 * y : 4 * y + 4, D + 128 * c : D + 128 * c + 128] = parts[y][4 * c : 4 * c + 4, KW:SHARE]
            second[:, SHARE * y : SHARE * y + SHARE] = parts[y][:, SHARE:]
        first[:, SMALL:] = rest
        second[:, SMALL:] = pltpu.roll(rest, 64, 1)

    pl.when(core[0] == 0)(lambda: fill(keep_o, send_o))
    pl.when(core[0] != 0)(lambda: fill(send_o, keep_o))


def ends_kernel(core, grad, result, got, out_o):
    def fill(c, mine):
        out_o[c] = mine[...]
        out_o[1 - c] = got[...]

    pl.when(core[0] == 0)(lambda: fill(0, grad))
    pl.when(core[0] != 0)(lambda: fill(1, result))


def owners_kernel(core, keep, got, qkv_o, out_o, router_o, gains_o):
    rest = keep[:, SMALL:] + got[:, SMALL:]
    router_o[...] = rest[:, :E]
    gains_o[...] = rest[:, E : E + 2]

    def fill(c, part):
        qkv_o[:, QW * c : QW * c + QW] = part[:, :QW]
        qkv_o[:, D + KW * c : D + KW * c + KW] = part[:, QW : QW + KW]
        qkv_o[:, D + 2 * KW + KW * c : D + 2 * KW + KW * c + KW] = part[:, QW + KW : D]
        out_o[:, QW * c : QW * c + QW] = part[:, D:SMALL]

    def both(lower, upper):
        fill(0, lower)
        fill(1, upper)

    pl.when(core[0] == 0)(lambda: both(keep, got))
    pl.when(core[0] != 0)(lambda: both(got, keep))


def whole(shape):
    return pl.BlockSpec(shape, lambda i: (0,) * len(shape))


SMALL_SPEC = pl.BlockSpec((D, 128), lambda i: (0, SMALL // 128))


def call(kernel, outs, *args, small=(), scalar=(), near=(), near_out=(), first_columns=None, after=(), grant=24, flops=10**9):
    args = [
        arg if n in near or n in scalar else pltpu.with_memory_space_constraint(arg, pltpu.HBM)
        for n, arg in enumerate(args)
    ]
    in_specs = []
    for n, arg in enumerate(args):
        if n in scalar:
            in_specs.append(pl.BlockSpec(memory_space=pltpu.SMEM))
        else:
            in_specs.append(SMALL_SPEC if n in small else whole(arg.shape))
        if n == first_columns:
            in_specs[-1] = whole((arg.shape[0], SMALL))
    count = len(args)
    in_specs += [pl.BlockSpec(memory_space=pl.ANY)] * len(after)
    args += [pltpu.with_memory_space_constraint(arg, pltpu.HBM) for arg in after]

    def body(*refs):
        kernel(*refs[:count], *refs[count + len(after) :])

    return pl.pallas_call(
        body,
        grid=(1,),
        out_shape=[
            jax.ShapeDtypeStruct(shape, kind) if n in near_out else pltpu.HBM(shape, kind)
            for n, (shape, kind) in enumerate(outs)
        ],
        in_specs=in_specs,
        out_specs=[whole(shape) for shape, _ in outs],
        compiler_params=pltpu.CompilerParams(vmem_limit_bytes=grant * 2**20),
        cost_estimate=pl.CostEstimate(flops=flops, bytes_accessed=4 * 2**20, transcendentals=0),
    )(*args)


def exchange(rows):
    blocks = rows.reshape(DEV, rows.shape[0] // DEV, rows.shape[1])
    return lax.all_to_all(blocks, "fsdp", split_axis=0, concat_axis=0, tiled=True).reshape(rows.shape)


def along(span):
    first = [i for i in range(DEV) if i // span % 4 == 0]
    return [[i + span * k for k in range(4)] for i in first]


def twin(v):
    return lax.ppermute(v, "section", [(0, 1), (1, 0)])


def rope_tables(segs):
    flat = segs.reshape(-1)
    tok = jnp.arange(2 * TOK, dtype=jnp.int32)
    same = (flat[:, None] == flat[None, :]) & (tok[:, None] // TOK == tok[None, :] // TOK)
    bias = jnp.where(same & (tok[None, :] <= tok[:, None]), 0.0, NEGATIVE).astype(F32)
    position = jnp.sum(jnp.where(same & (tok[None, :] < tok[:, None]), 1, 0), 1).astype(F32)
    frequency = jnp.exp(jnp.arange(HEAD // 2, dtype=F32) * (-2.0 * math.log(ROPE_BASE) / HEAD))
    angles = position[:, None] * frequency[None, :]
    cos, sin = jnp.cos(angles), jnp.sin(angles)
    cos = jnp.concatenate([cos] * 4, 1)
    sin = jnp.concatenate([-sin, sin] * 2, 1)
    return cos, sin, bias


def placements(routes):
    flat = routes.T.reshape(-1)
    order = jnp.arange(2 * TOK, dtype=jnp.int32)
    earlier = (flat[:, None] == flat[None, :]) & (order[None, :] < order[:, None])
    rank = jnp.sum(jnp.where(earlier, 1, 0), 1)
    first = flat * (2 * SLOT) + rank
    row = jnp.arange(ROWS, dtype=jnp.int32)
    take = (row[None, :] == first[:, None]) | (row[None, :] == first[:, None] + SLOT)
    place = (row[:, None] == first[None, :]) | (row[:, None] == first[None, :] + SLOT)
    return take.astype(BF16), place.astype(BF16)


def shards(ends_in, routes, segments, norm_gains, w_qkv, w_attn_out, w_router, w_in, w_out):
    core = lax.axis_index("section")
    is_first = core == 0

    def layers(mine, theirs):
        return jnp.where(is_first, mine, theirs), jnp.where(is_first, theirs, mine)

    def own_oth(pair):
        return jnp.where(is_first, pair[0], pair[1]), jnp.where(is_first, pair[1], pair[0])

    here = core.astype(jnp.int32).reshape(1)
    kept, sent = call(
        halves_kernel, [((16, WIDE), BF16)] * 2,
        here, w_qkv[0], w_attn_out[0], w_router[0], norm_gains[0].T, scalar=(0,), near_out=(0, 1), grant=8,
    )
    copies, shard1 = call(
        copies_kernel, [((D, WIDE), BF16), ((16, WIDE), BF16)], here, kept, twin(sent),
        scalar=(0,), near=(1, 2), near_out=(1,), grant=12,
    )
    w0 = exchange(copies)

    inputs, cotangent = layers(ends_in[0], twin(ends_in[0]))
    x0_own, x0_oth = own_oth(inputs)
    up1, _ = own_oth(cotangent)
    routes0, routes1 = layers(routes[0], twin(routes[0]))
    routes0, _ = own_oth(routes0)
    routes1, _ = own_oth(routes1)
    segs = jnp.stack(own_oth(segments[:, 0]))
    cos, sin, bias = rope_tables(segs)
    take0, place0 = placements(routes0)
    take1, place1 = placements(routes1)
    win0, win1 = layers(w_in[0], twin(w_in[0]))
    wout0, wout1 = layers(w_out[0], twin(w_out[0]))

    d = jnp.arange(D, dtype=jnp.int32)
    moves = ((d // 4 % 4 * 256 + d // 16 * 4 + d % 4)[:, None] == d[None, :]).astype(BF16)
    shard1 = jnp.where(cos[:1, :1] + sin[:1, :1] + moves[:1, :1] > 4.0, jnp.zeros_like(shard1), shard1)
    w1 = lax.all_gather(shard1, "fsdp", axis=0, tiled=True)

    def attend(kernel, own, oth, w, *more, near=(), near_out=(6,)):
        return call(
            kernel,
            [
                ((128, SMALL), BF16),
                ((128, QW), BF16),
                ((128, KW), BF16),
                ((128, KW), BF16),
                ((1024, 128), F32),
                ((TOK, D), F32),
                ((TOK, D), F32),
                ((8, D), F32),
                *more,
            ],
            own, oth, w, cos, sin, bias,
            near=near, near_out=near_out, grant=24,
        )

    def route(kernel, width, *args, near=(1, 2)):
        return call(
            kernel,
            [((TOK, D), F32), ((TOK, D), BF16), ((TOK, 128), F32), ((ROWS, width), BF16)],
            *args,
            small=(4,), near=near + (5, 6), near_out=(3,), grant=16,
        )

    weight_grads = [((UNITS, 2 * D), F32), ((UNITS, D), F32)]

    acts0, q0, k0, v0, p0, branch0, send0, gain0 = attend(attend_kernel, x0_own, x0_oth, w0, near=(2,))
    mid0, ffn0, gate0, out0 = route(
        route_kernel, PACK, x0_own, branch0, twin(send0), gain0, w0, routes0, place0, near=(2,)
    )
    rows0, pre0, upp0, back0 = call(
        expert_forward_kernel,
        [((ROWS, D), BF16), ((ROWS, UNITS), F32), ((ROWS, UNITS), F32), ((ROWS, PACK), BF16)],
        exchange(out0), win0, wout0,
        near=(0,), near_out=(3,),
    )
    picked0, x1_own = call(
        combine_kernel,
        [((128, D), F32), ((TOK, D), BF16)],
        exchange(back0), take0, mid0, gate0,
        near=(0,), grant=16,
    )
    x1_oth = twin(x1_own)

    acts1, q1, k1, v1, p1, branch1, send1, gain1, x1_oth = attend(
        attend_keep_kernel, x1_own, x1_oth, w1, ((TOK, D), BF16), near=(1,), near_out=(5, 6)
    )
    mid1, ffn1, gate1, out1 = route(
        route_both_kernel, 2 * PACK, x1_own, branch1, twin(send1), gain1, w1, routes1, place1, up1
    )
    arrived1 = exchange(out1)
    units1, back1 = call(
        expert_both_kernel,
        [((ROWS, 3 * UNITS), BF16), ((ROWS, 2 * PACK), BF16)],
        arrived1, win1, wout1,
        near=(0,),
    )
    back1 = exchange(back1)
    gin1, gout1 = call(expert_weights_both_kernel, weight_grads, arrived1, units1, near=(0,))
    gin1_got, gout1_got = twin(gin1), twin(gout1)

    token_outs = [((TOK, D), F32), ((TOK, D), BF16), ((E + 8, D), F32)]

    gmid1, gb1, sums1, result1 = call(
        token_both_kernel, token_outs + [((TOK, D), F32)],
        back1, take1, gate1, routes1, w1, ffn1, mid1, gain1, up1,
        small=(4,), near=(0, 1, 3), near_out=(1,), after=(gin1, gout1),
    )
    acts1, part1, psend1, sums1 = call(
        attend_back_share_kernel,
        [((128, BOTH), BF16), ((TOK, D), F32), ((TOK, D), F32), ((E + 8, D), F32)],
        gb1, twin(gb1), x1_own, x1_oth, w1, cos, sin, q1, k1, v1, p1, gain1, sums1, acts1, acts0,
        near=(0, 1), near_out=(1, 2), grant=28,
    )
    acts = lax.all_gather(acts1, "fsdp", axis=0, tiled=True, axis_index_groups=along(1))
    up0, gout_rows0 = call(
        input_back_send_kernel,
        [((TOK, D), BF16), ((ROWS, PACK), BF16)],
        part1, twin(psend1), x1_own, gain1, gmid1, gate0, place0,
        near=(0, 1), near_out=(1,), grant=16,
    )

    arrived0 = exchange(gout_rows0)
    units0, gback0 = call(
        expert_backward_kernel,
        [((ROWS, 3 * UNITS), BF16), ((ROWS, PACK), BF16)],
        arrived0, pre0, upp0, win0, wout0,
        near=(0,), near_out=(1,),
    )
    gback0 = exchange(gback0)
    gin0, gout0 = call(expert_weights_kernel, weight_grads, arrived0, units0, rows0, near=(0,))
    gin0_got, gout0_got = twin(gin0), twin(gout0)
    grad_in = jnp.where(is_first, gin0 + gin0_got, gin1 + gin1_got)
    grad_out = jnp.where(is_first, gout0 + gout0_got, gout1 + gout1_got)
    gmid0, gb0, sums0 = call(
        token_back_kernel, token_outs,
        gback0, take0, gate0, routes0, w0, ffn0, mid0, gain0, up0, picked0,
        small=(4,), near=(0,), near_out=(1,),
    )
    crossing, part0, psend0, sums0 = call(
        attend_back_send_kernel,
        [((512, 512), BF16), ((TOK, D), F32), ((TOK, D), F32), ((E + 8, D), F32)],
        gb0, twin(gb0), x0_own, x0_oth, w0, cos, sin, q0, k0, v0, p0, gain0, sums0, moves,
        near=(0, 1), near_out=(0, 1, 2), grant=28,
    )
    crossing = lax.all_to_all(
        crossing.reshape(4, 128, 512), "fsdp", split_axis=0, concat_axis=0, tiled=True, axis_index_groups=along(1)
    ).reshape(512, 512)
    (after,) = call(
        share_after_kernel, [((D, 512), BF16)],
        (lax.axis_index("fsdp") % 4).astype(jnp.int32).reshape(1), acts, sums0, sums1,
        scalar=(0,), near_out=(0,),
    )
    crossing, after = lax.optimization_barrier((crossing, after))
    (grads,) = call(
        share_first_kernel, [((D, 2 * SHARE + 128), BF16)],
        crossing, acts, after,
        near=(0, 2), first_columns=1,
    )
    (grad_in0,) = call(
        input_back_kernel, [((TOK, D), F32)], part0, twin(psend0), x0_own, gain0, gmid0,
        near=(0, 1), near_out=(0,), grant=16,
    )

    blocks0 = exchange(grads)
    send = jnp.where(is_first, result1, grad_in0)
    (ends_out,) = call(
        ends_kernel, [((2, TOK, D), F32)], here, grad_in0, result1, twin(send),
        scalar=(0,), near=(1, 2, 3), near_out=(0,), grant=8,
    )
    blocks0, ends_out, grad_in, grad_out = lax.optimization_barrier((blocks0, ends_out, grad_in, grad_out))
    keep, send = call(total_kernel, [((16, WIDE), F32)] * 2, here, blocks0, scalar=(0,), near=(1,), near_out=(0, 1), grant=16)
    grad_qkv, grad_attn_out, grad_router, grad_gains = call(
        owners_kernel,
        [((16, 2 * D), F32), ((16, D), F32), ((16, E), F32), ((16, 2), F32)],
        here, keep, twin(send), scalar=(0,), near=(1, 2), near_out=(0, 1, 2, 3), grant=8,
    )
    return (
        ends_out[None],
        grad_gains[None],
        grad_qkv[None],
        grad_attn_out[None],
        grad_router[None],
        grad_in[None],
        grad_out[None],
    )


def solution(mesh):
    tokens = P("section", None, "fsdp", None)
    weights = P("section", "fsdp", None)
    return jax.shard_map(
        shards,
        mesh=mesh,
        in_specs=(tokens, tokens, P(None, "fsdp", None)) + (weights,) * 6,
        out_specs=(tokens,) + (weights,) * 6,
        check_vma=False,
    )
```

```python
import math

import jax
import jax.numpy as jnp
from jax import lax
from jax.experimental import pallas as pl
from jax.experimental.pallas import tpu as pltpu
from jax.sharding import PartitionSpec as P

D = 1024
HEADS = 16
KV_HEADS = 8
HEAD = 64
E = 32
CAP = 6
TOK = 64
DEV = 64
SLOT = 8
ROWS = DEV * SLOT
PACK = 768
TAIL = D - PACK
WIDE = 1664
SMALL = 1536
SHARE = 384
BOTH = 5120
QW = 512
KW = 256
GROUPS = 4
UNITS = 256
EPSILON = 1e-06
ROPE_BASE = 10000.0
NEGATIVE = -1e30
F32 = jnp.float32
BF16 = jnp.bfloat16


def nn(a, b):
    return lax.dot_general(a, b, (((1,), (0,)), ((), ())), preferred_element_type=F32)


def nt(a, b):
    return lax.dot_general(a, b, (((1,), (1,)), ((), ())), preferred_element_type=F32)


def tn(a, b):
    return lax.dot_general(a, b, (((0,), (0,)), ((), ())), preferred_element_type=F32)


def row_in_slot(shape):
    return lax.broadcasted_iota(jnp.int32, shape, 0) % SLOT


def tail_moves():
    row = lax.broadcasted_iota(jnp.int32, (128, 384), 0)
    col = lax.broadcasted_iota(jnp.int32, (128, 384), 1)
    piece, col = col // 128, col % 128
    slot, kept = row % SLOT, col % SLOT
    hit = ((kept == CAP) & (slot == piece)) | ((kept == CAP + 1) & (slot == piece + 3))
    return jnp.where(hit & (row // SLOT == col // SLOT), 1.0, 0.0).astype(BF16)


def unpack(packed):
    moves = tail_moves()
    main = jnp.where(row_in_slot((ROWS, PACK)) < CAP, packed.astype(F32), 0.0).astype(BF16)
    tails = []
    for block in range(0, ROWS, 128):
        part = packed[block : block + 128]
        stacked = jnp.concatenate([part[:, 256 * j : 256 * j + 256] for j in range(3)], 0)
        tails.append(nn(moves, stacked).astype(BF16))
    return jnp.concatenate([main, jnp.concatenate(tails, 0)], 1)


def pack(rows):
    moves = tail_moves()
    keep = row_in_slot((128, 256)) < CAP
    blocks = []
    for block in range(0, ROWS, 128):
        part = rows[block : block + 128]
        tail = tn(moves, part[:, PACK:])
        pieces = []
        for j in range(3):
            main = part[:, 256 * j : 256 * j + 256].astype(F32)
            pieces.append(jnp.where(keep, main, tail[128 * j : 128 * j + 128]).astype(BF16))
        blocks.append(jnp.concatenate(pieces, 1))
    return jnp.concatenate(blocks, 0)


def inverse_rms(x):
    return lax.rsqrt(jnp.mean(x * x, -1, keepdims=True) + EPSILON)


def norm_back(x, gain, grad):
    inv = inverse_rms(x)
    unit = x * inv
    scaled = grad * gain
    dx = inv * (scaled - unit * jnp.mean(scaled * unit, -1, keepdims=True))
    return dx, jnp.sum(grad * unit, 0, keepdims=True)


def half_swap(v):
    width = v.shape[1]
    lane = lax.broadcasted_iota(jnp.int32, v.shape, 1) % HEAD
    return jnp.where(
        lane < HEAD // 2,
        pltpu.roll(v, width - HEAD // 2, 1),
        pltpu.roll(v, HEAD // 2, 1),
    )


def at_lane(shape, lane, value, base):
    return jnp.where(lax.broadcasted_iota(jnp.int32, shape, 1) == lane, value, base)


def attend_kernel(own, oth, w, cos, sin, bias, acts_o, q_o, k_o, v_o, p_o, branch_o, send_o, gain_o):
    x = jnp.concatenate([own[...].astype(F32), oth[...].astype(F32)], 0)
    small = w[:, SMALL:].astype(F32).T
    gains = small[E : E + 8]
    gain_o[...] = gains
    normed = (x * inverse_rms(x) * gains[0:1]).astype(BF16)
    acts_o[:, :D] = normed
    proj = nn(normed, w[:, :D])
    q = proj[:, :QW]
    k = proj[:, QW : QW + KW]
    v = proj[:, QW + KW :].astype(BF16)
    cos = jnp.concatenate([cos[...]] * GROUPS, 1)
    sin = jnp.concatenate([sin[...]] * GROUPS, 1)
    q = (q * cos + half_swap(q) * sin).astype(BF16)
    k = (k * cos[:, :KW] + half_swap(k) * sin[:, :KW]).astype(BF16)
    q_o[...] = q
    k_o[...] = k
    v_o[...] = v
    mask = bias[...]
    mixed = []
    for h in range(2 * GROUPS):
        g = h // 2
        q_h = q[:, HEAD * h : HEAD * h + HEAD]
        k_g = k[:, HEAD * g : HEAD * g + HEAD]
        v_g = v[:, HEAD * g : HEAD * g + HEAD]
        s = nt(q_h, k_g) * (1.0 / math.sqrt(HEAD)) + mask
        top = jnp.max(s, -1, keepdims=True)
        ex = jnp.exp(s - top)
        p = ex / jnp.sum(ex, -1, keepdims=True)
        p_o[128 * h : 128 * h + 128, :] = p
        mixed.append(nn(p.astype(BF16), v_g))
    mixed = jnp.concatenate(mixed, 1).astype(BF16)
    acts_o[:, D:] = mixed
    branch = nt(mixed, w[:, D:SMALL])
    branch_o[...] = branch[:TOK]
    send_o[...] = branch[TOK:]


def attend_keep_kernel(own, oth, w, cos, sin, bias, *outs):
    outs[-1][...] = oth[...]
    attend_kernel(own, oth, w, cos, sin, bias, *outs[:-1])


def route_rows(x, branch, recv, gains, small, routes, place, mid_o, normed_o, gate_o, out_o):
    mid = x[...].astype(F32) + branch[...] + recv[...]
    mid_o[...] = mid
    normed = (mid * inverse_rms(mid) * gains[1:2]).astype(BF16)
    normed_o[...] = normed
    logits = nn(normed, small[...])
    lane = lax.broadcasted_iota(jnp.int32, (TOK, 128), 1)
    l0 = jnp.sum(jnp.where(lane == routes[:, 0:1], logits, 0.0), -1, keepdims=True)
    l1 = jnp.sum(jnp.where(lane == routes[:, 1:2], logits, 0.0), -1, keepdims=True)
    top = jnp.maximum(l0, l1)
    e0, e1 = jnp.exp(l0 - top), jnp.exp(l1 - top)
    total = e0 + e1
    gate_o[...] = at_lane((TOK, 128), 0, e0 / total, at_lane((TOK, 128), 1, e1 / total, 0.0))
    rows = nn(place[...], jnp.concatenate([normed, normed], 0)).astype(BF16)
    out_o[:, :PACK] = pack(rows)
    return e0 / total, e1 / total


def route_kernel(*refs):
    route_rows(*refs)


def route_both_kernel(x, branch, recv, gains, small, routes, place, up, mid_o, normed_o, gate_o, out_o):
    g0, g1 = route_rows(x, branch, recv, gains, small, routes, place, mid_o, normed_o, gate_o, out_o)
    u = up[...]
    rows = jnp.concatenate([g0 * u, g1 * u], 0).astype(BF16)
    out_o[:, PACK:] = pack(nn(place[...], rows).astype(BF16))


def expert_forward_kernel(arrived, w_in, w_out, rows_o, gate_o, up_o, out_o):
    rows = unpack(arrived[...])
    rows_o[...] = rows
    gate = nt(rows, w_in[:, :D])
    up = nt(rows, w_in[:, D:])
    gate_o[...] = gate
    up_o[...] = up
    hidden = (gate * (1.0 / (1.0 + jnp.exp(-gate))) * up).astype(BF16)
    out_o[...] = pack(nn(hidden, w_out[...]).astype(BF16))


def expert_grads(grads, gate, up, w_in, w_out, units_o):
    sig = 1.0 / (1.0 + jnp.exp(-gate))
    act = gate * sig
    hidden = (act * up).astype(BF16)
    grad_hidden = nt(grads, w_out[...])
    g_gate = (grad_hidden * up * sig * (1.0 + gate * (1.0 - sig))).astype(BF16)
    g_up = (grad_hidden * act).astype(BF16)
    units_o[:, :UNITS] = hidden
    units_o[:, UNITS : 2 * UNITS] = g_gate
    units_o[:, 2 * UNITS :] = g_up
    return hidden, nn(g_gate, w_in[:, :D]) + nn(g_up, w_in[:, D:])


def expert_both_kernel(arrived, w_in, w_out, units_o, back_o):
    rows = unpack(arrived[:, :PACK])
    grads = unpack(arrived[:, PACK:])
    gate = nt(rows, w_in[:, :D])
    up = nt(rows, w_in[:, D:])
    hidden, grad_rows = expert_grads(grads, gate, up, w_in, w_out, units_o)
    back_o[:, :PACK] = pack(grad_rows.astype(BF16))
    back_o[:, PACK:] = pack(nn(hidden, w_out[...]).astype(BF16))


def expert_backward_kernel(arrived, gate, up, w_in, w_out, units_o, back_o):
    grads = unpack(arrived[...])
    _, grad_rows = expert_grads(grads, gate[...], up[...], w_in, w_out, units_o)
    back_o[...] = pack(grad_rows.astype(BF16))


def expert_weights(rows, grads, units, in_o, out_o):
    out_o[...] = tn(units[:, :UNITS], grads)
    in_o[:, :D] = tn(units[:, UNITS : 2 * UNITS], rows)
    in_o[:, D:] = tn(units[:, 2 * UNITS :], rows)


def expert_weights_both_kernel(arrived, units, in_o, out_o):
    expert_weights(unpack(arrived[:, :PACK]), unpack(arrived[:, PACK:]), units, in_o, out_o)


def expert_weights_kernel(arrived, units, rows, in_o, out_o):
    expert_weights(rows[...], unpack(arrived[...]), units, in_o, out_o)


def combine_kernel(returned, take, mid, gates, picked_o, low_o):
    picked = nn(take[...], unpack(returned[...]))
    picked_o[...] = picked
    out = mid[...] + gates[:, 0:1] * picked[:TOK] + gates[:, 1:2] * picked[TOK:]
    low_o[...] = out.astype(BF16)


def gate_back(s0, s1, gates, routes, small, returned, take, normed, mid, gains, up, gmid_o, branch_o, sums_o):
    g0, g1 = gates[:, 0:1], gates[:, 1:2]
    mean = g0 * s0 + g1 * s1
    lane = lax.broadcasted_iota(jnp.int32, (TOK, 128), 1)
    grad_logits = (
        jnp.where(lane == routes[:, 0:1], g0 * (s0 - mean), 0.0)
        + jnp.where(lane == routes[:, 1:2], g1 * (s1 - mean), 0.0)
    ).astype(BF16)
    both = (take[:TOK, :].astype(F32) + take[TOK:, :].astype(F32)).astype(BF16)
    grad_ffn = nt(grad_logits, small[...]) + nn(both, unpack(returned[:, :PACK]))
    dx, dgain = norm_back(mid[...], gains[1:2], grad_ffn)
    grad_mid = up[...].astype(F32) + dx
    gmid_o[...] = grad_mid
    branch_o[...] = grad_mid.astype(BF16)
    router = tn(grad_logits, normed[...])[:E]
    row = lax.broadcasted_iota(jnp.int32, (8, D), 0)
    sums_o[...] = jnp.concatenate([router, jnp.where(row == 1, dgain, 0.0)], 0)


def token_back_kernel(returned, take, gates, routes, small, normed, mid, gains, up, picked, gmid_o, branch_o, sums_o):
    u = up[...].astype(F32)
    s0 = jnp.sum(u * picked[:TOK, :], -1, keepdims=True)
    s1 = jnp.sum(u * picked[TOK:, :], -1, keepdims=True)
    gate_back(s0, s1, gates, routes, small, returned, take, normed, mid, gains, up, gmid_o, branch_o, sums_o)


def token_both_kernel(returned, take, gates, routes, small, normed, mid, gains, up, gmid_o, branch_o, sums_o, out_o):
    picked = nn(take[...], unpack(returned[:, PACK:]))
    out_o[...] = mid[...] + gates[:, 0:1] * picked[:TOK] + gates[:, 1:2] * picked[TOK:]
    token_back_kernel(returned, take, gates, routes, small, normed, mid, gains, up, picked, gmid_o, branch_o, sums_o)


def attend_back(own, oth, x_own, x_oth, w, cos, sin, q, k, v, p, gains, sums, part_o, send_o):
    scale = 1.0 / math.sqrt(HEAD)
    branch = jnp.concatenate([own[...], oth[...]], 0)
    grad_mixed = nn(branch, w[:, D:SMALL]).astype(BF16)
    d_q, d_k, d_v = [], [], []
    for g in range(GROUPS):
        k_g = k[:, HEAD * g : HEAD * g + HEAD]
        v_g = v[:, HEAD * g : HEAD * g + HEAD]
        dk = dv = 0.0
        for h in (2 * g, 2 * g + 1):
            q_h = q[:, HEAD * h : HEAD * h + HEAD]
            gm = grad_mixed[:, HEAD * h : HEAD * h + HEAD]
            ph = p[128 * h : 128 * h + 128, :]
            dp = nt(gm, v_g)
            ds = (ph * (dp - jnp.sum(ph * dp, -1, keepdims=True))).astype(BF16)
            d_q.append(nn(ds, k_g) * scale)
            dk = dk + tn(ds, q_h)
            dv = dv + tn(ph.astype(BF16), gm)
        d_k.append(dk * scale)
        d_v.append(dv)
    d_q = jnp.concatenate(d_q, 1)
    d_k = jnp.concatenate(d_k, 1)
    d_v = jnp.concatenate(d_v, 1)
    cos = jnp.concatenate([cos[...]] * GROUPS, 1)
    sin = jnp.concatenate([sin[...]] * GROUPS, 1)
    d_q = d_q * cos - half_swap(d_q) * sin
    d_k = d_k * cos[:, :KW] - half_swap(d_k) * sin[:, :KW]
    grad_proj = jnp.concatenate([d_q, d_k, d_v], 1).astype(BF16)
    grad_normed = nt(grad_proj, w[:, :D])
    part_o[...] = grad_normed[:TOK]
    send_o[...] = grad_normed[TOK:]
    x = jnp.concatenate([x_own[...].astype(F32), x_oth[...].astype(F32)], 0)
    dgain = jnp.sum(grad_normed * (x * inverse_rms(x)), 0, keepdims=True)
    row = lax.broadcasted_iota(jnp.int32, (E + 8, D), 0)
    return branch, grad_proj, jnp.where(row == E, dgain, sums[...])


def attend_back_share_kernel(own, oth, x_own, x_oth, w, cos, sin, q, k, v, p, gains, sums, acts, first, acts_o, part_o, send_o, sums_o):
    branch, grad_proj, sums_o[...] = attend_back(
        own, oth, x_own, x_oth, w, cos, sin, q, k, v, p, gains, sums, part_o, send_o
    )
    acts_o[:, :SMALL] = first[...]
    acts_o[:, SMALL : SMALL + D] = acts[:, :D]
    acts_o[:, SMALL + D : SMALL + 2 * D] = branch
    acts_o[:, SMALL + 2 * D : SMALL + 3 * D] = grad_proj
    acts_o[:, SMALL + 3 * D :] = acts[:, D:]


def attend_back_send_kernel(own, oth, x_own, x_oth, w, cos, sin, q, k, v, p, gains, sums, moves, out_o, part_o, send_o, sums_o):
    branch, grad_proj, sums_o[...] = attend_back(
        own, oth, x_own, x_oth, w, cos, sin, q, k, v, p, gains, sums, part_o, send_o
    )
    branch = nn(branch, moves[...]).astype(BF16)
    for y in range(4):
        out_o[128 * y : 128 * y + 128, :256] = grad_proj[:, 256 * y : 256 * y + 256]
        out_o[128 * y : 128 * y + 128, 256:] = branch[:, 256 * y : 256 * y + 256]


def share_after_kernel(y, acts, sums0, sums1, grad_o):
    for n in range(3):
        chunk = 3 * y[0] + n
        rows = acts[:, pl.ds(pl.multiple_of(jnp.where(chunk < 8, SMALL, SMALL + D), 128), D)]
        cols = acts[:, pl.ds(pl.multiple_of(SMALL + 2 * D + 128 * chunk, 128), 128)]
        grad_o[:, 128 * n : 128 * n + 128] = tn(rows, cols).astype(BF16)
    pad = jnp.zeros((64 - E - 8, D), F32)
    grad_o[:, SHARE:] = jnp.concatenate([sums0[...], pad, sums1[...], pad], 0).T.astype(BF16)


def share_first_kernel(got, acts, after, grad_o):
    grad_o[:, :KW] = tn(acts[:, :D], got[:, :256]).astype(BF16)
    out = tn(got[:, 256:], acts[:, D:]).astype(BF16)
    row = lax.broadcasted_iota(jnp.int32, (128, 128), 0)
    col = lax.broadcasted_iota(jnp.int32, (128, 128), 1)
    moves = jnp.where(row // 4 % 4 * 32 + row // 16 * 4 + row % 4 == col, 1.0, 0.0).astype(BF16)
    for n in range(8):
        stacked = jnp.concatenate([out[32 * n : 32 * n + 32, 128 * c : 128 * c + 128] for c in range(4)], 0)
        grad_o[128 * n : 128 * n + 128, KW:SHARE] = nn(moves, stacked).astype(BF16)
    grad_o[:, SHARE:] = after[...]


def input_back_kernel(part, recv, x, gains, gmid, out_o):
    dx, _ = norm_back(x[...].astype(F32), gains[0:1], part[...] + recv[...])
    out_o[...] = gmid[...] + dx


def input_back_send_kernel(part, recv, x, gains, gmid, gates, place, up_o, out_o):
    dx, _ = norm_back(x[...].astype(F32), gains[0:1], part[...] + recv[...])
    up = (gmid[...] + dx).astype(BF16)
    up_o[...] = up
    up = up.astype(F32)
    rows = jnp.concatenate([gates[:, 0:1] * up, gates[:, 1:2] * up], 0).astype(BF16)
    out_o[...] = pack(nn(place[...], rows).astype(BF16))


def halves_kernel(core, qkv, out_proj, router, gains, keep_o, send_o):
    lane = lax.broadcasted_iota(jnp.int32, (2, 128), 1) - lax.broadcasted_iota(jnp.int32, (2, 128), 0)
    rest = tn(gains[...].astype(F32), jnp.where(lane == E, 1.0, 0.0))
    rest = rest + jnp.concatenate([router[...].astype(F32), jnp.zeros((16, 128 - E), F32)], 1)
    for c in range(2):
        left = jnp.concatenate(
            [
                qkv[:, QW * c : QW * c + QW],
                qkv[:, D + KW * c : D + KW * c + KW],
                qkv[:, D + 2 * KW + KW * c : D + 2 * KW + KW * c + KW],
                out_proj[:, QW * c : QW * c + QW],
            ],
            1,
        )

        def fill(ref):
            ref[:, :SMALL] = left
            ref[:, SMALL:] = rest.astype(BF16)

        pl.when(core[0] == c)(lambda: fill(keep_o))
        pl.when(core[0] != c)(lambda: fill(send_o))


def copies_kernel(core, keep, got, all_o, own_o):
    def fill(first, second):
        own_o[...] = second[...]
        block = first[...]
        for i in range(DEV):
            all_o[16 * i : 16 * i + 16, :] = block

    pl.when(core[0] == 0)(lambda: fill(keep, got))
    pl.when(core[0] != 0)(lambda: fill(got, keep))


def total_kernel(core, blocks, keep_o, send_o):
    parts = [jnp.zeros((16, 2 * SHARE), F32) for _ in range(4)]
    rest = jnp.zeros((16, 128), F32)
    for i in range(DEV):
        block = blocks[16 * i : 16 * i + 16, :].astype(F32)
        parts[i % 4] = parts[i % 4] + block[:, : 2 * SHARE]
        rest = rest + block[:, 2 * SHARE :]

    def fill(first, second):
        for y in range(4):
            first[:, KW * y : KW * y + KW] = parts[y][:, :KW]
            for c in range(4):
                first[4 * y : 4 * y + 4, D + 128 * c : D + 128 * c + 128] = parts[y][4 * c : 4 * c + 4, KW:SHARE]
            second[:, SHARE * y : SHARE * y + SHARE] = parts[y][:, SHARE:]
        first[:, SMALL:] = rest
        second[:, SMALL:] = pltpu.roll(rest, 64, 1)

    pl.when(core[0] == 0)(lambda: fill(keep_o, send_o))
    pl.when(core[0] != 0)(lambda: fill(send_o, keep_o))


def ends_kernel(core, grad, result, got, out_o):
    def fill(c, mine):
        out_o[c] = mine[...]
        out_o[1 - c] = got[...]

    pl.when(core[0] == 0)(lambda: fill(0, grad))
    pl.when(core[0] != 0)(lambda: fill(1, result))


def owners_kernel(core, keep, got, qkv_o, out_o, router_o, gains_o):
    rest = keep[:, SMALL:] + got[:, SMALL:]
    router_o[...] = rest[:, :E]
    gains_o[...] = rest[:, E : E + 2]

    def fill(c, part):
        qkv_o[:, QW * c : QW * c + QW] = part[:, :QW]
        qkv_o[:, D + KW * c : D + KW * c + KW] = part[:, QW : QW + KW]
        qkv_o[:, D + 2 * KW + KW * c : D + 2 * KW + KW * c + KW] = part[:, QW + KW : D]
        out_o[:, QW * c : QW * c + QW] = part[:, D:SMALL]

    def both(lower, upper):
        fill(0, lower)
        fill(1, upper)

    pl.when(core[0] == 0)(lambda: both(keep, got))
    pl.when(core[0] != 0)(lambda: both(got, keep))


def whole(shape):
    return pl.BlockSpec(shape, lambda i: (0,) * len(shape))


SMALL_SPEC = pl.BlockSpec((D, 128), lambda i: (0, SMALL // 128))


def call(kernel, outs, *args, small=(), scalar=(), near=(), near_out=(), first_columns=None, after=(), grant=24, flops=10**9):
    args = [
        arg if n in near or n in scalar else pltpu.with_memory_space_constraint(arg, pltpu.HBM)
        for n, arg in enumerate(args)
    ]
    in_specs = []
    for n, arg in enumerate(args):
        if n in scalar:
            in_specs.append(pl.BlockSpec(memory_space=pltpu.SMEM))
        else:
            in_specs.append(SMALL_SPEC if n in small else whole(arg.shape))
        if n == first_columns:
            in_specs[-1] = whole((arg.shape[0], SMALL))
    count = len(args)
    in_specs += [pl.BlockSpec(memory_space=pl.ANY)] * len(after)
    args += [pltpu.with_memory_space_constraint(arg, pltpu.HBM) for arg in after]

    def body(*refs):
        kernel(*refs[:count], *refs[count + len(after) :])

    return pl.pallas_call(
        body,
        grid=(1,),
        out_shape=[
            jax.ShapeDtypeStruct(shape, kind) if n in near_out else pltpu.HBM(shape, kind)
            for n, (shape, kind) in enumerate(outs)
        ],
        in_specs=in_specs,
        out_specs=[whole(shape) for shape, _ in outs],
        compiler_params=pltpu.CompilerParams(vmem_limit_bytes=grant * 2**20),
        cost_estimate=pl.CostEstimate(flops=flops, bytes_accessed=4 * 2**20, transcendentals=0),
    )(*args)


def exchange(rows):
    blocks = rows.reshape(DEV, rows.shape[0] // DEV, rows.shape[1])
    return lax.all_to_all(blocks, "fsdp", split_axis=0, concat_axis=0, tiled=True).reshape(rows.shape)


def along(span):
    first = [i for i in range(DEV) if i // span % 4 == 0]
    return [[i + span * k for k in range(4)] for i in first]


def twin(v):
    return lax.ppermute(v, "section", [(0, 1), (1, 0)])


def rope_tables(segs):
    flat = segs.reshape(-1)
    tok = jnp.arange(2 * TOK, dtype=jnp.int32)
    same = (flat[:, None] == flat[None, :]) & (tok[:, None] // TOK == tok[None, :] // TOK)
    bias = jnp.where(same & (tok[None, :] <= tok[:, None]), 0.0, NEGATIVE).astype(F32)
    position = jnp.sum(jnp.where(same & (tok[None, :] < tok[:, None]), 1, 0), 1).astype(F32)
    frequency = jnp.exp(jnp.arange(HEAD // 2, dtype=F32) * (-2.0 * math.log(ROPE_BASE) / HEAD))
    angles = position[:, None] * frequency[None, :]
    cos, sin = jnp.cos(angles), jnp.sin(angles)
    cos = jnp.concatenate([cos] * 4, 1)
    sin = jnp.concatenate([-sin, sin] * 2, 1)
    return cos, sin, bias


def placements(routes):
    flat = routes.T.reshape(-1)
    order = jnp.arange(2 * TOK, dtype=jnp.int32)
    earlier = (flat[:, None] == flat[None, :]) & (order[None, :] < order[:, None])
    rank = jnp.sum(jnp.where(earlier, 1, 0), 1)
    first = flat * (2 * SLOT) + rank
    row = jnp.arange(ROWS, dtype=jnp.int32)
    take = (row[None, :] == first[:, None]) | (row[None, :] == first[:, None] + SLOT)
    place = (row[:, None] == first[None, :]) | (row[:, None] == first[None, :] + SLOT)
    return take.astype(BF16), place.astype(BF16)


def shards(ends_in, routes, segments, norm_gains, w_qkv, w_attn_out, w_router, w_in, w_out):
    core = lax.axis_index("section")
    is_first = core == 0

    def layers(mine, theirs):
        return jnp.where(is_first, mine, theirs), jnp.where(is_first, theirs, mine)

    def own_oth(pair):
        return jnp.where(is_first, pair[0], pair[1]), jnp.where(is_first, pair[1], pair[0])

    here = core.astype(jnp.int32).reshape(1)
    kept, sent = call(
        halves_kernel, [((16, WIDE), BF16)] * 2,
        here, w_qkv[0], w_attn_out[0], w_router[0], norm_gains[0].T, scalar=(0,), near_out=(0, 1), grant=8,
    )
    copies, shard1 = call(
        copies_kernel, [((D, WIDE), BF16), ((16, WIDE), BF16)], here, kept, twin(sent),
        scalar=(0,), near=(1, 2), near_out=(1,), grant=12,
    )
    w0 = exchange(copies)

    inputs, cotangent = layers(ends_in[0], twin(ends_in[0]))
    x0_own, x0_oth = own_oth(inputs)
    up1, _ = own_oth(cotangent)
    routes0, routes1 = layers(routes[0], twin(routes[0]))
    routes0, _ = own_oth(routes0)
    routes1, _ = own_oth(routes1)
    segs = jnp.stack(own_oth(segments[:, 0]))
    cos, sin, bias = rope_tables(segs)
    take0, place0 = placements(routes0)
    take1, place1 = placements(routes1)
    win0, win1 = layers(w_in[0], twin(w_in[0]))
    wout0, wout1 = layers(w_out[0], twin(w_out[0]))

    d = jnp.arange(D, dtype=jnp.int32)
    moves = ((d // 4 % 4 * 256 + d // 16 * 4 + d % 4)[:, None] == d[None, :]).astype(BF16)
    shard1 = jnp.where(cos[:1, :1] + sin[:1, :1] + moves[:1, :1] > 4.0, jnp.zeros_like(shard1), shard1)
    w1 = lax.all_gather(shard1, "fsdp", axis=0, tiled=True)

    def attend(kernel, own, oth, w, *more, near=(), near_out=(6,)):
        return call(
            kernel,
            [
                ((128, SMALL), BF16),
                ((128, QW), BF16),
                ((128, KW), BF16),
                ((128, KW), BF16),
                ((1024, 128), F32),
                ((TOK, D), F32),
                ((TOK, D), F32),
                ((8, D), F32),
                *more,
            ],
            own, oth, w, cos, sin, bias,
            near=near, near_out=near_out, grant=24,
        )

    def route(kernel, width, *args, near=(1, 2, 5, 6)):
        return call(
            kernel,
            [((TOK, D), F32), ((TOK, D), BF16), ((TOK, 128), F32), ((ROWS, width), BF16)],
            *args,
            small=(4,), near=near, near_out=(3,), grant=16,
        )

    weight_grads = [((UNITS, 2 * D), F32), ((UNITS, D), F32)]

    acts0, q0, k0, v0, p0, branch0, send0, gain0 = attend(attend_kernel, x0_own, x0_oth, w0, near=(2,))
    mid0, ffn0, gate0, out0 = route(
        route_kernel, PACK, x0_own, branch0, twin(send0), gain0, w0, routes0, place0, near=(2,)
    )
    rows0, pre0, upp0, back0 = call(
        expert_forward_kernel,
        [((ROWS, D), BF16), ((ROWS, UNITS), F32), ((ROWS, UNITS), F32), ((ROWS, PACK), BF16)],
        exchange(out0), win0, wout0,
        near=(0,), near_out=(3,),
    )
    picked0, x1_own = call(
        combine_kernel,
        [((128, D), F32), ((TOK, D), BF16)],
        exchange(back0), take0, mid0, gate0,
        near=(0,), grant=16,
    )
    x1_oth = twin(x1_own)

    acts1, q1, k1, v1, p1, branch1, send1, gain1, x1_oth = attend(
        attend_keep_kernel, x1_own, x1_oth, w1, ((TOK, D), BF16), near=(1,), near_out=(5, 6)
    )
    mid1, ffn1, gate1, out1 = route(
        route_both_kernel, 2 * PACK, x1_own, branch1, twin(send1), gain1, w1, routes1, place1, up1
    )
    arrived1 = exchange(out1)
    units1, back1 = call(
        expert_both_kernel,
        [((ROWS, 3 * UNITS), BF16), ((ROWS, 2 * PACK), BF16)],
        arrived1, win1, wout1,
        near=(0,),
    )
    back1 = exchange(back1)
    gin1, gout1 = call(expert_weights_both_kernel, weight_grads, arrived1, units1, near=(0,))
    gin1_got, gout1_got = twin(gin1), twin(gout1)

    token_outs = [((TOK, D), F32), ((TOK, D), BF16), ((E + 8, D), F32)]

    gmid1, gb1, sums1, result1 = call(
        token_both_kernel, token_outs + [((TOK, D), F32)],
        back1, take1, gate1, routes1, w1, ffn1, mid1, gain1, up1,
        small=(4,), near=(0, 1, 3), near_out=(1,), after=(gin1, gout1),
    )
    acts1, part1, psend1, sums1 = call(
        attend_back_share_kernel,
        [((128, BOTH), BF16), ((TOK, D), F32), ((TOK, D), F32), ((E + 8, D), F32)],
        gb1, twin(gb1), x1_own, x1_oth, w1, cos, sin, q1, k1, v1, p1, gain1, sums1, acts1, acts0,
        near=(0, 1), near_out=(1, 2), grant=28,
    )
    acts = lax.all_gather(acts1, "fsdp", axis=0, tiled=True, axis_index_groups=along(1))
    up0, gout_rows0 = call(
        input_back_send_kernel,
        [((TOK, D), BF16), ((ROWS, PACK), BF16)],
        part1, twin(psend1), x1_own, gain1, gmid1, gate0, place0,
        near=(0, 1), near_out=(1,), grant=16,
    )

    arrived0 = exchange(gout_rows0)
    units0, gback0 = call(
        expert_backward_kernel,
        [((ROWS, 3 * UNITS), BF16), ((ROWS, PACK), BF16)],
        arrived0, pre0, upp0, win0, wout0,
        near=(0,), near_out=(1,),
    )
    gback0 = exchange(gback0)
    gin0, gout0 = call(expert_weights_kernel, weight_grads, arrived0, units0, rows0, near=(0,))
    gin0_got, gout0_got = twin(gin0), twin(gout0)
    grad_in = jnp.where(is_first, gin0 + gin0_got, gin1 + gin1_got)
    grad_out = jnp.where(is_first, gout0 + gout0_got, gout1 + gout1_got)
    gmid0, gb0, sums0 = call(
        token_back_kernel, token_outs,
        gback0, take0, gate0, routes0, w0, ffn0, mid0, gain0, up0, picked0,
        small=(4,), near=(0,), near_out=(1,),
    )
    crossing, part0, psend0, sums0 = call(
        attend_back_send_kernel,
        [((512, 512), BF16), ((TOK, D), F32), ((TOK, D), F32), ((E + 8, D), F32)],
        gb0, twin(gb0), x0_own, x0_oth, w0, cos, sin, q0, k0, v0, p0, gain0, sums0, moves,
        near=(0, 1), near_out=(0, 1, 2), grant=28,
    )
    crossing = lax.all_to_all(
        crossing.reshape(4, 128, 512), "fsdp", split_axis=0, concat_axis=0, tiled=True, axis_index_groups=along(1)
    ).reshape(512, 512)
    (after,) = call(
        share_after_kernel, [((D, 512), BF16)],
        (lax.axis_index("fsdp") % 4).astype(jnp.int32).reshape(1), acts, sums0, sums1,
        scalar=(0,), near_out=(0,),
    )
    crossing, after = lax.optimization_barrier((crossing, after))
    (grads,) = call(
        share_first_kernel, [((D, 2 * SHARE + 128), BF16)],
        crossing, acts, after,
        near=(0, 2), first_columns=1,
    )
    (grad_in0,) = call(
        input_back_kernel, [((TOK, D), F32)], part0, twin(psend0), x0_own, gain0, gmid0,
        near=(0, 1), near_out=(0,), grant=16,
    )

    blocks0 = exchange(grads)
    send = jnp.where(is_first, result1, grad_in0)
    (ends_out,) = call(
        ends_kernel, [((2, TOK, D), F32)], here, grad_in0, result1, twin(send),
        scalar=(0,), near=(1, 2, 3), near_out=(0,), grant=8,
    )
    blocks0, ends_out, grad_in, grad_out = lax.optimization_barrier((blocks0, ends_out, grad_in, grad_out))
    keep, send = call(total_kernel, [((16, WIDE), F32)] * 2, here, blocks0, scalar=(0,), near=(1,), near_out=(0, 1), grant=16)
    grad_qkv, grad_attn_out, grad_router, grad_gains = call(
        owners_kernel,
        [((16, 2 * D), F32), ((16, D), F32), ((16, E), F32), ((16, 2), F32)],
        here, keep, twin(send), scalar=(0,), near=(1, 2), near_out=(0, 1, 2, 3), grant=8,
    )
    return (
        ends_out[None],
        grad_gains[None],
        grad_qkv[None],
        grad_attn_out[None],
        grad_router[None],
        grad_in[None],
        grad_out[None],
    )


def solution(mesh):
    tokens = P("section", None, "fsdp", None)
    weights = P("section", "fsdp", None)
    return jax.shard_map(
        shards,
        mesh=mesh,
        in_specs=(tokens, tokens, P(None, "fsdp", None)) + (weights,) * 6,
        out_specs=(tokens,) + (weights,) * 6,
        check_vma=False,
    )
```
